128 devices in a mesh: rep: 64 (over y, x, z_hi, core), shard: 2 (over z_lo).
Axes of the slice: x: 4, y: 4, z: 4 (z_hi: 2, z_lo: 2; z = z_hi * 2 + z_lo), core: 2. Of those that a mesh axis runs over, the one named last changes fastest.
Arguments:
- tokens: bfloat16 [24576, 768], P(('rep', 'shard')), may hold values from -6 to 6
- cotangent: bfloat16 [24576, 768], P(('rep', 'shard')), may hold values from -6 to 6
- attn_gain: bfloat16 [768], P('shard'), may hold values from 0.5 to 1.5
- w_qkv: bfloat16 [768, 2304], P('shard'), may hold values from -0.21875 to 0.21875
- w_out: bfloat16 [768, 768], P('shard'), may hold values from -1.75 to 1.75
- rel_bias: bfloat16 [32, 12], P('shard'), may hold values from -3 to 3
- buckets: int32 [384], replicated, may hold values from 0 to 31, as said below
- ffn_gain: bfloat16 [768], P('shard'), may hold values from 0.5 to 1.5
- w_router: bfloat16 [768, 64], P('shard'), may hold values from -0.21875 to 0.21875
- w_in: bfloat16 [64, 768, 3072], P('rep', None, 'shard'), may hold values from -0.21875 to 0.21875
- w_back: bfloat16 [64, 3072, 768], P('rep', 'shard'), may hold values from -6 to 6
- choice_ids: int32 [24576, 2], P(('rep', 'shard')), may hold values from 0 to 63, all different within a row; in each aligned block of 192 rows (0 to 191, 192 to 383, ...) at most 7 rows name the same one
Outputs:
- layer_out: bfloat16 [24576, 768], P(('rep', 'shard'))
- grad_tokens: float32 [24576, 768], P(('rep', 'shard'))
- grad_attn_gain: float32 [768], P('shard')
- grad_w_qkv: float32 [768, 2304], P('shard')
- grad_w_out: float32 [768, 768], P('shard')
- grad_rel_bias: float32 [32, 12], P('shard')
- grad_ffn_gain: float32 [768], P('shard')
- grad_w_router: float32 [768, 64], P('shard')
- grad_w_in: float32 [64, 768, 3072], P('rep', None, 'shard')
- grad_w_back: float32 [64, 3072, 768], P('rep', 'shard')
The draws below stay inside these ranges and needn't reach their ends.
Inputs may be any that keep to these rules, and one draw needn't show every extreme that they name: buckets[0] is 0; from one distance to the next the entry stays or rises by one, and it reaches 31. `choice_ids`: the two experts of a row differ; among the rows of one device no expert is named more than 7 times, and in every draw some expert is named exactly 7 times by the rows of some device.
All inputs are finite; a program needn't handle non-finite values.
Results may differ from the reference program's by a relative error of at most 0.018.
Values may be sent and summed in bfloat16 or wider, within the bound.
A program may use at most 128 MiB of HBM per device.

```python
import math
import jax
import jax.numpy as jnp
import numpy as np
from jax import lax

D = 768
HEADS = 12
HEAD_DIM = 64
FF = 3072
EXPERTS = 64
TOP = 2
BUCKETS = 32
TOK_DEV = 192
SEQ = 384
TOKENS = 24576
CAP = 7
N_REP = 64
N_SHARD = 2


def draw_buckets(key, part):
    cuts = jax.random.permutation(key, SEQ - 1)[:BUCKETS - 1] + 1
    marks = jnp.zeros((SEQ,), jnp.int32).at[cuts].set(1)
    return jnp.cumsum(marks).astype(jnp.int32)


def level_of(rng, dims, split, smallest, high):
    factor_of, own = 1.0, jax.random.fold_in(rng, 6)
    for dim, shards_of in split:
        steps = jnp.exp(jax.random.uniform(jax.random.fold_in(own, dim), (shards_of,), jnp.float32, smallest / len(split), high / len(split)))
        factor_of = factor_of * jnp.repeat(steps, dims[dim] // shards_of).reshape([-1 if axis == dim else 1 for axis in range(len(dims))])
    return factor_of


def routed_block(stream_key, own, number, rows, count, top, limit, lean):
    sequence = jax.random.permutation(stream_key, count)
    crowded, usual = shares(count, rows * top, limit, lean, True), shares(count, rows * top, limit, lean, False)
    places = jnp.arange(count)

    def named(lengths, turn):
        used = int((lengths > 0).sum())
        fixed = max(1, used // 4)
        shifted = fixed + (places - fixed + turn * (used - fixed)) % max(1, count - fixed)
        return jnp.zeros((count,), jnp.int32).at[sequence[jnp.where(places < fixed, places, shifted)]].set(jnp.asarray(lengths, jnp.int32))

    lengths = jnp.where(number % 4 == 0, named(crowded, number // 4), named(usual, number - number // 4 - 1))
    mixed = jax.random.permutation(jax.random.fold_in(own, 3), count)
    donor, receiver = mixed[0:count // 2 * 2:2], mixed[1:count // 2 * 2:2]
    slack = jnp.minimum(lengths[donor] - 1, limit - lengths[receiver]) // 2
    slack = jnp.where((donor == sequence[0]) | (receiver == sequence[0]) | (lengths[receiver] == 0), 0, jnp.maximum(slack, 0))
    shifted = jax.random.randint(jax.random.fold_in(own, 4), (count // 2,), 0, 1 << 20) % (slack + 1)
    lengths = lengths.at[donor].add(-shifted).at[receiver].add(shifted)
    items = jnp.searchsorted(jnp.cumsum(lengths), jnp.arange(rows * top), side="right").astype(jnp.int32)
    table = items.reshape(top, rows).T
    table = table[jax.random.permutation(jax.random.fold_in(own, 1), rows)]
    turn = jax.random.randint(jax.random.fold_in(own, 2), (rows, 1), 0, top)
    return jnp.take_along_axis(table, (jnp.arange(top)[None, :] + turn) % top, axis=1)


def shares(number_of, total, reach, slope, full):
    loads = [(1 << 20) // math.isqrt(grade ** slope) + 1 for grade in range(1, number_of + 1)]
    largest = reach if full else min(reach, max(-(-total // number_of), total * loads[0] // sum(loads)))
    least = 1 if total - largest >= number_of - 1 else 0
    given, surplus = [largest] + [least] * (number_of - 1), total - largest - least * (number_of - 1)
    while surplus > 0:
        free = [i for i in range(1, number_of) if given[i] < largest] or [i for i in range(1, number_of) if given[i] < reach]
        pool, remaining = sum([loads[i] for i in free]), surplus
        for i in free:
            extra = min(reach - given[i], max(1, remaining * loads[i] // pool), surplus)
            given[i] = given[i] + extra
            surplus = surplus - extra
    return np.array(given)


def normal_values(own_key, shape, deviation, reach, split=(), held_as=jnp.bfloat16):
    array = jax.random.normal(own_key, shape, jnp.float32) * deviation
    if len(split) > 0:
        array = level_of(own_key, shape, split, -0.22, 0.18) * array
    return jnp.clip(array, min=-reach, max=reach).astype(held_as)


def setup_inputs(seed: int = 0) -> dict:
    arg_keys = jax.random.split(jax.random.key(seed), 13)
    tokens = normal_values(arg_keys[0], (TOKENS, D), 1.0, 6.0, ((0, 128),))
    cotangent = normal_values(arg_keys[1], (TOKENS, D), 1.0, 6.0, ((0, 128),))
    attn_gain = jnp.clip(1.0 + 0.1 * jax.random.normal(arg_keys[2], (D,), jnp.float32), 0.5, 1.5).astype(jnp.bfloat16)
    w_qkv = normal_values(arg_keys[3], (D, 3 * D), D ** -0.5, 0.21875, ((0, 2),))
    w_out = normal_values(arg_keys[4], (D, D), (D // 64) ** -0.5, 1.75, ((0, 2),))
    rel_bias = normal_values(arg_keys[5], (BUCKETS, HEADS), 0.5, 3.0, ((0, 2),))
    buckets = draw_buckets(jax.random.fold_in(arg_keys[12], 71), 0)
    ffn_gain = jnp.clip(1.0 + 0.1 * jax.random.normal(arg_keys[7], (D,), jnp.float32), 0.5, 1.5).astype(jnp.bfloat16)
    w_router = normal_values(arg_keys[8], (D, EXPERTS), D ** -0.5, 0.21875, ((0, 2),))
    w_in = normal_values(arg_keys[9], (EXPERTS, D, FF), D ** -0.5, 0.21875, ((0, 64), (2, 2)))
    w_back = normal_values(arg_keys[10], (EXPERTS, FF, D), (max(1, 2048 // (EXPERTS * EXPERTS))) ** -0.5, 6.0, ((0, 64), (1, 2)))
    choice_ids_keys = jax.random.split(jax.random.fold_in(arg_keys[11], 1), TOKENS // TOK_DEV)
    choice_ids_turns = jax.random.permutation(jax.random.fold_in(arg_keys[11], 3), TOKENS // TOK_DEV)
    choice_ids = jax.vmap(lambda own, number: routed_block(jax.random.fold_in(arg_keys[11], 2), own, number, TOK_DEV, EXPERTS, TOP, CAP, 0))(choice_ids_keys, choice_ids_turns).reshape((TOKENS, TOP))
    return {"tokens": tokens, "cotangent": cotangent, "attn_gain": attn_gain, "w_qkv": w_qkv, "w_out": w_out, "rel_bias": rel_bias, "buckets": buckets, "ffn_gain": ffn_gain, "w_router": w_router, "w_in": w_in, "w_back": w_back, "choice_ids": choice_ids}


EPSILON = 1e-06
MASKED = -1e+30
HIGH = lax.Precision.HIGHEST

@jax.custom_vjp
def low(v):
    return lax.optimization_barrier(v.astype(jnp.bfloat16)).astype(jnp.float32)

@jax.custom_vjp
def low_back(v):
    return v

def low_keep(v):
    return (low(v), None)

def low_pass(kept, grad):
    return (grad,)

def back_keep(v):
    return (v, None)

def back_low(kept, grad):
    return (low(grad),)
low.defvjp(low_keep, low_pass)
low_back.defvjp(back_keep, back_low)

def rms_scale(values):
    return lax.rsqrt(lax.optimization_barrier(jnp.mean(values * values, axis=-1, keepdims=True)) + EPSILON)

def reference(tokens, cotangent, attn_gain, w_qkv, w_out, rel_bias, buckets, ffn_gain, w_router, w_in, w_back, choice_ids):
    flat_ids = choice_ids.reshape(-1).astype(jnp.int32)
    assigned = flat_ids.shape[0]
    ordering = jnp.argsort(flat_ids, stable=True).astype(jnp.int32)
    sorted_tok = (ordering // TOP).astype(jnp.int32)
    counts = lax.optimization_barrier(jnp.sum((flat_ids[None, :] == jnp.arange(EXPERTS, dtype=jnp.int32)[:, None]).astype(jnp.int32), axis=1)).astype(jnp.int32)
    starts = (jnp.cumsum(counts) - counts).astype(jnp.int32)
    most_rows = N_REP * N_SHARD * CAP
    slot_ids = jnp.arange(most_rows, dtype=jnp.int32)
    position = jnp.arange(SEQ, dtype=jnp.int32)
    distance = position[:, None] - position[None, :]
    causal = distance >= 0
    bucket_of = buckets[jnp.clip(distance, 0, SEQ - 1)]
    score_scale = HEAD_DIM ** (-0.5)
    targets = ordering[jnp.minimum(starts[:, None] + slot_ids[None, :], assigned - 1)]

    def forward(inputs, gain_one, weight_qkv, weight_out, table, gain_two, weight_router, weight_in, weight_back):
        normed_one = low(inputs * rms_scale(inputs) * gain_one)
        projected = low(low_back(jnp.dot(normed_one, weight_qkv, precision=HIGH)))
        bias_full = jnp.transpose(table[bucket_of], (2, 0, 1))

        def attend(seq_rows):
            queries = seq_rows[:, :D].reshape(SEQ, HEADS, HEAD_DIM)
            key_rows = seq_rows[:, D:2 * D].reshape(SEQ, HEADS, HEAD_DIM)
            value_rows = seq_rows[:, 2 * D:].reshape(SEQ, HEADS, HEAD_DIM)
            scores = jnp.einsum('ihd,jhd->hij', queries, key_rows, precision=HIGH) * score_scale + bias_full
            scores = jnp.where(causal[None], low_back(scores), MASKED)
            chances = low(jax.nn.softmax(scores, axis=-1))
            mixed_rows = jnp.einsum('hij,jhd->ihd', chances, value_rows, precision=HIGH)
            return low(low_back(mixed_rows)).reshape(SEQ, D)
        attended = lax.map(jax.checkpoint(attend), projected.reshape(N_REP, SEQ, 3 * D)).reshape(TOKENS, D)
        hidden_one = inputs + low_back(jnp.dot(attended, weight_out, precision=HIGH))
        normed_two = low(hidden_one * rms_scale(hidden_one) * gain_two)
        logits = low_back(jnp.dot(normed_two, weight_router, precision=HIGH))
        router = jax.nn.softmax(logits, axis=-1)
        gate_values = jnp.take_along_axis(router, choice_ids, axis=1)

        def expert(expert_item):
            index, one_in, one_back = expert_item
            live_rows = (slot_ids < counts[index]).astype(inputs.dtype)
            picked_rows = sorted_tok[jnp.minimum(starts[index] + slot_ids, assigned - 1)]
            rows_in = low_back(normed_two[picked_rows])
            pre_act = low_back(jnp.dot(rows_in, one_in, precision=HIGH))
            activated = low(jax.nn.gelu(pre_act))
            result_rows = low(low_back(jnp.dot(activated, one_back, precision=HIGH)))
            return result_rows * live_rows[:, None]
        results = lax.map(jax.checkpoint(expert), (jnp.arange(EXPERTS, dtype=jnp.int32), weight_in, weight_back))
        per_assignment = jnp.zeros((assigned, D), inputs.dtype).at[targets.reshape(-1)].add(results.reshape(-1, D))
        expert_sum = lax.optimization_barrier(jnp.sum(gate_values[:, :, None] * per_assignment.reshape(TOKENS, TOP, D), axis=1))
        return hidden_one + expert_sum
    primals = (tokens.astype(jnp.float32), attn_gain.astype(jnp.float32), w_qkv.astype(jnp.float32), w_out.astype(jnp.float32), rel_bias.astype(jnp.float32), ffn_gain.astype(jnp.float32), w_router.astype(jnp.float32), w_in.astype(jnp.float32), w_back.astype(jnp.float32))
    layer_out, pullback = jax.vjp(forward, *primals)
    grads = pullback(cotangent.astype(jnp.float32))
    return (layer_out.astype(jnp.bfloat16), grads[0], grads[1], grads[2], grads[3], grads[4], grads[5], grads[6], grads[7], grads[8])
```

```python
import functools

import jax
import jax.numpy as jnp
from jax import lax
from jax.experimental import pallas as pl
from jax.experimental.pallas import tpu as pltpu
from jax.sharding import PartitionSpec as P

EPSILON = 1e-06
MASKED = -1e30
MESH = pl.DeviceIdType.MESH
VMEM_SPEC = pl.BlockSpec(memory_space=pltpu.VMEM)
F32 = jnp.float32
BF16 = jnp.bfloat16


def up(number, step):
    return -(-number // step) * step


def greet(peers):
    barrier = pltpu.get_barrier_semaphore()
    for peer in peers:
        pl.semaphore_signal(barrier, inc=1, device_id=peer, device_id_type=MESH)
    pl.semaphore_wait(barrier, len(peers))


def gather_kernel(tok_ref, small_ref, w_ref, tok_out, small_out, w_out, sends, recvs, local):
    rep, mine = lax.axis_index("rep"), lax.axis_index("shard")
    peer = (rep, 1 - mine)
    half = w_out.shape[2] // 3
    greet([peer])
    copies = [
        pltpu.make_async_remote_copy(
            tok_ref, tok_out.at[mine], sends.at[0], recvs.at[0], peer, device_id_type=MESH
        ),
        pltpu.make_async_remote_copy(
            small_ref, small_out.at[mine], sends.at[1], recvs.at[1], peer, device_id_type=MESH
        ),
    ]
    kept = [
        pltpu.make_async_copy(tok_ref, tok_out.at[mine], local.at[0]),
        pltpu.make_async_copy(small_ref, small_out.at[mine], local.at[1]),
    ]
    for block in range(3):
        theirs = pl.ds(pl.multiple_of((2 * block + 1 - mine) * half, 128), half)
        ours = pl.ds(pl.multiple_of((2 * block + mine) * half, 128), half)
        to = w_out.at[mine, :, pl.ds(block * half, half)]
        copies.append(
            pltpu.make_async_remote_copy(
                w_ref.at[:, theirs],
                to,
                sends.at[2 + block],
                recvs.at[2 + block],
                peer,
                device_id_type=MESH,
            )
        )
        kept.append(pltpu.make_async_copy(w_ref.at[:, ours], to, local.at[2 + block]))
    for copy in copies + kept:
        copy.start()
    for copy in copies + kept:
        copy.wait()


def gather_pair(tokens, small, w_qkv):
    rows = w_qkv.shape[0]
    return pl.pallas_call(
        gather_kernel,
        out_shape=[
            jax.ShapeDtypeStruct((2,) + tokens.shape, BF16),
            jax.ShapeDtypeStruct((2,) + small.shape, BF16),
            jax.ShapeDtypeStruct((2, rows, w_qkv.shape[1] // 2), BF16),
        ],
        in_specs=[VMEM_SPEC] * 3,
        out_specs=[VMEM_SPEC] * 3,
        scratch_shapes=[pltpu.SemaphoreType.DMA((5,))] * 3,
        compiler_params=pltpu.CompilerParams(
            collective_id=0, has_side_effects=True, vmem_limit_bytes=24 * 2**20
        ),
    )(tokens, small, w_qkv)


def share_kernel(block_ref, out_ref, send, recv, local):
    rep, mine = lax.axis_index("rep"), lax.axis_index("shard")
    peer = (rep, 1 - mine)
    greet([peer])
    copy = pltpu.make_async_remote_copy(
        block_ref, out_ref.at[mine], send, recv, peer, device_id_type=MESH
    )
    copy.start()
    kept = pltpu.make_async_copy(block_ref, out_ref.at[mine], local)
    kept.start()
    kept.wait()
    copy.wait()


def share_pair(block, number):
    return pl.pallas_call(
        share_kernel,
        out_shape=jax.ShapeDtypeStruct((2,) + block.shape, block.dtype),
        in_specs=[VMEM_SPEC],
        out_specs=VMEM_SPEC,
        scratch_shapes=[pltpu.SemaphoreType.DMA] * 3,
        compiler_params=pltpu.CompilerParams(
            collective_id=number, has_side_effects=True, vmem_limit_bytes=16 * 2**20
        ),
    )(block)


def trade_kernel(parts_ref, out_ref, send, recv):
    rep, mine = lax.axis_index("rep"), lax.axis_index("shard")
    peer = (rep, 1 - mine)
    greet([peer])
    copy = pltpu.make_async_remote_copy(
        parts_ref.at[1 - mine], out_ref, send, recv, peer, device_id_type=MESH
    )
    copy.start()
    copy.wait()


def trade_pair(parts, number):
    return pl.pallas_call(
        trade_kernel,
        out_shape=jax.ShapeDtypeStruct(parts.shape[1:], parts.dtype),
        in_specs=[VMEM_SPEC],
        out_specs=VMEM_SPEC,
        scratch_shapes=[pltpu.SemaphoreType.DMA] * 2,
        compiler_params=pltpu.CompilerParams(
            collective_id=number, has_side_effects=True, vmem_limit_bytes=16 * 2**20
        ),
    )(parts)


def sum_kernel(
    sizes,
    both,
    cut,
    in_ref,
    out_ref,
    chip_in,
    chip,
    row_in,
    column_in,
    row_sum,
    column_sum,
    deep,
    deep_in,
    send,
    recv,
):
    ys, xs, zs = sizes
    rows = in_ref.shape[2]
    rep, mine = lax.axis_index("rep"), lax.axis_index("shard")
    core = lax.rem(rep, 2)
    z = lax.rem(rep // 2, zs)
    x = lax.rem(rep // (2 * zs), xs)
    y = rep // (2 * zs * xs)

    def place(y_at, x_at, z_at, core_at):
        return ((y_at * xs + x_at) * zs + z_at) * 2 + core_at

    xp = [lax.rem(x + step, xs) for step in range(1, xs)]
    yp = [lax.rem(y + step, ys) for step in range(1, ys)]
    zp = [lax.rem(z + step, zs) for step in range(1, zs)]
    core_peer = (place(y, x, z, 1 - core), mine)
    x_peers = [(place(y, at, z, core), mine) for at in xp]
    y_peers = [(place(at, x, z, core), mine) for at in yp]
    z_peers = [(place(y, x, at, core), mine) for at in zp]
    pair_peer = (rep, 1 - mine)
    greet([core_peer, pair_peer] + x_peers + y_peers + z_peers)
    number = [0]

    def send_to(source, target, peer):
        i = number[0]
        number[0] += 1
        copy = pltpu.make_async_remote_copy(
            source, target, send.at[i], recv.at[i], peer, device_id_type=MESH
        )
        copy.start()
        return copy

    def finish(copies):
        for copy in copies:
            copy.wait()

    first, second = pl.ds(0, cut), pl.ds(cut, rows - cut)

    finish([send_to(in_ref.at[:, 1 - core], chip_in, core_peer)])

    def add_chip(i, carry):
        total = in_ref[i, core].astype(F32) + chip_in[i].astype(F32)
        chip[i // (xs * zs), lax.rem(i // zs, xs), lax.rem(i, zs)] = total.astype(BF16)
        return carry

    lax.fori_loop(0, ys * xs * zs, add_chip, 0)
    copies = [
        send_to(chip.at[:, at, :, first], row_in.at[i], peer)
        for i, (at, peer) in enumerate(zip(xp, x_peers))
    ]
    copies += [
        send_to(chip.at[at, :, :, second], column_in.at[i], peer)
        for i, (at, peer) in enumerate(zip(yp, y_peers))
    ]
    finish(copies)

    def add_row(i, carry):
        for k in range(zs):
            total = chip[i, x, k, first].astype(F32)
            for j in range(xs - 1):
                total = total + row_in[j, i, k].astype(F32)
            row_sum[i, k] = total.astype(BF16)
        return carry

    def add_column(i, carry):
        for k in range(zs):
            total = chip[y, i, k, second].astype(F32)
            for j in range(ys - 1):
                total = total + column_in[j, i, k].astype(F32)
            column_sum[i, k] = total.astype(BF16)
        return carry

    lax.fori_loop(0, ys, add_row, 0)
    lax.fori_loop(0, xs, add_column, 0)
    copies = [
        send_to(row_sum.at[at], row_in.at[xs - 1 + i, 0], peer)
        for i, (at, peer) in enumerate(zip(yp, y_peers))
    ]
    copies += [
        send_to(column_sum.at[at], column_in.at[ys - 1 + i, 0], peer)
        for i, (at, peer) in enumerate(zip(xp, x_peers))
    ]
    finish(copies)
    for k in range(zs):
        total = row_sum[y, k].astype(F32)
        for i in range(ys - 1):
            total = total + row_in[xs - 1 + i, 0, k].astype(F32)
        deep[k, first] = total.astype(BF16)
        total = column_sum[x, k].astype(F32)
        for i in range(xs - 1):
            total = total + column_in[ys - 1 + i, 0, k].astype(F32)
        deep[k, second] = total.astype(BF16)
    finish(
        [send_to(deep.at[at], deep_in.at[i], peer) for i, (at, peer) in enumerate(zip(zp, z_peers))]
    )
    total = deep[z].astype(F32)
    for i in range(zs - 1):
        total = total + deep_in[i].astype(F32)
    done = total.astype(BF16)
    own = pl.ds(pl.multiple_of(mine * both, 16), both)
    other = pl.ds(pl.multiple_of((1 - mine) * both, 16), both)
    deep_in[zs - 1] = done
    out = out_ref.at[y, x, z, core]
    copies = [send_to(deep_in.at[zs - 1, other], out.at[own], pair_peer)]
    kept = pltpu.make_async_copy(deep_in.at[zs - 1, own], out.at[own], send.at[number[0]])
    kept.start()
    rest = pl.ds(2 * both, rows - 2 * both)
    out_ref[y, x, z, core, rest] = done[2 * both :]
    kept.wait()
    finish(copies)
    number[0] += 1
    finish([send_to(out, out, peer) for peer in z_peers])
    firsts, seconds = (
        out_ref.at[y, x, :, core, first],
        out_ref.at[y, x, :, core, second],
    )
    copies = [send_to(firsts, firsts, peer) for peer in y_peers]
    copies += [send_to(seconds, seconds, peer) for peer in x_peers]
    finish(copies)
    firsts, seconds = (
        out_ref.at[:, x, :, core, first],
        out_ref.at[y, :, :, core, second],
    )
    copies = [send_to(firsts, firsts, peer) for peer in x_peers]
    copies += [send_to(seconds, seconds, peer) for peer in y_peers]
    finish(copies)
    whole = out_ref.at[:, :, :, core]
    finish([send_to(whole, whole, core_peer)])


def sum_all(chunks, both, sizes):
    ys, xs, zs = sizes
    count, rows, lanes = chunks.shape
    cut = up(rows // 2, 16)
    per_core = count // 2
    many = 4 * (xs + ys) + 2 * zs
    result = pl.pallas_call(
        functools.partial(sum_kernel, sizes, both, cut),
        out_shape=jax.ShapeDtypeStruct((ys, xs, zs, 2, rows, lanes), BF16),
        in_specs=[VMEM_SPEC],
        out_specs=VMEM_SPEC,
        scratch_shapes=[
            pltpu.VMEM((per_core, rows, lanes), BF16),
            pltpu.VMEM((ys, xs, zs, rows, lanes), BF16),
            pltpu.VMEM((xs + ys - 2, ys, zs, cut, lanes), BF16),
            pltpu.VMEM((xs + ys - 2, xs, zs, rows - cut, lanes), BF16),
            pltpu.VMEM((ys, zs, cut, lanes), BF16),
            pltpu.VMEM((xs, zs, rows - cut, lanes), BF16),
            pltpu.VMEM((zs, rows, lanes), BF16),
            pltpu.VMEM((zs, rows, lanes), BF16),
            pltpu.SemaphoreType.DMA((many,)),
            pltpu.SemaphoreType.DMA((many,)),
        ],
        compiler_params=pltpu.CompilerParams(
            collective_id=5, has_side_effects=True, vmem_limit_bytes=40 * 2**20
        ),
    )(chunks.reshape(per_core, 2, rows, lanes))
    return result.reshape(count, rows, lanes)


def rms_factor(values):
    return lax.rsqrt(jnp.mean(values * values, axis=-1, keepdims=True) + EPSILON)


def rms_backward(values, factor, gain_row, grad_normed):
    unit_rows = values * factor
    grad_unit = grad_normed * gain_row
    grad_gain = jnp.sum(grad_normed * unit_rows, axis=0)
    inner = jnp.mean(grad_unit * unit_rows, axis=-1, keepdims=True)
    return (factor * (grad_unit - unit_rows * inner), grad_gain)


def dot(a, b, contract):
    return lax.dot_general(a, b, (contract, ((), ())), preferred_element_type=F32)


def tiles(matrix):
    rows, columns = matrix.shape
    return matrix.reshape(rows, columns // 128, 128).transpose(1, 0, 2).reshape(-1, 128)


def untile(stack, rows):
    return stack.reshape(-1, rows, 128).transpose(1, 0, 2).reshape(rows, -1)


def to_chunks(stack, count):
    rows = up(stack.shape[0], 16 * count)
    return jnp.pad(stack, ((0, rows - stack.shape[0]), (0, 0))).reshape(count, rows // count, 128)


def body(
    sizes,
    tokens,
    cotangent,
    attn_gain,
    w_qkv,
    w_out,
    rel_bias,
    buckets,
    ffn_gain,
    w_router,
    w_in,
    w_back,
    choice_ids,
):
    rows, width = tokens.shape
    half = width // 2
    bucket_half, heads = rel_bias.shape
    head = width // heads
    own_heads = heads // 2
    experts = w_router.shape[1]
    top = choice_ids.shape[1]
    capacity = up(max(2, 5 * rows * top // (4 * experts)), 8)
    slots = experts * capacity
    scale = head ** (-0.5)
    mine = lax.axis_index("shard")
    seq = 2 * rows

    small = jnp.zeros((half + bucket_half, 128), BF16)
    small = small.at[:half, :experts].set(w_router)
    small = small.at[:half, experts].set(attn_gain).at[:half, experts + 1].set(ffn_gain)
    small = small.at[half:, :heads].set(rel_bias)
    tok_all, small_all, w_all = gather_pair(tokens, small, w_qkv)
    features = small_all[:, :half].reshape(width, 128)
    router_full = features[:, :experts]
    gain_one = features[:, experts].astype(F32)
    gain_two = features[:, experts + 1].astype(F32)
    table = small_all[:, half:, :heads].reshape(2 * bucket_half, heads)
    table_own = lax.dynamic_slice_in_dim(table, mine * own_heads, own_heads, 1)
    w_own = w_all.reshape(width, 3 * half)

    pair_inputs = tok_all.reshape(seq, width).astype(F32)
    normed_one = (pair_inputs * rms_factor(pair_inputs) * gain_one).astype(BF16)
    projected = dot(normed_one, w_own, ((1,), (0,))).astype(BF16)
    queries, keys, values = (
        projected[:, i * half : (i + 1) * half].reshape(seq, own_heads, head) for i in range(3)
    )
    position = jnp.arange(seq, dtype=jnp.int32)
    distance = position[:, None] - position[None, :]
    levels = jnp.arange(2 * bucket_half, dtype=jnp.int32)
    low = jnp.sum((buckets[None, :] < levels[:, None]).astype(jnp.int32), axis=1)
    high = jnp.concatenate([low[1:], jnp.full((1,), seq, jnp.int32)])
    one_hot = (
        (distance[None] >= low[:, None, None]) & (distance[None] < high[:, None, None])
    ).astype(BF16)
    bias = jnp.einsum("bh,bij->hij", table_own, one_hot, preferred_element_type=F32)
    scores = jnp.einsum("ihd,jhd->hij", queries, keys, preferred_element_type=F32) * scale + bias
    scores = jnp.where((distance >= 0)[None], scores, MASKED)
    peak = jnp.max(scores, axis=-1, keepdims=True)
    raised = jnp.exp(scores - peak)
    chances = raised / jnp.sum(raised, axis=-1, keepdims=True)
    chances_low = chances.astype(BF16)
    mixed = (
        jnp.einsum("hij,jhd->ihd", chances_low, values, preferred_element_type=F32)
        .astype(BF16)
        .reshape(seq, half)
    )
    attended = dot(mixed, w_out, ((1,), (0,))).reshape(2, rows, width)
    attended_other = trade_pair(attended.astype(BF16), 1)
    inputs = tokens.astype(F32)
    hidden_one = (
        inputs
        + lax.dynamic_index_in_dim(attended, mine, 0, keepdims=False)
        + attended_other.astype(F32)
    )

    factor_two = rms_factor(hidden_one)
    normed_two = (hidden_one * factor_two * gain_two).astype(BF16)
    logits = dot(normed_two, router_full, ((1,), (0,)))
    router = jax.nn.softmax(logits, axis=-1)
    levels = jnp.arange(experts, dtype=jnp.int32)
    chosen = (choice_ids[:, :, None] == levels).astype(F32)
    gates = jnp.sum(chosen * router[:, None, :], axis=2)
    flat_ids = choice_ids.reshape(-1)
    member = (flat_ids[:, None] == levels[None, :]).astype(BF16)
    order = jnp.arange(rows * top, dtype=jnp.int32)
    before = (order[:, None] > order[None, :]).astype(BF16)
    earlier = dot(before, member, ((1,), (0,)))
    rank = jnp.sum(earlier * member.astype(F32), axis=1).astype(jnp.int32)
    slot = (flat_ids * capacity + rank).reshape(rows, top)
    combine = (slot[:, :, None] == jnp.arange(slots, dtype=jnp.int32)).astype(BF16)
    dispatch = jnp.sum(combine, axis=1)
    grad_out = cotangent.astype(F32)
    grad_picked = (gates[:, :, None] * grad_out[:, None, :]).astype(BF16)

    def to_experts(out_rows):
        blocks = out_rows.reshape(experts, 1, capacity, width)
        blocks = jnp.broadcast_to(blocks, (experts, 2, capacity, width))
        blocks = blocks.reshape(2 * experts, capacity, width)
        got = lax.all_to_all(blocks, ("rep", "shard"), split_axis=0, concat_axis=0, tiled=True)
        return got.reshape(2 * slots, width)

    def to_tokens(expert_rows):
        blocks = expert_rows.reshape(2 * experts, capacity, width)
        got = lax.all_to_all(blocks, ("rep", "shard"), split_axis=0, concat_axis=0, tiled=True)
        both = jnp.sum(got.reshape(experts, 2, capacity, width).astype(F32), axis=1)
        return both.astype(BF16).reshape(slots, width)

    arrived = to_experts(dot(dispatch, normed_two, ((0,), (0,))).astype(BF16))
    sent_grads = dot(
        combine.reshape(rows * top, slots), grad_picked.reshape(rows * top, width), ((0,), (0,))
    ).astype(BF16)
    grad_result = to_experts(sent_grads)

    expert_in, expert_back = w_in[0], w_back[0]
    pre = dot(arrived, expert_in, ((1,), (0,)))
    activated, gelu_pullback = jax.vjp(jax.nn.gelu, pre)
    activated = activated.astype(BF16)
    result = dot(activated, expert_back, ((1,), (0,))).astype(BF16)
    returned = to_tokens(result)
    grad_active = dot(grad_result, expert_back, ((1,), (1,)))
    grad_pre = gelu_pullback(grad_active)[0].astype(BF16)
    grad_arrived = dot(grad_pre, expert_in, ((1,), (1,))).astype(BF16)
    grad_sent = to_tokens(grad_arrived)
    grad_back_expert = dot(activated, grad_result, ((0,), (0,)))
    grad_in_expert = dot(arrived, grad_pre, ((0,), (0,)))

    picked = jnp.einsum("rms,sd->rmd", combine, returned, preferred_element_type=F32)
    hidden_two = hidden_one + jnp.sum(gates[:, :, None] * picked, axis=1)
    grad_gates = jnp.sum(grad_out[:, None, :] * picked, axis=2)
    grad_normed_two = dot(dispatch, grad_sent, ((1,), (0,)))
    grad_chances = jnp.sum(chosen * grad_gates[:, :, None], axis=1)
    grad_logits = (
        router * (grad_chances - jnp.sum(router * grad_chances, axis=-1, keepdims=True))
    ).astype(BF16)
    grad_router = dot(normed_two, grad_logits, ((0,), (0,)))
    grad_normed_two = grad_normed_two + dot(grad_logits, router_full, ((1,), (1,)))
    grad_norm, grad_gain_two = rms_backward(hidden_one, factor_two, gain_two, grad_normed_two)
    grad_hidden = grad_out + grad_norm

    grad_attended = share_pair(grad_hidden.astype(BF16), 2).reshape(seq, width)
    grad_w_out = dot(mixed, grad_attended, ((0,), (0,)))
    grad_mixed = dot(grad_attended, w_out, ((1,), (1,))).astype(BF16)
    grad_mixed = grad_mixed.reshape(seq, own_heads, head)
    grad_chance = jnp.einsum("ihd,jhd->hij", grad_mixed, values, preferred_element_type=F32)
    inner = jnp.sum(chances * grad_chance, axis=-1, keepdims=True)
    grad_scores = (chances * (grad_chance - inner)).astype(BF16)
    grad_table = jnp.einsum("hij,bij->bh", grad_scores, one_hot, preferred_element_type=F32)
    grad_q = jnp.einsum("hij,jhd->ihd", grad_scores, keys, preferred_element_type=F32) * scale
    grad_k = jnp.einsum("hij,ihd->jhd", grad_scores, queries, preferred_element_type=F32) * scale
    grad_v = jnp.einsum("hij,ihd->jhd", chances_low, grad_mixed, preferred_element_type=F32)
    grad_projected = jnp.concatenate(
        [grad.reshape(seq, half) for grad in (grad_q, grad_k, grad_v)], axis=1
    ).astype(BF16)
    grad_w_qkv = dot(normed_one, grad_projected, ((0,), (0,)))
    grad_normed = dot(grad_projected, w_own, ((1,), (1,))).reshape(2, rows, width)
    grad_other = trade_pair(grad_normed.astype(BF16), 3)
    grad_normed_one = lax.dynamic_index_in_dim(
        grad_normed, mine, 0, keepdims=False
    ) + grad_other.astype(F32)
    grad_norm, grad_gain_one = rms_backward(inputs, rms_factor(inputs), gain_one, grad_normed_one)
    grad_inputs = grad_hidden + grad_norm

    table_wide = jnp.zeros((2 * bucket_half, 128), F32)
    table_wide = lax.dynamic_update_slice(table_wide, grad_table, (0, mine * own_heads))
    misc = jnp.zeros((width, 128), F32)
    misc = misc.at[:, :experts].set(grad_router)
    misc = misc.at[:, experts].set(grad_gain_one).at[:, experts + 1].set(grad_gain_two)
    replicas = experts
    per_half = []
    for i in range(2):
        part = [
            tiles(grad_w_qkv[i * half : (i + 1) * half].astype(BF16)),
            misc[i * half : (i + 1) * half].astype(BF16),
            table_wide[i * bucket_half : (i + 1) * bucket_half].astype(BF16),
        ]
        per_half.append(to_chunks(jnp.concatenate(part, axis=0), replicas))
    both = per_half[0].shape[1]
    per_half.append(to_chunks(tiles(grad_w_out.astype(BF16)), replicas))
    total = sum_all(jnp.concatenate(per_half, axis=1), both, sizes)
    qkv_rows = half * 3 * half // 128
    parts = [total[:, i * both : (i + 1) * both].reshape(-1, 128) for i in range(2)]
    qkv = [untile(part[:qkv_rows], half).reshape(half, 3, half) for part in parts]
    qkv = jnp.stack(qkv, axis=2).reshape(half, 6 * half).astype(F32)
    misc = parts[0][qkv_rows:].astype(F32) + parts[1][qkv_rows:].astype(F32)
    sum_out = total[:, 2 * both :].reshape(-1, 128)[: half * width // 128]
    sum_out = untile(sum_out, half).astype(F32)
    return (
        hidden_two.astype(BF16),
        grad_inputs,
        misc[:half, experts],
        qkv,
        sum_out,
        misc[half : half + bucket_half, :heads],
        misc[:half, experts + 1],
        misc[:half, :experts],
        grad_in_expert[None],
        grad_back_expert[None],
    )


SIZES = {64: (4, 4, 2), 4: (2, 1, 1), 8: (2, 2, 1)}


def solution(mesh):
    in_specs = (
        P(("rep", "shard"), None),
        P(("rep", "shard"), None),
        P("shard"),
        P("shard", None),
        P("shard", None),
        P("shard", None),
        P(),
        P("shard"),
        P("shard", None),
        P("rep", None, "shard"),
        P("rep", "shard", None),
        P(("rep", "shard"), None),
    )
    out_specs = (
        P(("rep", "shard"), None),
        P(("rep", "shard"), None),
        P("shard"),
        P("shard", None),
        P("shard", None),
        P("shard", None),
        P("shard"),
        P("shard", None),
        P("rep", None, "shard"),
        P("rep", "shard", None),
    )
    sizes = SIZES[mesh.shape["rep"]]
    return jax.shard_map(
        functools.partial(body, sizes),
        mesh=mesh,
        in_specs=in_specs,
        out_specs=out_specs,
        check_vma=False,
    )
```

```python
import functools

import jax
import jax.numpy as jnp
from jax import lax
from jax.experimental import pallas as pl
from jax.experimental.pallas import tpu as pltpu
from jax.sharding import PartitionSpec as P

EPSILON = 1e-06
MASKED = -1e30
MESH = pl.DeviceIdType.MESH
VMEM_SPEC = pl.BlockSpec(memory_space=pltpu.VMEM)
F32 = jnp.float32
BF16 = jnp.bfloat16


def up(number, step):
    return -(-number // step) * step


def greet(peers):
    barrier = pltpu.get_barrier_semaphore()
    for peer in peers:
        pl.semaphore_signal(barrier, inc=1, device_id=peer, device_id_type=MESH)
    pl.semaphore_wait(barrier, len(peers))


def iota(shape, axis):
    return lax.broadcasted_iota(jnp.int32, shape, axis)


def dot(a, b, contract):
    return lax.dot_general(a, b, (contract, ((), ())), preferred_element_type=F32)


def matmul(a, b):
    return dot(a, b, ((1,), (0,)))


def matmul_t(a, b):
    return dot(a, b, ((1,), (1,)))


def t_matmul(a, b):
    return dot(a, b, ((0,), (0,)))


def two_parts(values):
    high = values.astype(BF16)
    return high, (values - high.astype(F32)).astype(BF16)


def rms_factor(values):
    return lax.rsqrt(jnp.mean(values * values, axis=-1, keepdims=True) + EPSILON)


def gain_row(small_ref, half, first):
    blocks = half // 128
    pieces = [
        small_ref[side, pl.ds(half + first + i, 1), :].astype(F32)
        for side in range(2)
        for i in range(blocks)
    ]
    return jnp.concatenate(pieces, axis=1)


def router_weight(small_ref, half):
    return jnp.concatenate([small_ref[0, :half, :], small_ref[1, :half, :]], axis=0)


def front_kernel(
    sizes,
    dims,
    tok_ref,
    small_ref,
    wqkv_ref,
    wout_ref,
    bucket_ref,
    dispatch_ref,
    n1_ref,
    proj_ref,
    chance_ref,
    mixed_ref,
    w_all,
    small_all,
    hidden_ref,
    n2_ref,
    router_ref,
    outgoing_ref,
    tok_all,
    bias_rows,
    part_out,
    part_in,
    send,
    recv,
    local,
):
    heads, experts, capacity, buckets = dims
    ys, xs, zs = sizes
    rows, width = tok_ref.shape
    half = width // 2
    seq = 2 * rows
    own_heads = heads // 2
    head = width // heads
    slots = experts * capacity
    rep, mine = lax.axis_index("rep"), lax.axis_index("shard")
    other = 1 - mine
    core = lax.rem(rep, 2)
    peer = (rep, other)
    core_peer = (rep + 1 - 2 * core, mine)
    peers = [peer, core_peer]
    if zs == 2:
        z = lax.rem(rep // 2, 2)
        far_peer = (rep + 2 * (1 - 2 * z), other)
        peers.append(far_peer)
    greet(peers)

    def remote(i, source, target, to):
        copy = pltpu.make_async_remote_copy(
            source, target, send.at[i], recv.at[i], to, device_id_type=MESH
        )
        copy.start()
        return copy

    small_copy = remote(0, small_ref, small_all.at[mine], peer)
    near = half // 2 if zs == 1 else up(half // 12, 16)
    fetched = [(peer, 0, near)]
    if zs == 2:
        fetched.append((far_peer, near, half // 2 - near))
    weight_copies = []
    for j, (to, first, count) in enumerate(fetched):
        at = pl.ds(pl.multiple_of(core * (half // 2) + first, 16), count)
        for block in range(3):
            theirs = pl.ds(pl.multiple_of((2 * block + other) * half, 128), half)
            weight_copies.append(
                remote(
                    2 + 3 * j + block,
                    wqkv_ref.at[at, theirs],
                    w_all.at[mine, at, pl.ds(block * half, half)],
                    to,
                )
            )
    tok_copy = remote(1, tok_ref, tok_all.at[mine], peer)
    kept = [
        pltpu.make_async_copy(tok_ref, tok_all.at[mine], local.at[0]),
        pltpu.make_async_copy(small_ref, small_all.at[mine], local.at[1]),
    ]
    for block in range(3):
        ours = pl.ds(pl.multiple_of((2 * block + mine) * half, 128), half)
        kept.append(
            pltpu.make_async_copy(
                wqkv_ref.at[:, ours], w_all.at[mine, :, pl.ds(block * half, half)], local.at[2 + block]
            )
        )
    for copy in kept:
        copy.start()
    for copy in kept:
        copy.wait()
    small_copy.wait()

    table = jnp.concatenate([small_all[0, half + 16 :, :], small_all[1, half + 16 :, :]], axis=0)
    levels = iota((buckets, 2 * seq), 0)
    one_hot = (levels == bucket_ref[...]).astype(F32).astype(BF16)
    bias_rows[...] = t_matmul(table, one_hot)
    gain_one = gain_row(small_all, half, 0)
    gain_two = gain_row(small_all, half, half // 128)

    for copy in weight_copies:
        copy.wait()
    got = w_all.at[other, pl.ds(pl.multiple_of(core * (half // 2), 16), half // 2)]
    passed = remote(8, got, got, core_peer)
    tok_copy.wait()
    for side in range(2):
        values = tok_all[side].astype(F32)
        n1_ref[side * rows : (side + 1) * rows, :] = (
            values * rms_factor(values) * gain_one
        ).astype(BF16)
    passed.wait()
    normed = n1_ref[...]
    for block in range(3):
        columns = pl.ds(block * half, half)
        total = matmul(normed[:, :half], w_all[0, :, columns])
        total = total + matmul(normed[:, half:], w_all[1, :, columns])
        proj_ref[:, columns] = total.astype(BF16)

    scale = head ** (-0.5)
    causal = iota((seq, seq), 0) >= iota((seq, seq), 1)
    for h in range(own_heads):
        at = h * head
        query = proj_ref[:, at : at + head]
        key = proj_ref[:, half + at : half + at + head]
        value = proj_ref[:, 2 * half + at : 2 * half + at + head]
        row = bias_rows[pl.ds(mine * own_heads + h, 1), :]
        bias = pltpu.roll(
            jnp.broadcast_to(row, (seq, 2 * seq)), 0, 1, stride=1, stride_axis=0
        )[:, :seq]
        scores = jnp.where(causal, matmul_t(query, key) * scale + bias, MASKED)
        raised = jnp.exp(scores - jnp.max(scores, axis=-1, keepdims=True))
        chance = (raised / jnp.sum(raised, axis=-1, keepdims=True)).astype(BF16)
        chance_ref[h] = chance
        mixed_ref[:, at : at + head] = matmul(chance, value).astype(BF16)

    theirs = pl.ds(pl.multiple_of(other * rows, 16), rows)
    ours = pl.ds(pl.multiple_of(mine * rows, 16), rows)
    part_out[...] = matmul(mixed_ref[theirs, :], wout_ref[...]).astype(BF16)
    part_copy = remote(9, part_out, part_in, peer)
    hidden = tok_ref[...].astype(F32) + matmul(mixed_ref[ours, :], wout_ref[...])
    part_copy.wait()
    hidden = hidden + part_in[...].astype(F32)
    hidden_ref[...] = hidden
    normed = (hidden * rms_factor(hidden) * gain_two).astype(BF16)
    n2_ref[...] = normed
    logits = matmul(normed, router_weight(small_all, half))
    logits = jnp.where(iota((rows, 128), 1) < experts, logits, MASKED)
    raised = jnp.exp(logits - jnp.max(logits, axis=-1, keepdims=True))
    router = raised / jnp.sum(raised, axis=-1, keepdims=True)
    router_ref[...] = router

    dispatch = dispatch_ref[...]
    shift = capacity.bit_length() - 1
    spread = (iota((128, slots), 0) == (iota((128, slots), 1) >> shift)).astype(F32).astype(BF16)
    row_of, slot_of = iota((slots, slots), 0), iota((slots, slots), 1)
    carrier = ((row_of & (capacity - 1)) == capacity - 1) & (
        (row_of >> shift) == (slot_of >> shift)
    )
    place = iota((slots, 128), 0) & (capacity - 1)
    gates = jnp.zeros((slots, 128), F32)
    for i, part in enumerate(two_parts(router)):
        gate = jnp.sum(matmul(part, spread) * dispatch.astype(F32), axis=0, keepdims=True)
        left = jnp.where(carrier, gate, 0.0).astype(BF16)
        right = (place == iota((slots, 128), 1) - i * capacity).astype(F32).astype(BF16)
        gates = gates + matmul(left, right)
    sent = t_matmul(dispatch, normed)
    outgoing_ref[...] = sent.astype(BF16)
    outgoing_ref[:, :128] = (sent[:, :128] + gates).astype(BF16)


def front(sizes, dims, tokens, small, w_qkv, w_out, bucket_row, dispatch):
    rows, width = tokens.shape
    heads, experts, capacity, buckets = dims
    half, seq, slots = width // 2, 2 * rows, experts * capacity
    shapes = [
        ((seq, width), BF16),
        ((seq, 3 * half), BF16),
        ((heads // 2, seq, seq), BF16),
        ((seq, half), BF16),
        ((2, half, 3 * half), BF16),
        ((2,) + small.shape, BF16),
        ((rows, width), F32),
        ((rows, width), BF16),
        ((rows, 128), F32),
        ((slots, width), BF16),
    ]
    return pl.pallas_call(
        functools.partial(front_kernel, sizes, dims),
        out_shape=[jax.ShapeDtypeStruct(*shape) for shape in shapes],
        in_specs=[VMEM_SPEC] * 6,
        out_specs=[VMEM_SPEC] * len(shapes),
        scratch_shapes=[
            pltpu.VMEM((2, rows, width), BF16),
            pltpu.VMEM((128, 2 * seq), F32),
            pltpu.VMEM((rows, width), BF16),
            pltpu.VMEM((rows, width), BF16),
            pltpu.SemaphoreType.DMA((10,)),
            pltpu.SemaphoreType.DMA((10,)),
            pltpu.SemaphoreType.DMA((5,)),
        ],
        compiler_params=pltpu.CompilerParams(
            collective_id=0, has_side_effects=True, vmem_limit_bytes=48 * 2**20
        ),
        cost_estimate=pl.CostEstimate(flops=30 * 10**9, bytes_accessed=10**8, transcendentals=10**6),
    )(tokens, small, w_qkv, w_out, bucket_row, dispatch)


def back_kernel(
    sizes,
    dims,
    both,
    cut,
    sent_ref,
    dispatch_ref,
    gout_ref,
    tok_ref,
    n1_ref,
    proj_ref,
    chance_ref,
    mixed_ref,
    w_all,
    small_all,
    hidden_ref,
    n2_ref,
    router_ref,
    wout_ref,
    bucket_ref,
    gtok_ref,
    gqkv_ref,
    gout_w_ref,
    grouter_ref,
    gsmall_ref,
    att_all,
    dqkv,
    sums,
    part_out,
    part_in,
    comm,
    total_ref,
    chip_in,
    chip,
    row_in,
    column_in,
    row_sum,
    column_sum,
    deep,
    deep_in,
    send,
    recv,
):
    heads, experts, capacity, buckets = dims
    ys, xs, zs = sizes
    rows, width = tok_ref.shape
    half = width // 2
    seq = 2 * rows
    own_heads = heads // 2
    head = width // heads
    blocks = half // 128
    chunk_rows = comm.shape[2]
    rep, mine = lax.axis_index("rep"), lax.axis_index("shard")
    other = 1 - mine
    core = lax.rem(rep, 2)
    z = lax.rem(rep // 2, zs)
    x = lax.rem(rep // (2 * zs), xs)
    y = rep // (2 * zs * xs)

    def place(y_at, x_at, z_at, core_at):
        return ((y_at * xs + x_at) * zs + z_at) * 2 + core_at

    xp = [lax.rem(x + step, xs) for step in range(1, xs)]
    yp = [lax.rem(y + step, ys) for step in range(1, ys)]
    zp = [lax.rem(z + step, zs) for step in range(1, zs)]
    core_peer = (place(y, x, z, 1 - core), mine)
    x_peers = [(place(y, at, z, core), mine) for at in xp]
    y_peers = [(place(at, x, z, core), mine) for at in yp]
    z_peers = [(place(y, x, at, core), mine) for at in zp]
    peer = (rep, other)
    greet([core_peer, peer] + x_peers + y_peers + z_peers)
    number = [0]

    def send_to(source, target, to):
        i = number[0]
        number[0] += 1
        copy = pltpu.make_async_remote_copy(
            source, target, send.at[i], recv.at[i], to, device_id_type=MESH
        )
        copy.start()
        return copy

    def finish(copies):
        for copy in copies:
            copy.wait()

    shift = capacity.bit_length() - 1
    wide = 2 * experts * capacity
    row_of, slot_of = iota((wide, wide), 1), iota((wide, wide), 0)
    carrier = (row_of == ((slot_of >> shift) << shift) + capacity - 1).astype(F32).astype(BF16)
    carried = matmul(carrier, sent_ref[:, :128])
    lane = iota((wide, 128), 1)
    slot = iota((wide, 128), 0)
    mask = ((lane & (capacity - 1)) == (slot & (capacity - 1))) & (lane < 2 * capacity)
    d_gate = jnp.sum(jnp.where(mask, carried, 0.0), axis=1, keepdims=True)
    d_gate = jnp.where((slot >> (shift + 1)) == lane, d_gate, 0.0)
    dispatch = dispatch_ref[...]
    high, low = two_parts(d_gate)
    d_router = matmul(dispatch, high) + matmul(dispatch, low)
    router = router_ref[...]
    d_logits = router * (d_router - jnp.sum(router * d_router, axis=-1, keepdims=True))
    d_logits = d_logits.astype(BF16)
    d_n2 = matmul(dispatch, sent_ref[...]) + matmul_t(d_logits, router_weight(small_all, half))
    hidden = hidden_ref[...]
    factor = rms_factor(hidden)
    unit = hidden * factor
    scaled = d_n2 * gain_row(small_all, half, blocks)
    d_hidden = gout_ref[...].astype(F32) + factor * (
        scaled - unit * jnp.mean(scaled * unit, axis=-1, keepdims=True)
    )
    att_all[mine] = d_hidden.astype(BF16)
    shared = send_to(att_all.at[mine], att_all.at[mine], peer)
    gtok_ref[...] = d_hidden
    g_gain_two = jnp.sum(d_n2 * unit, axis=0, keepdims=True)
    g_router = t_matmul(n2_ref[...], d_logits)

    def store(part, first, block):
        base = part * both
        span = both if part < 2 else chunk_rows - 2 * both
        at = 0
        while at < block.shape[0]:
            chunk_at, inside = divmod(first + at, span)
            count = min(span - inside, block.shape[0] - at)
            comm[chunk_at // 2, chunk_at % 2, base + inside : base + inside + count, :] = block[
                at : at + count
            ]
            at += count

    tile_rows = 3 * blocks * half
    for side in range(2):
        store(side, tile_rows, g_router[side * half : (side + 1) * half].astype(BF16))
    shared.wait()

    d_att = [att_all[0], att_all[1]]
    for block in range(2 * blocks):
        columns = slice(block * 128, (block + 1) * 128)
        grad = t_matmul(mixed_ref[:rows, :], d_att[0][:, columns])
        grad = grad + t_matmul(mixed_ref[rows:, :], d_att[1][:, columns])
        store(2, block * half, grad.astype(BF16))
    d_mixed = jnp.concatenate(
        [matmul_t(part, wout_ref[...]).astype(BF16) for part in d_att], axis=0
    )
    scale = head ** (-0.5)
    flip = (iota((seq, seq), 0) + iota((seq, seq), 1) == seq - 1).astype(F32).astype(BF16)
    for h in range(own_heads):
        at = h * head
        query = proj_ref[:, at : at + head]
        key = proj_ref[:, half + at : half + at + head]
        value = proj_ref[:, 2 * half + at : 2 * half + at + head]
        d_o = d_mixed[:, at : at + head]
        chance = chance_ref[h]
        d_chance = matmul_t(d_o, value)
        wide_chance = chance.astype(F32)
        inner = jnp.sum(wide_chance * d_chance, axis=-1, keepdims=True)
        d_scores = (wide_chance * (d_chance - inner)).astype(BF16)
        dqkv[:, at : at + head] = (matmul(d_scores, key) * scale).astype(BF16)
        dqkv[:, half + at : half + at + head] = (t_matmul(d_scores, query) * scale).astype(BF16)
        dqkv[:, 2 * half + at : 2 * half + at + head] = t_matmul(chance, d_o).astype(BF16)
        flipped = matmul(flip, d_scores)
        flipped = jnp.concatenate([flipped, jnp.zeros((seq, seq), F32)], axis=1)
        lined = pltpu.roll(flipped, 0, 1, stride=1, stride_axis=0)
        sums[pl.ds(mine * own_heads + h, 1), :] = jnp.sum(lined, axis=0, keepdims=True)
        sums[pl.ds(other * own_heads + h, 1), :] = jnp.zeros((1, 2 * seq), F32)

    theirs = pl.ds(pl.multiple_of(other * rows, 16), rows)
    ours = pl.ds(pl.multiple_of(mine * rows, 16), rows)

    def d_normed(which):
        return jnp.concatenate(
            [matmul_t(dqkv[which, :], w_all[side]) for side in range(2)], axis=1
        )

    part_out[...] = d_normed(theirs).astype(BF16)
    part_copy = send_to(part_out, part_in, peer)
    d_n1 = d_normed(ours)
    for block in range(3 * blocks):
        grad = t_matmul(n1_ref[...], dqkv[:, block * 128 : (block + 1) * 128]).astype(BF16)
        for side in range(2):
            store(side, block * half, grad[side * half : (side + 1) * half])
    levels = iota((buckets, 2 * seq), 0)
    one_hot = (levels == bucket_ref[...]).astype(F32).astype(BF16)
    high, low = two_parts(sums[...])
    g_table = (matmul_t(one_hot, high) + matmul_t(one_hot, low)).astype(BF16)
    for side in range(2):
        part = g_table[side * (buckets // 2) : (side + 1) * (buckets // 2)]
        store(side, tile_rows + half + 16, part)
    part_copy.wait()
    d_n1 = d_n1 + part_in[...].astype(F32)
    values = tok_ref[...].astype(F32)
    factor = rms_factor(values)
    unit = values * factor
    scaled = d_n1 * gain_row(small_all, half, 0)
    gtok_ref[...] = gtok_ref[...] + factor * (
        scaled - unit * jnp.mean(scaled * unit, axis=-1, keepdims=True)
    )
    g_gain_one = jnp.sum(d_n1 * unit, axis=0, keepdims=True)
    for side in range(2):
        pieces = [
            gain[:, side * half + i * 128 : side * half + (i + 1) * 128]
            for gain in (g_gain_one, g_gain_two)
            for i in range(blocks)
        ]
        pieces.append(jnp.zeros((16 - 2 * blocks, 128), F32))
        store(side, tile_rows + half, jnp.concatenate(pieces, axis=0).astype(BF16))

    first, second = pl.ds(0, cut), pl.ds(cut, chunk_rows - cut)
    finish([send_to(comm.at[:, 1 - core], chip_in, core_peer)])

    def add_chip(i, carry):
        total = comm[i, core].astype(F32) + chip_in[i].astype(F32)
        chip[i // (xs * zs), lax.rem(i // zs, xs), lax.rem(i, zs)] = total.astype(BF16)
        return carry

    lax.fori_loop(0, ys * xs * zs, add_chip, 0)
    copies = [
        send_to(chip.at[:, at, :, first], row_in.at[i], to)
        for i, (at, to) in enumerate(zip(xp, x_peers))
    ]
    copies += [
        send_to(chip.at[at, :, :, second], column_in.at[i], to)
        for i, (at, to) in enumerate(zip(yp, y_peers))
    ]
    finish(copies)

    def add_row(i, carry):
        for k in range(zs):
            total = chip[i, x, k, first].astype(F32)
            for j in range(xs - 1):
                total = total + row_in[j, i, k].astype(F32)
            row_sum[i, k] = total.astype(BF16)
        return carry

    def add_column(i, carry):
        for k in range(zs):
            total = chip[y, i, k, second].astype(F32)
            for j in range(ys - 1):
                total = total + column_in[j, i, k].astype(F32)
            column_sum[i, k] = total.astype(BF16)
        return carry

    lax.fori_loop(0, ys, add_row, 0)
    lax.fori_loop(0, xs, add_column, 0)
    copies = [
        send_to(row_sum.at[at], row_in.at[xs - 1 + i, 0], to)
        for i, (at, to) in enumerate(zip(yp, y_peers))
    ]
    copies += [
        send_to(column_sum.at[at], column_in.at[ys - 1 + i, 0], to)
        for i, (at, to) in enumerate(zip(xp, x_peers))
    ]
    finish(copies)
    for k in range(zs):
        total = row_sum[y, k].astype(F32)
        for i in range(ys - 1):
            total = total + row_in[xs - 1 + i, 0, k].astype(F32)
        deep[k, first] = total.astype(BF16)
        total = column_sum[x, k].astype(F32)
        for i in range(xs - 1):
            total = total + column_in[ys - 1 + i, 0, k].astype(F32)
        deep[k, second] = total.astype(BF16)
    finish([send_to(deep.at[at], deep_in.at[i], to) for i, (at, to) in enumerate(zip(zp, z_peers))])
    total = deep[z].astype(F32)
    for i in range(zs - 1):
        total = total + deep_in[i].astype(F32)
    done = total.astype(BF16)
    mine_at = pl.ds(pl.multiple_of(mine * both, 16), both)
    other_at = pl.ds(pl.multiple_of(other * both, 16), both)
    deep_in[zs - 1] = done
    out = total_ref.at[y, x, z, core]
    copies = [send_to(deep_in.at[zs - 1, other_at], out.at[mine_at], peer)]
    out[mine_at] = deep_in[zs - 1, mine_at]
    out[2 * both :] = done[2 * both :]
    finish(copies)
    finish([send_to(out, out, to) for to in z_peers])
    firsts = total_ref.at[y, x, :, core, first]
    seconds = total_ref.at[y, x, :, core, second]
    copies = [send_to(firsts, firsts, to) for to in y_peers]
    copies += [send_to(seconds, seconds, to) for to in x_peers]
    finish(copies)
    firsts = total_ref.at[:, x, :, core, first]
    seconds = total_ref.at[y, :, :, core, second]
    copies = [send_to(firsts, firsts, to) for to in x_peers]
    copies += [send_to(seconds, seconds, to) for to in y_peers]
    finish(copies)
    whole = total_ref.at[:, :, :, core]
    finish([send_to(whole, whole, core_peer)])

    def load(part, start, count):
        base = part * both
        span = both if part < 2 else chunk_rows - 2 * both
        pieces, at = [], 0
        while at < count:
            chunk_at, inside = divmod(start + at, span)
            size = min(span - inside, count - at)
            spot = (
                chunk_at // (2 * zs * xs),
                (chunk_at // (2 * zs)) % xs,
                (chunk_at // 2) % zs,
                chunk_at % 2,
            )
            pieces.append(total_ref[spot + (slice(base + inside, base + inside + size),)])
            at += size
        return pieces[0] if len(pieces) == 1 else jnp.concatenate(pieces, axis=0)

    for side in range(2):
        for block in range(3 * blocks):
            at = (block // blocks) * width + side * half + (block % blocks) * 128
            gqkv_ref[:, at : at + 128] = load(side, block * half, half)
    for block in range(2 * blocks):
        gout_w_ref[:, block * 128 : (block + 1) * 128] = load(2, block * half, half)
    grouter_ref[...] = sum(load(side, tile_rows, half).astype(F32) for side in range(2))
    gsmall_ref[...] = sum(
        load(side, tile_rows + half, 16 + buckets // 2).astype(F32) for side in range(2)
    )


def back(sizes, dims, sent, dispatch, cotangent, tokens, kept, w_out, bucket_row):
    ys, xs, zs = sizes
    heads, experts, capacity, buckets = dims
    rows, width = tokens.shape
    half, seq, lanes = width // 2, 2 * rows, 128
    count = 2 * ys * xs * zs
    both = up(3 * half * half // 128 + half + 16 + buckets // 2, 16 * count) // count
    chunk_rows = 2 * both + up(half * width // 128, 16 * count) // count
    cut = up(chunk_rows // 2, 16)
    per_core = count // 2
    many = 4 * (xs + ys) + 2 * zs + 4
    shapes = [
        ((rows, width), F32),
        ((half, 3 * width), BF16),
        ((half, width), BF16),
        ((half, 128), F32),
        ((16 + buckets // 2, 128), F32),
    ]
    return pl.pallas_call(
        functools.partial(back_kernel, sizes, dims, both, cut),
        out_shape=[jax.ShapeDtypeStruct(*shape) for shape in shapes],
        in_specs=[VMEM_SPEC] * 15,
        out_specs=[VMEM_SPEC] * len(shapes),
        scratch_shapes=[
            pltpu.VMEM((2, rows, width), BF16),
            pltpu.VMEM((seq, 3 * half), BF16),
            pltpu.VMEM((128, 2 * seq), F32),
            pltpu.VMEM((rows, width), BF16),
            pltpu.VMEM((rows, width), BF16),
            pltpu.VMEM((per_core, 2, chunk_rows, lanes), BF16),
            pltpu.VMEM((ys, xs, zs, 2, chunk_rows, lanes), BF16),
            pltpu.VMEM((per_core, chunk_rows, lanes), BF16),
            pltpu.VMEM((ys, xs, zs, chunk_rows, lanes), BF16),
            pltpu.VMEM((xs + ys - 2, ys, zs, cut, lanes), BF16),
            pltpu.VMEM((xs + ys - 2, xs, zs, chunk_rows - cut, lanes), BF16),
            pltpu.VMEM((ys, zs, cut, lanes), BF16),
            pltpu.VMEM((xs, zs, chunk_rows - cut, lanes), BF16),
            pltpu.VMEM((zs, chunk_rows, lanes), BF16),
            pltpu.VMEM((zs, chunk_rows, lanes), BF16),
            pltpu.SemaphoreType.DMA((many,)),
            pltpu.SemaphoreType.DMA((many,)),
        ],
        compiler_params=pltpu.CompilerParams(
            collective_id=1, has_side_effects=True, vmem_limit_bytes=56 * 2**20
        ),
        cost_estimate=pl.CostEstimate(flops=60 * 10**9, bytes_accessed=2 * 10**8, transcendentals=0),
    )(sent, dispatch, cotangent, tokens, *kept, w_out, bucket_row)


def body(
    sizes,
    tokens,
    cotangent,
    attn_gain,
    w_qkv,
    w_out,
    rel_bias,
    buckets,
    ffn_gain,
    w_router,
    w_in,
    w_back,
    choice_ids,
):
    rows, width = tokens.shape
    half = width // 2
    bucket_half, heads = rel_bias.shape
    experts = w_router.shape[1]
    top = choice_ids.shape[1]
    capacity = up(max(2, 5 * rows * top // (4 * experts)) + 1, 8)
    slots = experts * capacity
    seq = 2 * rows
    dims = (heads, experts, capacity, 2 * bucket_half)
    blocks = half // 128

    flat_ids = choice_ids.reshape(-1)
    levels = jnp.arange(experts, dtype=jnp.int32)
    member = (flat_ids[:, None] == levels[None, :]).astype(BF16)
    order = jnp.arange(rows * top, dtype=jnp.int32)
    before = (order[:, None] > order[None, :]).astype(BF16)
    earlier = matmul(before, member)
    rank = jnp.sum(earlier * member.astype(F32), axis=1).astype(jnp.int32)
    slot = (flat_ids * capacity + rank).reshape(rows, top)
    dispatch = jnp.sum(
        (slot[:, :, None] == jnp.arange(slots, dtype=jnp.int32)).astype(BF16), axis=1
    )
    dispatch_two = jnp.broadcast_to(
        dispatch.reshape(rows, experts, 1, capacity), (rows, experts, 2, capacity)
    ).reshape(rows, 2 * slots)

    def to_experts(out_rows):
        blocks = out_rows.reshape(experts, 1, capacity, width)
        blocks = jnp.broadcast_to(blocks, (experts, 2, capacity, width))
        return swap_all(blocks.reshape(2 * slots, width))

    def swap_all(all_rows):
        blocks = all_rows.reshape(2 * experts, capacity, width)
        got = lax.all_to_all(blocks, ("rep", "shard"), split_axis=0, concat_axis=0, tiled=True)
        return got.reshape(2 * slots, width)

    grad_rows = to_experts(t_matmul(dispatch, cotangent).astype(BF16))

    gains = jnp.concatenate([attn_gain.reshape(blocks, 128), ffn_gain.reshape(blocks, 128)])
    small = jnp.concatenate(
        [
            jnp.pad(w_router, ((0, 0), (0, 128 - experts))),
            jnp.pad(gains, ((0, 16 - 2 * blocks), (0, 0))),
            jnp.pad(rel_bias, ((0, 0), (0, 128 - heads))),
        ]
    )
    nothing = jnp.full((seq,), -1, jnp.int32)
    back_order = buckets[::-1]
    bucket_front = jnp.concatenate([buckets[:1], nothing, back_order[:-1]]).reshape(1, 2 * seq)
    bucket_back = jnp.concatenate([back_order, nothing]).reshape(1, 2 * seq)
    kept = front(sizes, dims, tokens, small, w_qkv, w_out, bucket_front, dispatch)
    *kept, outgoing = kept
    hidden_one, router = kept[6], kept[8]
    arrived = to_experts(outgoing)

    expert_in, expert_back = w_in[0], w_back[0]
    grad_plain = matmul_t(grad_rows, expert_back)
    carried = arrived.reshape(2 * experts, capacity, width)[:, -1, : 2 * capacity].astype(F32)
    gate = (carried[:, :capacity] + carried[:, capacity:]).reshape(2 * slots, 1)
    pre = matmul(arrived, expert_in)
    activated, gelu_pullback = jax.vjp(jax.nn.gelu, pre)
    activated = activated.astype(BF16)
    grad_pre = gelu_pullback(gate * grad_plain)[0].astype(BF16)
    d_gate = jnp.sum(activated.astype(F32) * grad_plain, axis=1)
    parts = two_parts(d_gate)
    d_gate = jnp.concatenate([part.reshape(2 * experts, capacity) for part in parts], axis=1)
    d_gate = jnp.pad(d_gate, ((0, 0), (0, width - 2 * capacity)))
    grad_arrived = matmul_t(grad_pre, expert_in).reshape(2 * experts, capacity, width)
    last = jnp.arange(capacity)[None, :, None] == capacity - 1
    grad_arrived = jnp.where(last, d_gate[:, None, :], grad_arrived.astype(BF16))
    sent = swap_all(grad_arrived)
    returned = swap_all(matmul(activated, expert_back).astype(BF16))
    grad_result = (gate * grad_rows.astype(F32)).astype(BF16)
    grad_back_expert = t_matmul(activated, grad_result)
    grad_in_expert = t_matmul(arrived, grad_pre)

    grad_tokens, g_qkv, g_out, g_router, g_small = back(
        sizes, dims, sent, dispatch_two, cotangent, tokens, kept, w_out, bucket_back
    )

    spread = jnp.broadcast_to(router[:, :experts, None], (rows, experts, 2 * capacity))
    weights = two_parts(dispatch_two.astype(F32) * spread.reshape(rows, 2 * slots))
    hidden_two = hidden_one + matmul(weights[0], returned) + matmul(weights[1], returned)
    return (
        hidden_two.astype(BF16),
        grad_tokens,
        g_small[:blocks].reshape(half),
        g_qkv.astype(F32),
        g_out.astype(F32),
        g_small[16:, :heads],
        g_small[blocks : 2 * blocks].reshape(half),
        g_router[:, :experts],
        grad_in_expert[None],
        grad_back_expert[None],
    )


SIZES = {64: (4, 4, 2), 4: (2, 1, 1), 8: (2, 2, 1)}


def solution(mesh):
    in_specs = (
        P(("rep", "shard"), None),
        P(("rep", "shard"), None),
        P("shard"),
        P("shard", None),
        P("shard", None),
        P("shard", None),
        P(),
        P("shard"),
        P("shard", None),
        P("rep", None, "shard"),
        P("rep", "shard", None),
        P(("rep", "shard"), None),
    )
    out_specs = (
        P(("rep", "shard"), None),
        P(("rep", "shard"), None),
        P("shard"),
        P("shard", None),
        P("shard", None),
        P("shard", None),
        P("shard"),
        P("shard", None),
        P("rep", None, "shard"),
        P("rep", "shard", None),
    )
    sizes = SIZES[mesh.shape["rep"]]
    return jax.shard_map(
        functools.partial(body, sizes),
        mesh=mesh,
        in_specs=in_specs,
        out_specs=out_specs,
        check_vma=False,
    )
```

```python
import functools

import jax
import jax.numpy as jnp
from jax import lax
from jax.experimental import pallas as pl
from jax.experimental.pallas import tpu as pltpu
from jax.sharding import PartitionSpec as P

EPSILON = 1e-06
MASKED = -1e30
MESH = pl.DeviceIdType.MESH
VMEM_SPEC = pl.BlockSpec(memory_space=pltpu.VMEM)
F32 = jnp.float32
BF16 = jnp.bfloat16


def greet_all(count):
    me = 2 * lax.axis_index("rep") + lax.axis_index("shard")
    barrier = pltpu.get_barrier_semaphore()

    def signal(step, carry):
        to = lax.rem(me + step, count)
        pl.semaphore_signal(
            barrier, inc=1, device_id=(to // 2, lax.rem(to, 2)), device_id_type=MESH
        )
        return carry

    lax.fori_loop(1, count, signal, 0)
    pl.semaphore_wait(barrier, count - 1)


def send_blocks(source_of, target, count, send, recv):
    me = 2 * lax.axis_index("rep") + lax.axis_index("shard")

    def start(step, carry):
        to = lax.rem(me + step, count)
        pltpu.make_async_remote_copy(
            source_of(to),
            target.at[me],
            send,
            recv,
            (to // 2, lax.rem(to, 2)),
            device_id_type=MESH,
        ).start()
        return carry

    lax.fori_loop(1, count, start, 0)


def wait_blocks(target, count, send, recv):
    rep, mine = lax.axis_index("rep"), lax.axis_index("shard")
    most = target.at[pl.ds(0, count - 1)]
    pltpu.make_async_remote_copy(
        most, most, send, recv, (rep, 1 - mine), device_id_type=MESH
    ).wait()


def up(number, step):
    return -(-number // step) * step


def greet(peers):
    barrier = pltpu.get_barrier_semaphore()
    for peer in peers:
        pl.semaphore_signal(barrier, inc=1, device_id=peer, device_id_type=MESH)
    pl.semaphore_wait(barrier, len(peers))


def iota(shape, axis):
    return lax.broadcasted_iota(jnp.int32, shape, axis)


def dot(a, b, contract):
    return lax.dot_general(a, b, (contract, ((), ())), preferred_element_type=F32)


def matmul(a, b):
    return dot(a, b, ((1,), (0,)))


def matmul_t(a, b):
    return dot(a, b, ((1,), (1,)))


def t_matmul(a, b):
    return dot(a, b, ((0,), (0,)))


def two_parts(values):
    high = values.astype(BF16)
    return high, (values - high.astype(F32)).astype(BF16)


def rms_factor(values):
    return lax.rsqrt(jnp.mean(values * values, axis=-1, keepdims=True) + EPSILON)


def gain_row(small_ref, half, first):
    blocks = half // 128
    pieces = [
        small_ref[side, pl.ds(half + first + i, 1), :].astype(F32)
        for side in range(2)
        for i in range(blocks)
    ]
    return jnp.concatenate(pieces, axis=1)


def router_weight(small_ref, half):
    return jnp.concatenate([small_ref[0, :half, :], small_ref[1, :half, :]], axis=0)


def front_kernel(
    sizes,
    dims,
    tok_ref,
    small_ref,
    wqkv_ref,
    wout_ref,
    bucket_ref,
    dispatch_ref,
    gout_ref,
    n1_ref,
    proj_ref,
    chance_ref,
    mixed_ref,
    w_all,
    small_all,
    hidden_ref,
    n2_ref,
    router_ref,
    arrived_ref,
    grad_rows_ref,
    tok_all,
    bias_rows,
    part_out,
    part_in,
    outgoing,
    outgoing_grads,
    send,
    recv,
    local,
):
    heads, experts, capacity, buckets = dims
    ys, xs, zs = sizes
    rows, width = tok_ref.shape
    half = width // 2
    seq = 2 * rows
    own_heads = heads // 2
    head = width // heads
    slots = experts * capacity
    rep, mine = lax.axis_index("rep"), lax.axis_index("shard")
    other = 1 - mine
    core = lax.rem(rep, 2)
    peer = (rep, other)
    core_peer = (rep + 1 - 2 * core, mine)
    devices = 2 * experts
    me = 2 * rep + mine
    if zs == 2:
        z = lax.rem(rep // 2, 2)
        far_peer = (rep + 2 * (1 - 2 * z), other)
    greet_all(devices)

    def remote(i, source, target, to):
        copy = pltpu.make_async_remote_copy(
            source, target, send.at[i], recv.at[i], to, device_id_type=MESH
        )
        copy.start()
        return copy

    small_copy = remote(0, small_ref, small_all.at[mine], peer)
    near = half // 2 if zs == 1 else up(half // 12, 16)
    fetched = [(peer, 0, near)]
    if zs == 2:
        fetched.append((far_peer, near, half // 2 - near))
    weight_copies = []
    for j, (to, first, count) in enumerate(fetched):
        at = pl.ds(pl.multiple_of(core * (half // 2) + first, 16), count)
        for block in range(3):
            theirs = pl.ds(pl.multiple_of((2 * block + other) * half, 128), half)
            weight_copies.append(
                remote(
                    2 + 3 * j + block,
                    wqkv_ref.at[at, theirs],
                    w_all.at[mine, at, pl.ds(block * half, half)],
                    to,
                )
            )
    tok_copy = remote(1, tok_ref, tok_all.at[mine], peer)
    kept = [
        pltpu.make_async_copy(tok_ref, tok_all.at[mine], local.at[0]),
        pltpu.make_async_copy(small_ref, small_all.at[mine], local.at[1]),
    ]
    for block in range(3):
        ours = pl.ds(pl.multiple_of((2 * block + mine) * half, 128), half)
        kept.append(
            pltpu.make_async_copy(
                wqkv_ref.at[:, ours], w_all.at[mine, :, pl.ds(block * half, half)], local.at[2 + block]
            )
        )
    for copy in kept:
        copy.start()
    for copy in kept:
        copy.wait()
    small_copy.wait()

    table = jnp.concatenate([small_all[0, half + 16 :, :], small_all[1, half + 16 :, :]], axis=0)
    levels = iota((buckets, 2 * seq), 0)
    one_hot = (levels == bucket_ref[...]).astype(F32).astype(BF16)
    bias_rows[...] = t_matmul(table, one_hot)
    gain_one = gain_row(small_all, half, 0)
    gain_two = gain_row(small_all, half, half // 128)
    dispatch = dispatch_ref[...]
    blocks = t_matmul(dispatch, gout_ref[...]).reshape(experts, capacity, width)
    outgoing_grads[...] = blocks.astype(BF16)

    for copy in weight_copies:
        copy.wait()
    got = w_all.at[other, pl.ds(pl.multiple_of(core * (half // 2), 16), half // 2)]
    passed = remote(8, got, got, core_peer)
    send_blocks(
        lambda to: outgoing_grads.at[to // 2], grad_rows_ref, devices, send.at[10], recv.at[10]
    )
    own_block = pltpu.make_async_copy(outgoing_grads.at[rep], grad_rows_ref.at[me], local.at[0])
    own_block.start()
    tok_copy.wait()
    for side in range(2):
        values = tok_all[side].astype(F32)
        n1_ref[side * rows : (side + 1) * rows, :] = (
            values * rms_factor(values) * gain_one
        ).astype(BF16)
    passed.wait()
    normed = n1_ref[...]
    for block in range(3):
        columns = pl.ds(block * half, half)
        total = matmul(normed[:, :half], w_all[0, :, columns])
        total = total + matmul(normed[:, half:], w_all[1, :, columns])
        proj_ref[:, columns] = total.astype(BF16)

    scale = head ** (-0.5)
    causal = iota((seq, seq), 0) >= iota((seq, seq), 1)
    for h in range(own_heads):
        at = h * head
        query = proj_ref[:, at : at + head]
        key = proj_ref[:, half + at : half + at + head]
        value = proj_ref[:, 2 * half + at : 2 * half + at + head]
        row = bias_rows[pl.ds(mine * own_heads + h, 1), :]
        bias = pltpu.roll(
            jnp.broadcast_to(row, (seq, 2 * seq)), 0, 1, stride=1, stride_axis=0
        )[:, :seq]
        scores = jnp.where(causal, matmul_t(query, key) * scale + bias, MASKED)
        raised = jnp.exp(scores - jnp.max(scores, axis=-1, keepdims=True))
        chance = (raised / jnp.sum(raised, axis=-1, keepdims=True)).astype(BF16)
        chance_ref[h] = chance
        mixed_ref[:, at : at + head] = matmul(chance, value).astype(BF16)

    theirs = pl.ds(pl.multiple_of(other * rows, 16), rows)
    ours = pl.ds(pl.multiple_of(mine * rows, 16), rows)
    part_out[...] = matmul(mixed_ref[theirs, :], wout_ref[...]).astype(BF16)
    part_copy = remote(9, part_out, part_in, peer)
    hidden = tok_ref[...].astype(F32) + matmul(mixed_ref[ours, :], wout_ref[...])
    part_copy.wait()
    hidden = hidden + part_in[...].astype(F32)
    hidden_ref[...] = hidden
    normed = (hidden * rms_factor(hidden) * gain_two).astype(BF16)
    n2_ref[...] = normed
    logits = matmul(normed, router_weight(small_all, half))
    logits = jnp.where(iota((rows, 128), 1) < experts, logits, MASKED)
    raised = jnp.exp(logits - jnp.max(logits, axis=-1, keepdims=True))
    router = raised / jnp.sum(raised, axis=-1, keepdims=True)
    router_ref[...] = router

    shift = capacity.bit_length() - 1
    spread = (iota((128, slots), 0) == (iota((128, slots), 1) >> shift)).astype(F32).astype(BF16)
    row_of, slot_of = iota((slots, slots), 0), iota((slots, slots), 1)
    carrier = ((row_of & (capacity - 1)) == capacity - 1) & (
        (row_of >> shift) == (slot_of >> shift)
    )
    place = iota((slots, 128), 0) & (capacity - 1)
    gates = jnp.zeros((slots, 128), F32)
    for i, part in enumerate(two_parts(router)):
        gate = jnp.sum(matmul(part, spread) * dispatch.astype(F32), axis=0, keepdims=True)
        left = jnp.where(carrier, gate, 0.0).astype(BF16)
        right = (place == iota((slots, 128), 1) - i * capacity).astype(F32).astype(BF16)
        gates = gates + matmul(left, right)
    sent = t_matmul(dispatch, normed)
    first = (sent[:, :128] + gates).reshape(experts, capacity, 128)
    outgoing[...] = sent.reshape(experts, capacity, width).astype(BF16)
    outgoing[:, :, :128] = first.astype(BF16)
    send_blocks(lambda to: outgoing.at[to // 2], arrived_ref, devices, send.at[11], recv.at[11])
    own_block.wait()
    own_block = pltpu.make_async_copy(outgoing.at[rep], arrived_ref.at[me], local.at[0])
    own_block.start()
    own_block.wait()
    wait_blocks(grad_rows_ref, devices, send.at[10], recv.at[10])
    wait_blocks(arrived_ref, devices, send.at[11], recv.at[11])


def front(sizes, dims, tokens, small, w_qkv, w_out, bucket_row, dispatch, cotangent):
    rows, width = tokens.shape
    heads, experts, capacity, buckets = dims
    half, seq, slots = width // 2, 2 * rows, experts * capacity
    shapes = [
        ((seq, width), BF16),
        ((seq, 3 * half), BF16),
        ((heads // 2, seq, seq), BF16),
        ((seq, half), BF16),
        ((2, half, 3 * half), BF16),
        ((2,) + small.shape, BF16),
        ((rows, width), F32),
        ((rows, width), BF16),
        ((rows, 128), F32),
        ((2 * experts, capacity, width), BF16),
        ((2 * experts, capacity, width), BF16),
    ]
    return pl.pallas_call(
        functools.partial(front_kernel, sizes, dims),
        out_shape=[jax.ShapeDtypeStruct(*shape) for shape in shapes],
        in_specs=[VMEM_SPEC] * 7,
        out_specs=[VMEM_SPEC] * len(shapes),
        scratch_shapes=[
            pltpu.VMEM((2, rows, width), BF16),
            pltpu.VMEM((128, 2 * seq), F32),
            pltpu.VMEM((rows, width), BF16),
            pltpu.VMEM((rows, width), BF16),
            pltpu.VMEM((experts, capacity, width), BF16),
            pltpu.VMEM((experts, capacity, width), BF16),
            pltpu.SemaphoreType.DMA((12,)),
            pltpu.SemaphoreType.DMA((12,)),
            pltpu.SemaphoreType.DMA((5,)),
        ],
        compiler_params=pltpu.CompilerParams(
            collective_id=0, has_side_effects=True, vmem_limit_bytes=48 * 2**20
        ),
        cost_estimate=pl.CostEstimate(flops=30 * 10**9, bytes_accessed=10**8, transcendentals=10**6),
    )(tokens, small, w_qkv, w_out, bucket_row, dispatch, cotangent)


def back_kernel(
    sizes,
    dims,
    both,
    cut,
    sent_ref,
    dispatch_ref,
    gout_ref,
    tok_ref,
    n1_ref,
    proj_ref,
    chance_ref,
    mixed_ref,
    w_all,
    small_all,
    hidden_ref,
    n2_ref,
    router_ref,
    wout_ref,
    bucket_ref,
    gtok_ref,
    gqkv_ref,
    gout_w_ref,
    grouter_ref,
    gsmall_ref,
    att_all,
    dqkv,
    sums,
    part_out,
    part_in,
    comm,
    total_ref,
    chip_in,
    chip,
    row_in,
    column_in,
    row_sum,
    column_sum,
    deep,
    deep_in,
    send,
    recv,
):
    heads, experts, capacity, buckets = dims
    ys, xs, zs = sizes
    rows, width = tok_ref.shape
    half = width // 2
    seq = 2 * rows
    own_heads = heads // 2
    head = width // heads
    blocks = half // 128
    chunk_rows = comm.shape[2]
    rep, mine = lax.axis_index("rep"), lax.axis_index("shard")
    other = 1 - mine
    core = lax.rem(rep, 2)
    z = lax.rem(rep // 2, zs)
    x = lax.rem(rep // (2 * zs), xs)
    y = rep // (2 * zs * xs)

    def place(y_at, x_at, z_at, core_at):
        return ((y_at * xs + x_at) * zs + z_at) * 2 + core_at

    xp = [lax.rem(x + step, xs) for step in range(1, xs)]
    yp = [lax.rem(y + step, ys) for step in range(1, ys)]
    zp = [lax.rem(z + step, zs) for step in range(1, zs)]
    core_peer = (place(y, x, z, 1 - core), mine)
    x_peers = [(place(y, at, z, core), mine) for at in xp]
    y_peers = [(place(at, x, z, core), mine) for at in yp]
    z_peers = [(place(y, x, at, core), mine) for at in zp]
    peer = (rep, other)
    greet([core_peer, peer] + x_peers + y_peers + z_peers)
    number = [0]

    def send_to(source, target, to):
        i = number[0]
        number[0] += 1
        copy = pltpu.make_async_remote_copy(
            source, target, send.at[i], recv.at[i], to, device_id_type=MESH
        )
        copy.start()
        return copy

    def finish(copies):
        for copy in copies:
            copy.wait()

    shift = capacity.bit_length() - 1
    wide = 2 * experts * capacity
    row_of, slot_of = iota((wide, wide), 1), iota((wide, wide), 0)
    carrier = (row_of == ((slot_of >> shift) << shift) + capacity - 1).astype(F32).astype(BF16)
    carried = matmul(carrier, sent_ref[:, :128])
    lane = iota((wide, 128), 1)
    slot = iota((wide, 128), 0)
    mask = ((lane & (capacity - 1)) == (slot & (capacity - 1))) & (lane < 2 * capacity)
    d_gate = jnp.sum(jnp.where(mask, carried, 0.0), axis=1, keepdims=True)
    d_gate = jnp.where((slot >> (shift + 1)) == lane, d_gate, 0.0)
    dispatch = dispatch_ref[...]
    high, low = two_parts(d_gate)
    d_router = matmul(dispatch, high) + matmul(dispatch, low)
    router = router_ref[...]
    d_logits = router * (d_router - jnp.sum(router * d_router, axis=-1, keepdims=True))
    d_logits = d_logits.astype(BF16)
    d_n2 = matmul(dispatch, sent_ref[...]) + matmul_t(d_logits, router_weight(small_all, half))
    hidden = hidden_ref[...]
    factor = rms_factor(hidden)
    unit = hidden * factor
    scaled = d_n2 * gain_row(small_all, half, blocks)
    d_hidden = gout_ref[...].astype(F32) + factor * (
        scaled - unit * jnp.mean(scaled * unit, axis=-1, keepdims=True)
    )
    att_all[mine] = d_hidden.astype(BF16)
    shared = send_to(att_all.at[mine], att_all.at[mine], peer)
    gtok_ref[...] = d_hidden
    g_gain_two = jnp.sum(d_n2 * unit, axis=0, keepdims=True)
    g_router = t_matmul(n2_ref[...], d_logits)

    def store(part, first, block):
        base = part * both
        span = both if part < 2 else chunk_rows - 2 * both
        at = 0
        while at < block.shape[0]:
            chunk_at, inside = divmod(first + at, span)
            count = min(span - inside, block.shape[0] - at)
            comm[chunk_at // 2, chunk_at % 2, base + inside : base + inside + count, :] = block[
                at : at + count
            ]
            at += count

    tile_rows = 3 * blocks * half
    for side in range(2):
        store(side, tile_rows, g_router[side * half : (side + 1) * half].astype(BF16))
    shared.wait()

    d_att = [att_all[0], att_all[1]]
    for block in range(2 * blocks):
        columns = slice(block * 128, (block + 1) * 128)
        grad = t_matmul(mixed_ref[:rows, :], d_att[0][:, columns])
        grad = grad + t_matmul(mixed_ref[rows:, :], d_att[1][:, columns])
        store(2, block * half, grad.astype(BF16))
    d_mixed = jnp.concatenate(
        [matmul_t(part, wout_ref[...]).astype(BF16) for part in d_att], axis=0
    )
    scale = head ** (-0.5)
    flip = (iota((seq, seq), 0) + iota((seq, seq), 1) == seq - 1).astype(F32).astype(BF16)
    for h in range(own_heads):
        at = h * head
        query = proj_ref[:, at : at + head]
        key = proj_ref[:, half + at : half + at + head]
        value = proj_ref[:, 2 * half + at : 2 * half + at + head]
        d_o = d_mixed[:, at : at + head]
        chance = chance_ref[h]
        d_chance = matmul_t(d_o, value)
        wide_chance = chance.astype(F32)
        inner = jnp.sum(wide_chance * d_chance, axis=-1, keepdims=True)
        d_scores = (wide_chance * (d_chance - inner)).astype(BF16)
        dqkv[:, at : at + head] = (matmul(d_scores, key) * scale).astype(BF16)
        dqkv[:, half + at : half + at + head] = (t_matmul(d_scores, query) * scale).astype(BF16)
        dqkv[:, 2 * half + at : 2 * half + at + head] = t_matmul(chance, d_o).astype(BF16)
        flipped = matmul(flip, d_scores)
        flipped = jnp.concatenate([flipped, jnp.zeros((seq, seq), F32)], axis=1)
        lined = pltpu.roll(flipped, 0, 1, stride=1, stride_axis=0)
        sums[pl.ds(mine * own_heads + h, 1), :] = jnp.sum(lined, axis=0, keepdims=True)
        sums[pl.ds(other * own_heads + h, 1), :] = jnp.zeros((1, 2 * seq), F32)

    theirs = pl.ds(pl.multiple_of(other * rows, 16), rows)
    ours = pl.ds(pl.multiple_of(mine * rows, 16), rows)

    def d_normed(which):
        return jnp.concatenate(
            [matmul_t(dqkv[which, :], w_all[side]) for side in range(2)], axis=1
        )

    part_out[...] = d_normed(theirs).astype(BF16)
    part_copy = send_to(part_out, part_in, peer)
    d_n1 = d_normed(ours)
    for block in range(3 * blocks):
        grad = t_matmul(n1_ref[...], dqkv[:, block * 128 : (block + 1) * 128]).astype(BF16)
        for side in range(2):
            store(side, block * half, grad[side * half : (side + 1) * half])
    levels = iota((buckets, 2 * seq), 0)
    one_hot = (levels == bucket_ref[...]).astype(F32).astype(BF16)
    high, low = two_parts(sums[...])
    g_table = (matmul_t(one_hot, high) + matmul_t(one_hot, low)).astype(BF16)
    for side in range(2):
        part = g_table[side * (buckets // 2) : (side + 1) * (buckets // 2)]
        store(side, tile_rows + half + 16, part)
    part_copy.wait()
    d_n1 = d_n1 + part_in[...].astype(F32)
    values = tok_ref[...].astype(F32)
    factor = rms_factor(values)
    unit = values * factor
    scaled = d_n1 * gain_row(small_all, half, 0)
    gtok_ref[...] = gtok_ref[...] + factor * (
        scaled - unit * jnp.mean(scaled * unit, axis=-1, keepdims=True)
    )
    g_gain_one = jnp.sum(d_n1 * unit, axis=0, keepdims=True)
    for side in range(2):
        pieces = [
            gain[:, side * half + i * 128 : side * half + (i + 1) * 128]
            for gain in (g_gain_one, g_gain_two)
            for i in range(blocks)
        ]
        pieces.append(jnp.zeros((16 - 2 * blocks, 128), F32))
        store(side, tile_rows + half, jnp.concatenate(pieces, axis=0).astype(BF16))

    first, second = pl.ds(0, cut), pl.ds(cut, chunk_rows - cut)
    finish([send_to(comm.at[:, 1 - core], chip_in, core_peer)])

    def add_chip(i, carry):
        total = comm[i, core].astype(F32) + chip_in[i].astype(F32)
        chip[i // (xs * zs), lax.rem(i // zs, xs), lax.rem(i, zs)] = total.astype(BF16)
        return carry

    lax.fori_loop(0, ys * xs * zs, add_chip, 0)
    copies = [
        send_to(chip.at[:, at, :, first], row_in.at[i], to)
        for i, (at, to) in enumerate(zip(xp, x_peers))
    ]
    copies += [
        send_to(chip.at[at, :, :, second], column_in.at[i], to)
        for i, (at, to) in enumerate(zip(yp, y_peers))
    ]
    finish(copies)

    def add_row(i, carry):
        for k in range(zs):
            total = chip[i, x, k, first].astype(F32)
            for j in range(xs - 1):
                total = total + row_in[j, i, k].astype(F32)
            row_sum[i, k] = total.astype(BF16)
        return carry

    def add_column(i, carry):
        for k in range(zs):
            total = chip[y, i, k, second].astype(F32)
            for j in range(ys - 1):
                total = total + column_in[j, i, k].astype(F32)
            column_sum[i, k] = total.astype(BF16)
        return carry

    lax.fori_loop(0, ys, add_row, 0)
    lax.fori_loop(0, xs, add_column, 0)
    copies = [
        send_to(row_sum.at[at], row_in.at[xs - 1 + i, 0], to)
        for i, (at, to) in enumerate(zip(yp, y_peers))
    ]
    copies += [
        send_to(column_sum.at[at], column_in.at[ys - 1 + i, 0], to)
        for i, (at, to) in enumerate(zip(xp, x_peers))
    ]
    finish(copies)
    for k in range(zs):
        total = row_sum[y, k].astype(F32)
        for i in range(ys - 1):
            total = total + row_in[xs - 1 + i, 0, k].astype(F32)
        deep[k, first] = total.astype(BF16)
        total = column_sum[x, k].astype(F32)
        for i in range(xs - 1):
            total = total + column_in[ys - 1 + i, 0, k].astype(F32)
        deep[k, second] = total.astype(BF16)
    finish([send_to(deep.at[at], deep_in.at[i], to) for i, (at, to) in enumerate(zip(zp, z_peers))])
    total = deep[z].astype(F32)
    for i in range(zs - 1):
        total = total + deep_in[i].astype(F32)
    done = total.astype(BF16)
    mine_at = pl.ds(pl.multiple_of(mine * both, 16), both)
    other_at = pl.ds(pl.multiple_of(other * both, 16), both)
    deep_in[zs - 1] = done
    out = total_ref.at[y, x, z, core]
    copies = [send_to(deep_in.at[zs - 1, other_at], out.at[mine_at], peer)]
    out[mine_at] = deep_in[zs - 1, mine_at]
    out[2 * both :] = done[2 * both :]
    finish(copies)
    finish([send_to(out, out, to) for to in z_peers])
    firsts = total_ref.at[y, x, :, core, first]
    seconds = total_ref.at[y, x, :, core, second]
    copies = [send_to(firsts, firsts, to) for to in y_peers]
    copies += [send_to(seconds, seconds, to) for to in x_peers]
    finish(copies)
    firsts = total_ref.at[:, x, :, core, first]
    seconds = total_ref.at[y, :, :, core, second]
    copies = [send_to(firsts, firsts, to) for to in x_peers]
    copies += [send_to(seconds, seconds, to) for to in y_peers]
    finish(copies)
    whole = total_ref.at[:, :, :, core]
    finish([send_to(whole, whole, core_peer)])

    def load(part, start, count):
        base = part * both
        span = both if part < 2 else chunk_rows - 2 * both
        pieces, at = [], 0
        while at < count:
            chunk_at, inside = divmod(start + at, span)
            size = min(span - inside, count - at)
            spot = (
                chunk_at // (2 * zs * xs),
                (chunk_at // (2 * zs)) % xs,
                (chunk_at // 2) % zs,
                chunk_at % 2,
            )
            pieces.append(total_ref[spot + (slice(base + inside, base + inside + size),)])
            at += size
        return pieces[0] if len(pieces) == 1 else jnp.concatenate(pieces, axis=0)

    for side in range(2):
        for block in range(3 * blocks):
            at = (block // blocks) * width + side * half + (block % blocks) * 128
            gqkv_ref[:, at : at + 128] = load(side, block * half, half)
    for block in range(2 * blocks):
        gout_w_ref[:, block * 128 : (block + 1) * 128] = load(2, block * half, half)
    grouter_ref[...] = sum(load(side, tile_rows, half).astype(F32) for side in range(2))
    gsmall_ref[...] = sum(
        load(side, tile_rows + half, 16 + buckets // 2).astype(F32) for side in range(2)
    )


def back(sizes, dims, sent, dispatch, cotangent, tokens, kept, w_out, bucket_row):
    ys, xs, zs = sizes
    heads, experts, capacity, buckets = dims
    rows, width = tokens.shape
    half, seq, lanes = width // 2, 2 * rows, 128
    count = 2 * ys * xs * zs
    both = up(3 * half * half // 128 + half + 16 + buckets // 2, 16 * count) // count
    chunk_rows = 2 * both + up(half * width // 128, 16 * count) // count
    cut = up(chunk_rows // 2, 16)
    per_core = count // 2
    many = 4 * (xs + ys) + 2 * zs + 4
    shapes = [
        ((rows, width), F32),
        ((half, 3 * width), BF16),
        ((half, width), BF16),
        ((half, 128), F32),
        ((16 + buckets // 2, 128), F32),
    ]
    return pl.pallas_call(
        functools.partial(back_kernel, sizes, dims, both, cut),
        out_shape=[jax.ShapeDtypeStruct(*shape) for shape in shapes],
        in_specs=[VMEM_SPEC] * 15,
        out_specs=[VMEM_SPEC] * len(shapes),
        scratch_shapes=[
            pltpu.VMEM((2, rows, width), BF16),
            pltpu.VMEM((seq, 3 * half), BF16),
            pltpu.VMEM((128, 2 * seq), F32),
            pltpu.VMEM((rows, width), BF16),
            pltpu.VMEM((rows, width), BF16),
            pltpu.VMEM((per_core, 2, chunk_rows, lanes), BF16),
            pltpu.VMEM((ys, xs, zs, 2, chunk_rows, lanes), BF16),
            pltpu.VMEM((per_core, chunk_rows, lanes), BF16),
            pltpu.VMEM((ys, xs, zs, chunk_rows, lanes), BF16),
            pltpu.VMEM((xs + ys - 2, ys, zs, cut, lanes), BF16),
            pltpu.VMEM((xs + ys - 2, xs, zs, chunk_rows - cut, lanes), BF16),
            pltpu.VMEM((ys, zs, cut, lanes), BF16),
            pltpu.VMEM((xs, zs, chunk_rows - cut, lanes), BF16),
            pltpu.VMEM((zs, chunk_rows, lanes), BF16),
            pltpu.VMEM((zs, chunk_rows, lanes), BF16),
            pltpu.SemaphoreType.DMA((many,)),
            pltpu.SemaphoreType.DMA((many,)),
        ],
        compiler_params=pltpu.CompilerParams(
            collective_id=1, has_side_effects=True, vmem_limit_bytes=56 * 2**20
        ),
        cost_estimate=pl.CostEstimate(flops=60 * 10**9, bytes_accessed=2 * 10**8, transcendentals=0),
    )(sent, dispatch, cotangent, tokens, *kept, w_out, bucket_row)


def body(
    sizes,
    tokens,
    cotangent,
    attn_gain,
    w_qkv,
    w_out,
    rel_bias,
    buckets,
    ffn_gain,
    w_router,
    w_in,
    w_back,
    choice_ids,
):
    rows, width = tokens.shape
    half = width // 2
    bucket_half, heads = rel_bias.shape
    experts = w_router.shape[1]
    top = choice_ids.shape[1]
    capacity = up(max(2, 5 * rows * top // (4 * experts)) + 1, 8)
    slots = experts * capacity
    seq = 2 * rows
    dims = (heads, experts, capacity, 2 * bucket_half)
    blocks = half // 128

    flat_ids = choice_ids.reshape(-1)
    levels = jnp.arange(experts, dtype=jnp.int32)
    member = (flat_ids[:, None] == levels[None, :]).astype(BF16)
    order = jnp.arange(rows * top, dtype=jnp.int32)
    before = (order[:, None] > order[None, :]).astype(BF16)
    earlier = matmul(before, member)
    rank = jnp.sum(earlier * member.astype(F32), axis=1).astype(jnp.int32)
    slot = (flat_ids * capacity + rank).reshape(rows, top)
    dispatch = jnp.sum(
        (slot[:, :, None] == jnp.arange(slots, dtype=jnp.int32)).astype(BF16), axis=1
    )
    dispatch_two = jnp.broadcast_to(
        dispatch.reshape(rows, experts, 1, capacity), (rows, experts, 2, capacity)
    ).reshape(rows, 2 * slots)

    def swap_all(all_rows):
        blocks = all_rows.reshape(2 * experts, capacity, width)
        got = lax.all_to_all(blocks, ("rep", "shard"), split_axis=0, concat_axis=0, tiled=True)
        return got.reshape(2 * slots, width)

    gains = jnp.concatenate([attn_gain.reshape(blocks, 128), ffn_gain.reshape(blocks, 128)])
    small = jnp.concatenate(
        [
            jnp.pad(w_router, ((0, 0), (0, 128 - experts))),
            jnp.pad(gains, ((0, 16 - 2 * blocks), (0, 0))),
            jnp.pad(rel_bias, ((0, 0), (0, 128 - heads))),
        ]
    )
    nothing = jnp.full((seq,), -1, jnp.int32)
    back_order = buckets[::-1]
    bucket_front = jnp.concatenate([buckets[:1], nothing, back_order[:-1]]).reshape(1, 2 * seq)
    bucket_back = jnp.concatenate([back_order, nothing]).reshape(1, 2 * seq)
    *kept, arrived, grad_rows = front(
        sizes, dims, tokens, small, w_qkv, w_out, bucket_front, dispatch, cotangent
    )
    hidden_one, router = kept[6], kept[8]
    arrived, grad_rows = (block.reshape(2 * slots, width) for block in (arrived, grad_rows))

    expert_in, expert_back = w_in[0], w_back[0]
    grad_plain = matmul_t(grad_rows, expert_back)
    carried = arrived.reshape(2 * experts, capacity, width)[:, -1, : 2 * capacity].astype(F32)
    gate = (carried[:, :capacity] + carried[:, capacity:]).reshape(2 * slots, 1)
    pre = matmul(arrived, expert_in)
    activated, gelu_pullback = jax.vjp(jax.nn.gelu, pre)
    activated = activated.astype(BF16)
    grad_pre = gelu_pullback(gate * grad_plain)[0].astype(BF16)
    d_gate = jnp.sum(activated.astype(F32) * grad_plain, axis=1)
    parts = two_parts(d_gate)
    d_gate = jnp.concatenate([part.reshape(2 * experts, capacity) for part in parts], axis=1)
    d_gate = jnp.pad(d_gate, ((0, 0), (0, width - 2 * capacity)))
    grad_arrived = matmul_t(grad_pre, expert_in).reshape(2 * experts, capacity, width)
    last = jnp.arange(capacity)[None, :, None] == capacity - 1
    grad_arrived = jnp.where(last, d_gate[:, None, :], grad_arrived.astype(BF16))
    sent = swap_all(grad_arrived)
    returned = swap_all(matmul(activated, expert_back).astype(BF16))
    grad_result = (gate * grad_rows.astype(F32)).astype(BF16)
    grad_back_expert = t_matmul(activated, grad_result)
    grad_in_expert = t_matmul(arrived, grad_pre)

    grad_tokens, g_qkv, g_out, g_router, g_small = back(
        sizes, dims, sent, dispatch_two, cotangent, tokens, kept, w_out, bucket_back
    )

    spread = jnp.broadcast_to(router[:, :experts, None], (rows, experts, 2 * capacity))
    weights = two_parts(dispatch_two.astype(F32) * spread.reshape(rows, 2 * slots))
    hidden_two = hidden_one + matmul(weights[0], returned) + matmul(weights[1], returned)
    return (
        hidden_two.astype(BF16),
        grad_tokens,
        g_small[:blocks].reshape(half),
        g_qkv.astype(F32),
        g_out.astype(F32),
        g_small[16:, :heads],
        g_small[blocks : 2 * blocks].reshape(half),
        g_router[:, :experts],
        grad_in_expert[None],
        grad_back_expert[None],
    )


SIZES = {64: (4, 4, 2), 4: (2, 1, 1), 8: (2, 2, 1)}


def solution(mesh):
    in_specs = (
        P(("rep", "shard"), None),
        P(("rep", "shard"), None),
        P("shard"),
        P("shard", None),
        P("shard", None),
        P("shard", None),
        P(),
        P("shard"),
        P("shard", None),
        P("rep", None, "shard"),
        P("rep", "shard", None),
        P(("rep", "shard"), None),
    )
    out_specs = (
        P(("rep", "shard"), None),
        P(("rep", "shard"), None),
        P("shard"),
        P("shard", None),
        P("shard", None),
        P("shard", None),
        P("shard"),
        P("shard", None),
        P("rep", None, "shard"),
        P("rep", "shard", None),
    )
    sizes = SIZES[mesh.shape["rep"]]
    return jax.shard_map(
        functools.partial(body, sizes),
        mesh=mesh,
        in_specs=in_specs,
        out_specs=out_specs,
        check_vma=False,
    )
```

```python
import functools

import jax
import jax.numpy as jnp
from jax import lax
from jax.experimental import pallas as pl
from jax.experimental.pallas import tpu as pltpu
from jax.sharding import PartitionSpec as P

EPSILON = 1e-06
MASKED = -1e30
MESH = pl.DeviceIdType.MESH
VMEM_SPEC = pl.BlockSpec(memory_space=pltpu.VMEM)
F32 = jnp.float32
BF16 = jnp.bfloat16


def greet_all(count):
    me = 2 * lax.axis_index("rep") + lax.axis_index("shard")
    barrier = pltpu.get_barrier_semaphore()

    def signal(step, carry):
        to = lax.rem(me + step, count)
        pl.semaphore_signal(
            barrier, inc=1, device_id=(to // 2, lax.rem(to, 2)), device_id_type=MESH
        )
        return carry

    lax.fori_loop(1, count, signal, 0)
    pl.semaphore_wait(barrier, count - 1)


def send_blocks(source_of, target, count, send, recv):
    me = 2 * lax.axis_index("rep") + lax.axis_index("shard")

    def start(step, carry):
        to = lax.rem(me + step, count)
        pltpu.make_async_remote_copy(
            source_of(to),
            target.at[me],
            send,
            recv,
            (to // 2, lax.rem(to, 2)),
            device_id_type=MESH,
        ).start()
        return carry

    lax.fori_loop(1, count, start, 0)


def wait_blocks(target, count, send, recv):
    rep, mine = lax.axis_index("rep"), lax.axis_index("shard")
    most = target.at[pl.ds(0, count - 1)]
    pltpu.make_async_remote_copy(
        most, most, send, recv, (rep, 1 - mine), device_id_type=MESH
    ).wait()


def up(number, step):
    return -(-number // step) * step


def greet(peers):
    barrier = pltpu.get_barrier_semaphore()
    for peer in peers:
        pl.semaphore_signal(barrier, inc=1, device_id=peer, device_id_type=MESH)
    pl.semaphore_wait(barrier, len(peers))


def iota(shape, axis):
    return lax.broadcasted_iota(jnp.int32, shape, axis)


def dot(a, b, contract):
    return lax.dot_general(a, b, (contract, ((), ())), preferred_element_type=F32)


def matmul(a, b):
    return dot(a, b, ((1,), (0,)))


def matmul_t(a, b):
    return dot(a, b, ((1,), (1,)))


def t_matmul(a, b):
    return dot(a, b, ((0,), (0,)))


def two_parts(values):
    high = values.astype(BF16)
    return high, (values - high.astype(F32)).astype(BF16)


def rms_factor(values):
    return lax.rsqrt(jnp.mean(values * values, axis=-1, keepdims=True) + EPSILON)


def gain_row(small_ref, half, first):
    blocks = half // 128
    pieces = [
        small_ref[side, pl.ds(half + first + i, 1), :].astype(F32)
        for side in range(2)
        for i in range(blocks)
    ]
    return jnp.concatenate(pieces, axis=1)


def router_weight(small_ref, half):
    return jnp.concatenate([small_ref[0, :half, :], small_ref[1, :half, :]], axis=0)


def lifted(block, capacity):
    count = block.shape[0]
    shift = capacity.bit_length() - 1
    source, slot = iota((count, count), 1), iota((count, count), 0)
    carrier = (source == ((slot >> shift) << shift) + capacity - 1).astype(F32).astype(BF16)
    carried = matmul(carrier, block)
    lane, slot = iota((count, 128), 1), iota((count, 128), 0)
    mask = ((lane & (capacity - 1)) == (slot & (capacity - 1))) & (lane < 2 * capacity)
    return jnp.sum(jnp.where(mask, carried, 0.0), axis=1, keepdims=True)


def lowered(column, capacity):
    count = column.shape[0]
    shift = capacity.bit_length() - 1
    target, slot = iota((count, count), 0), iota((count, count), 1)
    carrier = (target == ((slot >> shift) << shift) + capacity - 1).astype(F32).astype(BF16)
    lane, slot = iota((count, 128), 1), iota((count, 128), 0) & (capacity - 1)
    high, low = two_parts(column)
    spread = jnp.where(lane == slot, high.astype(F32), 0.0)
    spread = spread + jnp.where(lane == slot + capacity, low.astype(F32), 0.0)
    return matmul(carrier, spread.astype(BF16))


def front_kernel(
    sizes,
    dims,
    tok_ref,
    small_ref,
    wqkv_ref,
    wout_ref,
    bucket_ref,
    dispatch_ref,
    gout_ref,
    n1_ref,
    proj_ref,
    chance_ref,
    mixed_ref,
    w_all,
    small_all,
    hidden_ref,
    n2_ref,
    router_ref,
    arrived_ref,
    grad_rows_ref,
    tok_all,
    bias_rows,
    part_out,
    part_in,
    outgoing,
    outgoing_grads,
    send,
    recv,
    local,
):
    heads, experts, capacity, buckets = dims
    ys, xs, zs = sizes
    rows, width = tok_ref.shape
    half = width // 2
    seq = 2 * rows
    own_heads = heads // 2
    head = width // heads
    slots = experts * capacity
    rep, mine = lax.axis_index("rep"), lax.axis_index("shard")
    other = 1 - mine
    core = lax.rem(rep, 2)
    peer = (rep, other)
    core_peer = (rep + 1 - 2 * core, mine)
    devices = 2 * experts
    me = 2 * rep + mine
    if zs == 2:
        z = lax.rem(rep // 2, 2)
        far_peer = (rep + 2 * (1 - 2 * z), other)
    greet_all(devices)

    def remote(i, source, target, to):
        copy = pltpu.make_async_remote_copy(
            source, target, send.at[i], recv.at[i], to, device_id_type=MESH
        )
        copy.start()
        return copy

    small_copy = remote(0, small_ref, small_all.at[mine], peer)
    near = half // 2 if zs == 1 else up(half // 12, 16)
    fetched = [(peer, 0, near)]
    if zs == 2:
        fetched.append((far_peer, near, half // 2 - near))
    weight_copies = []
    for j, (to, first, count) in enumerate(fetched):
        at = pl.ds(pl.multiple_of(core * (half // 2) + first, 16), count)
        for block in range(3):
            theirs = pl.ds(pl.multiple_of((2 * block + other) * half, 128), half)
            weight_copies.append(
                remote(
                    2 + 3 * j + block,
                    wqkv_ref.at[at, theirs],
                    w_all.at[mine, at, pl.ds(block * half, half)],
                    to,
                )
            )
    tok_copy = remote(1, tok_ref, tok_all.at[mine], peer)
    kept = [
        pltpu.make_async_copy(tok_ref, tok_all.at[mine], local.at[0]),
        pltpu.make_async_copy(small_ref, small_all.at[mine], local.at[1]),
    ]
    for block in range(3):
        ours = pl.ds(pl.multiple_of((2 * block + mine) * half, 128), half)
        kept.append(
            pltpu.make_async_copy(
                wqkv_ref.at[:, ours], w_all.at[mine, :, pl.ds(block * half, half)], local.at[2 + block]
            )
        )
    for copy in kept:
        copy.start()
    for copy in kept:
        copy.wait()
    small_copy.wait()

    table = jnp.concatenate([small_all[0, half + 16 :, :], small_all[1, half + 16 :, :]], axis=0)
    levels = iota((buckets, 2 * seq), 0)
    one_hot = (levels == bucket_ref[...]).astype(F32).astype(BF16)
    bias_rows[...] = t_matmul(table, one_hot)
    gain_one = gain_row(small_all, half, 0)
    gain_two = gain_row(small_all, half, half // 128)
    dispatch = dispatch_ref[...]
    blocks = t_matmul(dispatch, gout_ref[...]).reshape(experts, capacity, width)
    outgoing_grads[...] = blocks.astype(BF16)

    for copy in weight_copies:
        copy.wait()
    got = w_all.at[other, pl.ds(pl.multiple_of(core * (half // 2), 16), half // 2)]
    passed = remote(8, got, got, core_peer)
    send_blocks(
        lambda to: outgoing_grads.at[to // 2], grad_rows_ref, devices, send.at[10], recv.at[10]
    )
    own_block = pltpu.make_async_copy(outgoing_grads.at[rep], grad_rows_ref.at[me], local.at[0])
    own_block.start()
    tok_copy.wait()
    for side in range(2):
        values = tok_all[side].astype(F32)
        n1_ref[side * rows : (side + 1) * rows, :] = (
            values * rms_factor(values) * gain_one
        ).astype(BF16)
    passed.wait()
    normed = n1_ref[...]
    for block in range(3):
        columns = pl.ds(block * half, half)
        total = matmul(normed[:, :half], w_all[0, :, columns])
        total = total + matmul(normed[:, half:], w_all[1, :, columns])
        proj_ref[:, columns] = total.astype(BF16)

    scale = head ** (-0.5)
    causal = iota((seq, seq), 0) >= iota((seq, seq), 1)
    for h in range(own_heads):
        at = h * head
        query = proj_ref[:, at : at + head]
        key = proj_ref[:, half + at : half + at + head]
        value = proj_ref[:, 2 * half + at : 2 * half + at + head]
        row = bias_rows[pl.ds(mine * own_heads + h, 1), :]
        bias = pltpu.roll(
            jnp.broadcast_to(row, (seq, 2 * seq)), 0, 1, stride=1, stride_axis=0
        )[:, :seq]
        scores = jnp.where(causal, matmul_t(query, key) * scale + bias, MASKED)
        raised = jnp.exp(scores - jnp.max(scores, axis=-1, keepdims=True))
        chance = (raised / jnp.sum(raised, axis=-1, keepdims=True)).astype(BF16)
        chance_ref[h] = chance
        mixed_ref[:, at : at + head] = matmul(chance, value).astype(BF16)

    theirs = pl.ds(pl.multiple_of(other * rows, 16), rows)
    ours = pl.ds(pl.multiple_of(mine * rows, 16), rows)
    part_out[...] = matmul(mixed_ref[theirs, :], wout_ref[...]).astype(BF16)
    part_copy = remote(9, part_out, part_in, peer)
    hidden = tok_ref[...].astype(F32) + matmul(mixed_ref[ours, :], wout_ref[...])
    part_copy.wait()
    hidden = hidden + part_in[...].astype(F32)
    hidden_ref[...] = hidden
    normed = (hidden * rms_factor(hidden) * gain_two).astype(BF16)
    n2_ref[...] = normed
    logits = matmul(normed, router_weight(small_all, half))
    logits = jnp.where(iota((rows, 128), 1) < experts, logits, MASKED)
    raised = jnp.exp(logits - jnp.max(logits, axis=-1, keepdims=True))
    router = raised / jnp.sum(raised, axis=-1, keepdims=True)
    router_ref[...] = router

    shift = capacity.bit_length() - 1
    spread = (iota((128, slots), 0) == (iota((128, slots), 1) >> shift)).astype(F32).astype(BF16)
    row_of, slot_of = iota((slots, slots), 0), iota((slots, slots), 1)
    carrier = ((row_of & (capacity - 1)) == capacity - 1) & (
        (row_of >> shift) == (slot_of >> shift)
    )
    place = iota((slots, 128), 0) & (capacity - 1)
    gates = jnp.zeros((slots, 128), F32)
    for i, part in enumerate(two_parts(router)):
        gate = jnp.sum(matmul(part, spread) * dispatch.astype(F32), axis=0, keepdims=True)
        left = jnp.where(carrier, gate, 0.0).astype(BF16)
        right = (place == iota((slots, 128), 1) - i * capacity).astype(F32).astype(BF16)
        gates = gates + matmul(left, right)
    sent = t_matmul(dispatch, normed)
    first = (sent[:, :128] + gates).reshape(experts, capacity, 128)
    outgoing[...] = sent.reshape(experts, capacity, width).astype(BF16)
    outgoing[:, :, :128] = first.astype(BF16)
    send_blocks(lambda to: outgoing.at[to // 2], arrived_ref, devices, send.at[11], recv.at[11])
    own_block.wait()
    own_block = pltpu.make_async_copy(outgoing.at[rep], arrived_ref.at[me], local.at[0])
    own_block.start()
    own_block.wait()
    wait_blocks(grad_rows_ref, devices, send.at[10], recv.at[10])
    wait_blocks(arrived_ref, devices, send.at[11], recv.at[11])


def front(sizes, dims, tokens, small, w_qkv, w_out, bucket_row, dispatch, cotangent):
    rows, width = tokens.shape
    heads, experts, capacity, buckets = dims
    half, seq, slots = width // 2, 2 * rows, experts * capacity
    shapes = [
        ((seq, width), BF16),
        ((seq, 3 * half), BF16),
        ((heads // 2, seq, seq), BF16),
        ((seq, half), BF16),
        ((2, half, 3 * half), BF16),
        ((2,) + small.shape, BF16),
        ((rows, width), F32),
        ((rows, width), BF16),
        ((rows, 128), F32),
        ((2 * experts, capacity, width), BF16),
        ((2 * experts, capacity, width), BF16),
    ]
    return pl.pallas_call(
        functools.partial(front_kernel, sizes, dims),
        out_shape=[jax.ShapeDtypeStruct(*shape) for shape in shapes],
        in_specs=[VMEM_SPEC] * 7,
        out_specs=[VMEM_SPEC] * len(shapes),
        scratch_shapes=[
            pltpu.VMEM((2, rows, width), BF16),
            pltpu.VMEM((128, 2 * seq), F32),
            pltpu.VMEM((rows, width), BF16),
            pltpu.VMEM((rows, width), BF16),
            pltpu.VMEM((experts, capacity, width), BF16),
            pltpu.VMEM((experts, capacity, width), BF16),
            pltpu.SemaphoreType.DMA((12,)),
            pltpu.SemaphoreType.DMA((12,)),
            pltpu.SemaphoreType.DMA((5,)),
        ],
        compiler_params=pltpu.CompilerParams(
            collective_id=0, has_side_effects=True, vmem_limit_bytes=48 * 2**20
        ),
        cost_estimate=pl.CostEstimate(flops=30 * 10**9, bytes_accessed=10**8, transcendentals=10**6),
    )(tokens, small, w_qkv, w_out, bucket_row, dispatch, cotangent)


def expert_kernel(
    capacity,
    rows_ref,
    grads_ref,
    in_ref,
    back_ref,
    active_ref,
    d_pre_ref,
    sent_ref,
    result_ref,
    d_result_ref,
):
    rows = rows_ref[...]
    grads = grads_ref[...]
    gate = lifted(rows[:, :128], capacity)
    d_result_ref[...] = (gate * grads.astype(F32)).astype(BF16)
    hidden = in_ref.shape[1]
    step = min(hidden, 512)
    root = 0.7978845608028654
    sent, result, d_gate = 0.0, 0.0, 0.0
    for at in range(0, hidden, step):
        w_in, w_back = in_ref[:, at : at + step], back_ref[at : at + step, :]
        pre = matmul(rows, w_in)
        d_active = matmul_t(grads, w_back)
        square = pre * pre
        wave = jnp.tanh(root * pre * (1.0 + 0.044715 * square))
        upper = 0.5 * (1.0 + wave)
        slope = upper + 0.5 * pre * (1.0 - wave * wave) * (
            root * (1.0 + 3 * 0.044715 * square)
        )
        active = (pre * upper).astype(BF16)
        d_gate = d_gate + jnp.sum(active.astype(F32) * d_active, axis=1, keepdims=True)
        d_pre = (gate * d_active * slope).astype(BF16)
        active_ref[:, at : at + step] = active
        d_pre_ref[:, at : at + step] = d_pre
        result = result + matmul(active, w_back)
        sent = sent + matmul_t(d_pre, w_in)
    result_ref[...] = result.astype(BF16)
    sent_ref[...] = sent.astype(BF16)
    sent_ref[:, :128] = (sent[:, :128] + lowered(d_gate, capacity)).astype(BF16)


def expert(capacity, rows, grads, w_in, w_back):
    count, width = rows.shape
    hidden = w_in.shape[1]
    step = min(count, max(256, capacity))
    by_rows = [pl.BlockSpec((step, size), lambda i: (i, 0)) for size in (width, hidden)]
    return pl.pallas_call(
        functools.partial(expert_kernel, capacity),
        grid=(count // step,),
        out_shape=[
            jax.ShapeDtypeStruct((count, hidden), BF16),
            jax.ShapeDtypeStruct((count, hidden), BF16),
            jax.ShapeDtypeStruct((count, width), BF16),
            jax.ShapeDtypeStruct((count, width), BF16),
            jax.ShapeDtypeStruct((count, width), BF16),
        ],
        in_specs=[
            by_rows[0],
            by_rows[0],
            pl.BlockSpec(w_in.shape, lambda i: (0, 0)),
            pl.BlockSpec(w_back.shape, lambda i: (0, 0)),
        ],
        out_specs=[by_rows[1], by_rows[1], by_rows[0], by_rows[0], by_rows[0]],
        compiler_params=pltpu.CompilerParams(vmem_limit_bytes=40 * 2**20),
        cost_estimate=pl.CostEstimate(
            flops=8 * count * width * hidden, bytes_accessed=2 * 10**7, transcendentals=count * hidden
        ),
    )(rows, grads, w_in, w_back)


def back_kernel(
    sizes,
    dims,
    both,
    cut,
    sent_ref,
    result_ref,
    dispatch_ref,
    gout_ref,
    tok_ref,
    n1_ref,
    proj_ref,
    chance_ref,
    mixed_ref,
    w_all,
    small_all,
    hidden_ref,
    n2_ref,
    router_ref,
    wout_ref,
    bucket_ref,
    layer_ref,
    gtok_ref,
    gqkv_ref,
    gout_w_ref,
    grouter_ref,
    gsmall_ref,
    att_all,
    dqkv,
    sums,
    part_out,
    part_in,
    comm,
    total_ref,
    chip_in,
    chip,
    row_in,
    column_in,
    row_sum,
    column_sum,
    deep,
    deep_in,
    returned,
    send,
    recv,
    all_sems,
):
    heads, experts, capacity, buckets = dims
    ys, xs, zs = sizes
    rows, width = tok_ref.shape
    half = width // 2
    seq = 2 * rows
    own_heads = heads // 2
    head = width // heads
    blocks = half // 128
    chunk_rows = comm.shape[2]
    rep, mine = lax.axis_index("rep"), lax.axis_index("shard")
    other = 1 - mine
    core = lax.rem(rep, 2)
    z = lax.rem(rep // 2, zs)
    x = lax.rem(rep // (2 * zs), xs)
    y = rep // (2 * zs * xs)

    def place(y_at, x_at, z_at, core_at):
        return ((y_at * xs + x_at) * zs + z_at) * 2 + core_at

    xp = [lax.rem(x + step, xs) for step in range(1, xs)]
    yp = [lax.rem(y + step, ys) for step in range(1, ys)]
    zp = [lax.rem(z + step, zs) for step in range(1, zs)]
    core_peer = (place(y, x, z, 1 - core), mine)
    x_peers = [(place(y, at, z, core), mine) for at in xp]
    y_peers = [(place(at, x, z, core), mine) for at in yp]
    z_peers = [(place(y, x, at, core), mine) for at in zp]
    peer = (rep, other)
    devices = 2 * experts
    me = 2 * rep + mine
    greet_all(devices)
    number = [0]

    def send_to(source, target, to):
        i = number[0]
        number[0] += 1
        copy = pltpu.make_async_remote_copy(
            source, target, send.at[i], recv.at[i], to, device_id_type=MESH
        )
        copy.start()
        return copy

    def finish(copies):
        for copy in copies:
            copy.wait()

    wide = sent_ref.shape[0]
    step = min(wide, max(256, capacity))
    d_gate = jnp.concatenate(
        [lifted(sent_ref[at : at + step, :128], capacity) for at in range(0, wide, step)], axis=0
    )
    shift = capacity.bit_length() - 1
    own_lane = (iota((wide, 128), 0) >> (shift + 1)) == iota((wide, 128), 1)
    d_gate = jnp.where(own_lane, d_gate, 0.0)
    dispatch = dispatch_ref[...]
    high, low = two_parts(d_gate)
    d_router = matmul(dispatch, high) + matmul(dispatch, low)
    router = router_ref[...]
    d_logits = router * (d_router - jnp.sum(router * d_router, axis=-1, keepdims=True))
    d_logits = d_logits.astype(BF16)
    d_n2 = matmul(dispatch, sent_ref[...]) + matmul_t(d_logits, router_weight(small_all, half))
    hidden = hidden_ref[...]
    factor = rms_factor(hidden)
    unit = hidden * factor
    scaled = d_n2 * gain_row(small_all, half, blocks)
    d_hidden = gout_ref[...].astype(F32) + factor * (
        scaled - unit * jnp.mean(scaled * unit, axis=-1, keepdims=True)
    )
    att_all[mine] = d_hidden.astype(BF16)
    shared = send_to(att_all.at[mine], att_all.at[mine], peer)
    send_blocks(lambda to: result_ref.at[to], returned, devices, all_sems.at[0], all_sems.at[1])
    own_block = pltpu.make_async_copy(result_ref.at[me], returned.at[me], all_sems.at[2])
    own_block.start()
    gtok_ref[...] = d_hidden
    g_gain_two = jnp.sum(d_n2 * unit, axis=0, keepdims=True)
    g_router = t_matmul(n2_ref[...], d_logits)

    def store(part, first, block):
        base = part * both
        span = both if part < 2 else chunk_rows - 2 * both
        at = 0
        while at < block.shape[0]:
            chunk_at, inside = divmod(first + at, span)
            count = min(span - inside, block.shape[0] - at)
            comm[chunk_at // 2, chunk_at % 2, base + inside : base + inside + count, :] = block[
                at : at + count
            ]
            at += count

    tile_rows = 3 * blocks * half
    for side in range(2):
        store(side, tile_rows, g_router[side * half : (side + 1) * half].astype(BF16))
    shared.wait()

    d_att = [att_all[0], att_all[1]]
    for block in range(2 * blocks):
        columns = slice(block * 128, (block + 1) * 128)
        grad = t_matmul(mixed_ref[:rows, :], d_att[0][:, columns])
        grad = grad + t_matmul(mixed_ref[rows:, :], d_att[1][:, columns])
        store(2, block * half, grad.astype(BF16))
    d_mixed = jnp.concatenate(
        [matmul_t(part, wout_ref[...]).astype(BF16) for part in d_att], axis=0
    )
    scale = head ** (-0.5)
    flip = (iota((seq, seq), 0) + iota((seq, seq), 1) == seq - 1).astype(F32).astype(BF16)
    for h in range(own_heads):
        at = h * head
        query = proj_ref[:, at : at + head]
        key = proj_ref[:, half + at : half + at + head]
        value = proj_ref[:, 2 * half + at : 2 * half + at + head]
        d_o = d_mixed[:, at : at + head]
        chance = chance_ref[h]
        d_chance = matmul_t(d_o, value)
        wide_chance = chance.astype(F32)
        inner = jnp.sum(wide_chance * d_chance, axis=-1, keepdims=True)
        d_scores = (wide_chance * (d_chance - inner)).astype(BF16)
        dqkv[:, at : at + head] = (matmul(d_scores, key) * scale).astype(BF16)
        dqkv[:, half + at : half + at + head] = (t_matmul(d_scores, query) * scale).astype(BF16)
        dqkv[:, 2 * half + at : 2 * half + at + head] = t_matmul(chance, d_o).astype(BF16)
        flipped = matmul(flip, d_scores)
        flipped = jnp.concatenate([flipped, jnp.zeros((seq, seq), F32)], axis=1)
        lined = pltpu.roll(flipped, 0, 1, stride=1, stride_axis=0)
        sums[pl.ds(mine * own_heads + h, 1), :] = jnp.sum(lined, axis=0, keepdims=True)
        sums[pl.ds(other * own_heads + h, 1), :] = jnp.zeros((1, 2 * seq), F32)

    theirs = pl.ds(pl.multiple_of(other * rows, 16), rows)
    ours = pl.ds(pl.multiple_of(mine * rows, 16), rows)

    def d_normed(which):
        return jnp.concatenate(
            [matmul_t(dqkv[which, :], w_all[side]) for side in range(2)], axis=1
        )

    part_out[...] = d_normed(theirs).astype(BF16)
    part_copy = send_to(part_out, part_in, peer)
    d_n1 = d_normed(ours)
    for block in range(3 * blocks):
        grad = t_matmul(n1_ref[...], dqkv[:, block * 128 : (block + 1) * 128]).astype(BF16)
        for side in range(2):
            store(side, block * half, grad[side * half : (side + 1) * half])
    levels = iota((buckets, 2 * seq), 0)
    one_hot = (levels == bucket_ref[...]).astype(F32).astype(BF16)
    high, low = two_parts(sums[...])
    g_table = (matmul_t(one_hot, high) + matmul_t(one_hot, low)).astype(BF16)
    for side in range(2):
        part = g_table[side * (buckets // 2) : (side + 1) * (buckets // 2)]
        store(side, tile_rows + half + 16, part)
    part_copy.wait()
    d_n1 = d_n1 + part_in[...].astype(F32)
    values = tok_ref[...].astype(F32)
    factor = rms_factor(values)
    unit = values * factor
    scaled = d_n1 * gain_row(small_all, half, 0)
    gtok_ref[...] = gtok_ref[...] + factor * (
        scaled - unit * jnp.mean(scaled * unit, axis=-1, keepdims=True)
    )
    g_gain_one = jnp.sum(d_n1 * unit, axis=0, keepdims=True)
    for side in range(2):
        pieces = [
            gain[:, side * half + i * 128 : side * half + (i + 1) * 128]
            for gain in (g_gain_one, g_gain_two)
            for i in range(blocks)
        ]
        pieces.append(jnp.zeros((16 - 2 * blocks, 128), F32))
        store(side, tile_rows + half, jnp.concatenate(pieces, axis=0).astype(BF16))

    first, second = pl.ds(0, cut), pl.ds(cut, chunk_rows - cut)
    chip_copy = send_to(comm.at[:, 1 - core], chip_in, core_peer)

    own_block.wait()
    wait_blocks(returned, devices, all_sems.at[0], all_sems.at[1])
    layer = hidden_ref[...]
    router_parts = two_parts(router_ref[...])
    per_step = step // capacity
    for i in range(wide // step):
        spread = (
            (iota((128, step), 1) + i * step) >> (shift + 1) == iota((128, step), 0)
        ).astype(F32).astype(BF16)
        weights = matmul(router_parts[0], spread) + matmul(router_parts[1], spread)
        weights = weights * dispatch_ref[:, i * step : (i + 1) * step].astype(F32)
        block = returned[i * per_step : (i + 1) * per_step].astype(F32)
        block = block.reshape(step, width).astype(BF16)
        for part in two_parts(weights):
            layer = layer + matmul(part, block)
    layer_ref[...] = layer.astype(BF16)
    finish([chip_copy])

    def add_chip(i, carry):
        total = comm[i, core].astype(F32) + chip_in[i].astype(F32)
        chip[i // (xs * zs), lax.rem(i // zs, xs), lax.rem(i, zs)] = total.astype(BF16)
        return carry

    lax.fori_loop(0, ys * xs * zs, add_chip, 0)
    copies = [
        send_to(chip.at[:, at, :, first], row_in.at[i], to)
        for i, (at, to) in enumerate(zip(xp, x_peers))
    ]
    copies += [
        send_to(chip.at[at, :, :, second], column_in.at[i], to)
        for i, (at, to) in enumerate(zip(yp, y_peers))
    ]
    finish(copies)

    def add_row(i, carry):
        for k in range(zs):
            total = chip[i, x, k, first].astype(F32)
            for j in range(xs - 1):
                total = total + row_in[j, i, k].astype(F32)
            row_sum[i, k] = total.astype(BF16)
        return carry

    def add_column(i, carry):
        for k in range(zs):
            total = chip[y, i, k, second].astype(F32)
            for j in range(ys - 1):
                total = total + column_in[j, i, k].astype(F32)
            column_sum[i, k] = total.astype(BF16)
        return carry

    lax.fori_loop(0, ys, add_row, 0)
    lax.fori_loop(0, xs, add_column, 0)
    copies = [
        send_to(row_sum.at[at], row_in.at[xs - 1 + i, 0], to)
        for i, (at, to) in enumerate(zip(yp, y_peers))
    ]
    copies += [
        send_to(column_sum.at[at], column_in.at[ys - 1 + i, 0], to)
        for i, (at, to) in enumerate(zip(xp, x_peers))
    ]
    finish(copies)
    for k in range(zs):
        total = row_sum[y, k].astype(F32)
        for i in range(ys - 1):
            total = total + row_in[xs - 1 + i, 0, k].astype(F32)
        deep[k, first] = total.astype(BF16)
        total = column_sum[x, k].astype(F32)
        for i in range(xs - 1):
            total = total + column_in[ys - 1 + i, 0, k].astype(F32)
        deep[k, second] = total.astype(BF16)
    finish([send_to(deep.at[at], deep_in.at[i], to) for i, (at, to) in enumerate(zip(zp, z_peers))])
    total = deep[z].astype(F32)
    for i in range(zs - 1):
        total = total + deep_in[i].astype(F32)
    done = total.astype(BF16)
    mine_at = pl.ds(pl.multiple_of(mine * both, 16), both)
    other_at = pl.ds(pl.multiple_of(other * both, 16), both)
    deep_in[zs - 1] = done
    out = total_ref.at[y, x, z, core]
    copies = [send_to(deep_in.at[zs - 1, other_at], out.at[mine_at], peer)]
    out[mine_at] = deep_in[zs - 1, mine_at]
    out[2 * both :] = done[2 * both :]
    finish(copies)
    finish([send_to(out, out, to) for to in z_peers])
    firsts = total_ref.at[y, x, :, core, first]
    seconds = total_ref.at[y, x, :, core, second]
    copies = [send_to(firsts, firsts, to) for to in y_peers]
    copies += [send_to(seconds, seconds, to) for to in x_peers]
    finish(copies)
    firsts = total_ref.at[:, x, :, core, first]
    seconds = total_ref.at[y, :, :, core, second]
    copies = [send_to(firsts, firsts, to) for to in x_peers]
    copies += [send_to(seconds, seconds, to) for to in y_peers]
    finish(copies)
    whole = total_ref.at[:, :, :, core]
    finish([send_to(whole, whole, core_peer)])

    def load(part, start, count):
        base = part * both
        span = both if part < 2 else chunk_rows - 2 * both
        pieces, at = [], 0
        while at < count:
            chunk_at, inside = divmod(start + at, span)
            size = min(span - inside, count - at)
            spot = (
                chunk_at // (2 * zs * xs),
                (chunk_at // (2 * zs)) % xs,
                (chunk_at // 2) % zs,
                chunk_at % 2,
            )
            pieces.append(total_ref[spot + (slice(base + inside, base + inside + size),)])
            at += size
        return pieces[0] if len(pieces) == 1 else jnp.concatenate(pieces, axis=0)

    for side in range(2):
        for block in range(3 * blocks):
            at = (block // blocks) * width + side * half + (block % blocks) * 128
            gqkv_ref[:, at : at + 128] = load(side, block * half, half)
    for block in range(2 * blocks):
        gout_w_ref[:, block * 128 : (block + 1) * 128] = load(2, block * half, half)
    grouter_ref[...] = sum(load(side, tile_rows, half).astype(F32) for side in range(2))
    gsmall_ref[...] = sum(
        load(side, tile_rows + half, 16 + buckets // 2).astype(F32) for side in range(2)
    )


def back(sizes, dims, sent, result, dispatch, cotangent, tokens, kept, w_out, bucket_row):
    ys, xs, zs = sizes
    heads, experts, capacity, buckets = dims
    rows, width = tokens.shape
    half, seq, lanes = width // 2, 2 * rows, 128
    count = 2 * ys * xs * zs
    both = up(3 * half * half // 128 + half + 16 + buckets // 2, 16 * count) // count
    chunk_rows = 2 * both + up(half * width // 128, 16 * count) // count
    cut = up(chunk_rows // 2, 16)
    per_core = count // 2
    many = 4 * (xs + ys) + 2 * zs + 4
    shapes = [
        ((rows, width), BF16),
        ((rows, width), F32),
        ((half, 3 * width), BF16),
        ((half, width), BF16),
        ((half, 128), F32),
        ((16 + buckets // 2, 128), F32),
    ]
    return pl.pallas_call(
        functools.partial(back_kernel, sizes, dims, both, cut),
        out_shape=[jax.ShapeDtypeStruct(*shape) for shape in shapes],
        in_specs=[VMEM_SPEC] * 16,
        out_specs=[VMEM_SPEC] * len(shapes),
        scratch_shapes=[
            pltpu.VMEM((2, rows, width), BF16),
            pltpu.VMEM((seq, 3 * half), BF16),
            pltpu.VMEM((128, 2 * seq), F32),
            pltpu.VMEM((rows, width), BF16),
            pltpu.VMEM((rows, width), BF16),
            pltpu.VMEM((per_core, 2, chunk_rows, lanes), BF16),
            pltpu.VMEM((ys, xs, zs, 2, chunk_rows, lanes), BF16),
            pltpu.VMEM((per_core, chunk_rows, lanes), BF16),
            pltpu.VMEM((ys, xs, zs, chunk_rows, lanes), BF16),
            pltpu.VMEM((xs + ys - 2, ys, zs, cut, lanes), BF16),
            pltpu.VMEM((xs + ys - 2, xs, zs, chunk_rows - cut, lanes), BF16),
            pltpu.VMEM((ys, zs, cut, lanes), BF16),
            pltpu.VMEM((xs, zs, chunk_rows - cut, lanes), BF16),
            pltpu.VMEM((zs, chunk_rows, lanes), BF16),
            pltpu.VMEM((zs, chunk_rows, lanes), BF16),
            pltpu.VMEM(result.shape, BF16),
            pltpu.SemaphoreType.DMA((many,)),
            pltpu.SemaphoreType.DMA((many,)),
            pltpu.SemaphoreType.DMA((3,)),
        ],
        compiler_params=pltpu.CompilerParams(
            collective_id=1, has_side_effects=True, vmem_limit_bytes=56 * 2**20
        ),
        cost_estimate=pl.CostEstimate(flops=60 * 10**9, bytes_accessed=2 * 10**8, transcendentals=0),
    )(sent, result, dispatch, cotangent, tokens, *kept, w_out, bucket_row)


def body(
    sizes,
    tokens,
    cotangent,
    attn_gain,
    w_qkv,
    w_out,
    rel_bias,
    buckets,
    ffn_gain,
    w_router,
    w_in,
    w_back,
    choice_ids,
):
    rows, width = tokens.shape
    half = width // 2
    bucket_half, heads = rel_bias.shape
    experts = w_router.shape[1]
    top = choice_ids.shape[1]
    capacity = up(max(2, 5 * rows * top // (4 * experts)) + 1, 8)
    slots = experts * capacity
    seq = 2 * rows
    dims = (heads, experts, capacity, 2 * bucket_half)
    blocks = half // 128

    flat_ids = choice_ids.reshape(-1)
    levels = jnp.arange(experts, dtype=jnp.int32)
    member = (flat_ids[:, None] == levels[None, :]).astype(BF16)
    order = jnp.arange(rows * top, dtype=jnp.int32)
    before = (order[:, None] > order[None, :]).astype(BF16)
    earlier = matmul(before, member)
    rank = jnp.sum(earlier * member.astype(F32), axis=1).astype(jnp.int32)
    slot = (flat_ids * capacity + rank).reshape(rows, top)
    dispatch = jnp.sum(
        (slot[:, :, None] == jnp.arange(slots, dtype=jnp.int32)).astype(BF16), axis=1
    )
    dispatch_two = jnp.broadcast_to(
        dispatch.reshape(rows, experts, 1, capacity), (rows, experts, 2, capacity)
    ).reshape(rows, 2 * slots)

    def swap_all(all_rows):
        blocks = all_rows.reshape(2 * experts, capacity, width)
        got = lax.all_to_all(blocks, ("rep", "shard"), split_axis=0, concat_axis=0, tiled=True)
        return got.reshape(2 * slots, width)

    gains = jnp.concatenate([attn_gain.reshape(blocks, 128), ffn_gain.reshape(blocks, 128)])
    small = jnp.concatenate(
        [
            jnp.pad(w_router, ((0, 0), (0, 128 - experts))),
            jnp.pad(gains, ((0, 16 - 2 * blocks), (0, 0))),
            jnp.pad(rel_bias, ((0, 0), (0, 128 - heads))),
        ]
    )
    nothing = jnp.full((seq,), -1, jnp.int32)
    back_order = buckets[::-1]
    bucket_front = jnp.concatenate([buckets[:1], nothing, back_order[:-1]]).reshape(1, 2 * seq)
    bucket_back = jnp.concatenate([back_order, nothing]).reshape(1, 2 * seq)
    *kept, arrived, grad_rows = front(
        sizes, dims, tokens, small, w_qkv, w_out, bucket_front, dispatch, cotangent
    )
    arrived, grad_rows = (block.reshape(2 * slots, width) for block in (arrived, grad_rows))

    expert_in, expert_back = w_in[0], w_back[0]
    activated, grad_pre, grad_arrived, result, grad_result = expert(
        capacity, arrived, grad_rows, expert_in, expert_back
    )
    sent = swap_all(grad_arrived)
    result = result.reshape(2 * experts, capacity, width)
    grad_back_expert = t_matmul(activated, grad_result)
    grad_in_expert = t_matmul(arrived, grad_pre)

    layer_out, grad_tokens, g_qkv, g_out, g_router, g_small = back(
        sizes, dims, sent, result, dispatch_two, cotangent, tokens, kept, w_out, bucket_back
    )

    return (
        layer_out,
        grad_tokens,
        g_small[:blocks].reshape(half),
        g_qkv.astype(F32),
        g_out.astype(F32),
        g_small[16:, :heads],
        g_small[blocks : 2 * blocks].reshape(half),
        g_router[:, :experts],
        grad_in_expert[None],
        grad_back_expert[None],
    )


SIZES = {64: (4, 4, 2), 4: (2, 1, 1), 8: (2, 2, 1)}


def solution(mesh):
    in_specs = (
        P(("rep", "shard"), None),
        P(("rep", "shard"), None),
        P("shard"),
        P("shard", None),
        P("shard", None),
        P("shard", None),
        P(),
        P("shard"),
        P("shard", None),
        P("rep", None, "shard"),
        P("rep", "shard", None),
        P(("rep", "shard"), None),
    )
    out_specs = (
        P(("rep", "shard"), None),
        P(("rep", "shard"), None),
        P("shard"),
        P("shard", None),
        P("shard", None),
        P("shard", None),
        P("shard"),
        P("shard", None),
        P("rep", None, "shard"),
        P("rep", "shard", None),
    )
    sizes = SIZES[mesh.shape["rep"]]
    return jax.shard_map(
        functools.partial(body, sizes),
        mesh=mesh,
        in_specs=in_specs,
        out_specs=out_specs,
        check_vma=False,
    )
```

```python
import functools

import jax
import jax.numpy as jnp
from jax import lax
from jax.experimental import pallas as pl
from jax.experimental.pallas import tpu as pltpu
from jax.sharding import PartitionSpec as P

EPSILON = 1e-06
MASKED = -1e30
MESH = pl.DeviceIdType.MESH
VMEM_SPEC = pl.BlockSpec(memory_space=pltpu.VMEM)
F32 = jnp.float32
BF16 = jnp.bfloat16


def greet_all(count):
    me = 2 * lax.axis_index("rep") + lax.axis_index("shard")
    barrier = pltpu.get_barrier_semaphore()

    def signal(step, carry):
        to = lax.rem(me + step, count)
        pl.semaphore_signal(
            barrier, inc=1, device_id=(to // 2, lax.rem(to, 2)), device_id_type=MESH
        )
        return carry

    lax.fori_loop(1, count, signal, 0)
    pl.semaphore_wait(barrier, count - 1)


def send_blocks(source_of, target, count, send, recv):
    me = 2 * lax.axis_index("rep") + lax.axis_index("shard")

    def start(step, carry):
        to = lax.rem(me + step, count)
        pltpu.make_async_remote_copy(
            source_of(to),
            target.at[me],
            send,
            recv,
            (to // 2, lax.rem(to, 2)),
            device_id_type=MESH,
        ).start()
        return carry

    lax.fori_loop(1, count, start, 0)


def wait_blocks(target, count, send, recv):
    rep, mine = lax.axis_index("rep"), lax.axis_index("shard")
    most = target.at[pl.ds(0, count - 1)]
    pltpu.make_async_remote_copy(
        most, most, send, recv, (rep, 1 - mine), device_id_type=MESH
    ).wait()


def up(number, step):
    return -(-number // step) * step


def greet(peers):
    barrier = pltpu.get_barrier_semaphore()
    for peer in peers:
        pl.semaphore_signal(barrier, inc=1, device_id=peer, device_id_type=MESH)
    pl.semaphore_wait(barrier, len(peers))


def iota(shape, axis):
    return lax.broadcasted_iota(jnp.int32, shape, axis)


def dot(a, b, contract):
    return lax.dot_general(a, b, (contract, ((), ())), preferred_element_type=F32)


def matmul(a, b):
    return dot(a, b, ((1,), (0,)))


def matmul_t(a, b):
    return dot(a, b, ((1,), (1,)))


def t_matmul(a, b):
    return dot(a, b, ((0,), (0,)))


def two_parts(values):
    high = values.astype(BF16)
    return high, (values - high.astype(F32)).astype(BF16)


def rms_factor(values):
    return lax.rsqrt(jnp.mean(values * values, axis=-1, keepdims=True) + EPSILON)


def gain_row(small_ref, half, first):
    blocks = half // 128
    pieces = [
        small_ref[side, pl.ds(half + first + i, 1), :].astype(F32)
        for side in range(2)
        for i in range(blocks)
    ]
    return jnp.concatenate(pieces, axis=1)


def router_weight(small_ref, half):
    return jnp.concatenate([small_ref[0, :half, :], small_ref[1, :half, :]], axis=0)


def lifted(block, capacity):
    count = block.shape[0]
    shift = capacity.bit_length() - 1
    source, slot = iota((count, count), 1), iota((count, count), 0)
    carrier = (source == ((slot >> shift) << shift) + capacity - 1).astype(F32).astype(BF16)
    carried = matmul(carrier, block)
    lane, slot = iota((count, 128), 1), iota((count, 128), 0)
    mask = ((lane & (capacity - 1)) == (slot & (capacity - 1))) & (lane < 2 * capacity)
    return jnp.sum(jnp.where(mask, carried, 0.0), axis=1, keepdims=True)


def lowered(column, capacity):
    count = column.shape[0]
    shift = capacity.bit_length() - 1
    target, slot = iota((count, count), 0), iota((count, count), 1)
    carrier = (target == ((slot >> shift) << shift) + capacity - 1).astype(F32).astype(BF16)
    lane, slot = iota((count, 128), 1), iota((count, 128), 0) & (capacity - 1)
    high, low = two_parts(column)
    spread = jnp.where(lane == slot, high.astype(F32), 0.0)
    spread = spread + jnp.where(lane == slot + capacity, low.astype(F32), 0.0)
    return matmul(carrier, spread.astype(BF16))


def front_kernel(
    sizes,
    dims,
    tok_ref,
    small_ref,
    wqkv_ref,
    wout_ref,
    bucket_ref,
    dispatch_ref,
    gout_ref,
    n1_ref,
    proj_ref,
    chance_ref,
    mixed_ref,
    w_all,
    small_all,
    hidden_ref,
    n2_ref,
    router_ref,
    arrived_ref,
    grad_rows_ref,
    tok_all,
    bias_rows,
    part_out,
    part_in,
    outgoing,
    outgoing_grads,
    send,
    recv,
    local,
):
    heads, experts, capacity, buckets = dims
    ys, xs, zs = sizes
    rows, width = tok_ref.shape
    half = width // 2
    seq = 2 * rows
    own_heads = heads // 2
    head = width // heads
    slots = experts * capacity
    rep, mine = lax.axis_index("rep"), lax.axis_index("shard")
    other = 1 - mine
    core = lax.rem(rep, 2)
    peer = (rep, other)
    core_peer = (rep + 1 - 2 * core, mine)
    devices = 2 * experts
    me = 2 * rep + mine
    if zs == 2:
        z = lax.rem(rep // 2, 2)
        far_peer = (rep + 2 * (1 - 2 * z), other)
    greet_all(devices)

    def remote(i, source, target, to):
        copy = pltpu.make_async_remote_copy(
            source, target, send.at[i], recv.at[i], to, device_id_type=MESH
        )
        copy.start()
        return copy

    small_copy = remote(0, small_ref, small_all.at[mine], peer)
    near = half // 2 if zs == 1 else up(half // 12, 16)
    fetched = [(peer, 0, near)]
    if zs == 2:
        fetched.append((far_peer, near, half // 2 - near))
    weight_copies = []
    for j, (to, first, count) in enumerate(fetched):
        at = pl.ds(pl.multiple_of(core * (half // 2) + first, 16), count)
        for block in range(3):
            theirs = pl.ds(pl.multiple_of((2 * block + other) * half, 128), half)
            weight_copies.append(
                remote(
                    2 + 3 * j + block,
                    wqkv_ref.at[at, theirs],
                    w_all.at[mine, at, pl.ds(block * half, half)],
                    to,
                )
            )
    tok_copy = remote(1, tok_ref, tok_all.at[mine], peer)
    kept = [
        pltpu.make_async_copy(tok_ref, tok_all.at[mine], local.at[0]),
        pltpu.make_async_copy(small_ref, small_all.at[mine], local.at[1]),
    ]
    for block in range(3):
        ours = pl.ds(pl.multiple_of((2 * block + mine) * half, 128), half)
        kept.append(
            pltpu.make_async_copy(
                wqkv_ref.at[:, ours], w_all.at[mine, :, pl.ds(block * half, half)], local.at[2 + block]
            )
        )
    for copy in kept:
        copy.start()
    for copy in kept:
        copy.wait()
    small_copy.wait()

    table = jnp.concatenate([small_all[0, half + 16 :, :], small_all[1, half + 16 :, :]], axis=0)
    levels = iota((buckets, 2 * seq), 0)
    one_hot = (levels == bucket_ref[...]).astype(F32).astype(BF16)
    bias_rows[...] = t_matmul(table, one_hot)
    gain_one = gain_row(small_all, half, 0)
    gain_two = gain_row(small_all, half, half // 128)
    dispatch = dispatch_ref[...]
    blocks = t_matmul(dispatch, gout_ref[...]).reshape(experts, capacity, width)
    outgoing_grads[...] = blocks.astype(BF16)
    send_blocks(
        lambda to: outgoing_grads.at[to // 2], grad_rows_ref, devices, send.at[10], recv.at[10]
    )
    own_block = pltpu.make_async_copy(outgoing_grads.at[rep], grad_rows_ref.at[me], local.at[0])
    own_block.start()

    for copy in weight_copies:
        copy.wait()
    got = w_all.at[other, pl.ds(pl.multiple_of(core * (half // 2), 16), half // 2)]
    passed = remote(8, got, got, core_peer)
    tok_copy.wait()
    for side in range(2):
        values = tok_all[side].astype(F32)
        n1_ref[side * rows : (side + 1) * rows, :] = (
            values * rms_factor(values) * gain_one
        ).astype(BF16)
    passed.wait()
    normed = n1_ref[...]
    for block in range(3):
        columns = pl.ds(block * half, half)
        total = matmul(normed[:, :half], w_all[0, :, columns])
        total = total + matmul(normed[:, half:], w_all[1, :, columns])
        proj_ref[:, columns] = total.astype(BF16)

    scale = head ** (-0.5)
    causal = iota((seq, seq), 0) >= iota((seq, seq), 1)
    for h in range(own_heads):
        at = h * head
        query = proj_ref[:, at : at + head]
        key = proj_ref[:, half + at : half + at + head]
        value = proj_ref[:, 2 * half + at : 2 * half + at + head]
        row = bias_rows[pl.ds(mine * own_heads + h, 1), :]
        bias = pltpu.roll(
            jnp.broadcast_to(row, (seq, 2 * seq)), 0, 1, stride=1, stride_axis=0
        )[:, :seq]
        scores = jnp.where(causal, matmul_t(query, key) * scale + bias, MASKED)
        raised = jnp.exp(scores - jnp.max(scores, axis=-1, keepdims=True))
        chance = (raised / jnp.sum(raised, axis=-1, keepdims=True)).astype(BF16)
        chance_ref[h] = chance
        mixed_ref[:, at : at + head] = matmul(chance, value).astype(BF16)

    theirs = pl.ds(pl.multiple_of(other * rows, 16), rows)
    ours = pl.ds(pl.multiple_of(mine * rows, 16), rows)
    part_out[...] = matmul(mixed_ref[theirs, :], wout_ref[...]).astype(BF16)
    part_copy = remote(9, part_out, part_in, peer)
    hidden = tok_ref[...].astype(F32) + matmul(mixed_ref[ours, :], wout_ref[...])
    part_copy.wait()
    hidden = hidden + part_in[...].astype(F32)
    hidden_ref[...] = hidden
    normed = (hidden * rms_factor(hidden) * gain_two).astype(BF16)
    n2_ref[...] = normed
    logits = matmul(normed, router_weight(small_all, half))
    logits = jnp.where(iota((rows, 128), 1) < experts, logits, MASKED)
    raised = jnp.exp(logits - jnp.max(logits, axis=-1, keepdims=True))
    router = raised / jnp.sum(raised, axis=-1, keepdims=True)
    router_ref[...] = router

    shift = capacity.bit_length() - 1
    spread = (iota((128, slots), 0) == (iota((128, slots), 1) >> shift)).astype(F32).astype(BF16)
    row_of, slot_of = iota((slots, slots), 0), iota((slots, slots), 1)
    carrier = ((row_of & (capacity - 1)) == capacity - 1) & (
        (row_of >> shift) == (slot_of >> shift)
    )
    place = iota((slots, 128), 0) & (capacity - 1)
    gates = jnp.zeros((slots, 128), F32)
    for i, part in enumerate(two_parts(router)):
        gate = jnp.sum(matmul(part, spread) * dispatch.astype(F32), axis=0, keepdims=True)
        left = jnp.where(carrier, gate, 0.0).astype(BF16)
        right = (place == iota((slots, 128), 1) - i * capacity).astype(F32).astype(BF16)
        gates = gates + matmul(left, right)
    sent = t_matmul(dispatch, normed)
    first = (sent[:, :128] + gates).reshape(experts, capacity, 128)
    outgoing[...] = sent.reshape(experts, capacity, width).astype(BF16)
    outgoing[:, :, :128] = first.astype(BF16)
    send_blocks(lambda to: outgoing.at[to // 2], arrived_ref, devices, send.at[11], recv.at[11])
    own_block.wait()
    own_block = pltpu.make_async_copy(outgoing.at[rep], arrived_ref.at[me], local.at[0])
    own_block.start()
    own_block.wait()
    wait_blocks(grad_rows_ref, devices, send.at[10], recv.at[10])
    wait_blocks(arrived_ref, devices, send.at[11], recv.at[11])


def front(sizes, dims, tokens, small, w_qkv, w_out, bucket_row, dispatch, cotangent):
    rows, width = tokens.shape
    heads, experts, capacity, buckets = dims
    half, seq, slots = width // 2, 2 * rows, experts * capacity
    shapes = [
        ((seq, width), BF16),
        ((seq, 3 * half), BF16),
        ((heads // 2, seq, seq), BF16),
        ((seq, half), BF16),
        ((2, half, 3 * half), BF16),
        ((2,) + small.shape, BF16),
        ((rows, width), F32),
        ((rows, width), BF16),
        ((rows, 128), F32),
        ((2 * experts, capacity, width), BF16),
        ((2 * experts, capacity, width), BF16),
    ]
    return pl.pallas_call(
        functools.partial(front_kernel, sizes, dims),
        out_shape=[jax.ShapeDtypeStruct(*shape) for shape in shapes],
        in_specs=[VMEM_SPEC] * 7,
        out_specs=[VMEM_SPEC] * len(shapes),
        scratch_shapes=[
            pltpu.VMEM((2, rows, width), BF16),
            pltpu.VMEM((128, 2 * seq), F32),
            pltpu.VMEM((rows, width), BF16),
            pltpu.VMEM((rows, width), BF16),
            pltpu.VMEM((experts, capacity, width), BF16),
            pltpu.VMEM((experts, capacity, width), BF16),
            pltpu.SemaphoreType.DMA((12,)),
            pltpu.SemaphoreType.DMA((12,)),
            pltpu.SemaphoreType.DMA((5,)),
        ],
        compiler_params=pltpu.CompilerParams(
            collective_id=0, has_side_effects=True, vmem_limit_bytes=48 * 2**20
        ),
        cost_estimate=pl.CostEstimate(flops=30 * 10**9, bytes_accessed=10**8, transcendentals=10**6),
    )(tokens, small, w_qkv, w_out, bucket_row, dispatch, cotangent)


def expert_kernel(
    capacity,
    rows_ref,
    grads_ref,
    in_ref,
    back_ref,
    active_ref,
    d_pre_ref,
    sent_ref,
    result_ref,
    d_result_ref,
):
    rows = rows_ref[...]
    grads = grads_ref[...]
    gate = lifted(rows[:, :128], capacity)
    d_result_ref[...] = (gate * grads.astype(F32)).astype(BF16)
    hidden = in_ref.shape[1]
    step = min(hidden, 512)
    root = 0.7978845608028654
    sent, result, d_gate = 0.0, 0.0, 0.0
    for at in range(0, hidden, step):
        w_in, w_back = in_ref[:, at : at + step], back_ref[at : at + step, :]
        pre = matmul(rows, w_in)
        d_active = matmul_t(grads, w_back)
        square = pre * pre
        wave = jnp.tanh(root * pre * (1.0 + 0.044715 * square))
        upper = 0.5 * (1.0 + wave)
        slope = upper + 0.5 * pre * (1.0 - wave * wave) * (
            root * (1.0 + 3 * 0.044715 * square)
        )
        active = (pre * upper).astype(BF16)
        d_gate = d_gate + jnp.sum(active.astype(F32) * d_active, axis=1, keepdims=True)
        d_pre = (gate * d_active * slope).astype(BF16)
        active_ref[:, at : at + step] = active
        d_pre_ref[:, at : at + step] = d_pre
        result = result + matmul(active, w_back)
        sent = sent + matmul_t(d_pre, w_in)
    result_ref[...] = result.astype(BF16)
    sent_ref[...] = sent.astype(BF16)
    sent_ref[:, :128] = (sent[:, :128] + lowered(d_gate, capacity)).astype(BF16)


def expert(capacity, rows, grads, w_in, w_back):
    count, width = rows.shape
    hidden = w_in.shape[1]
    step = min(count, max(256, capacity))
    by_rows = [pl.BlockSpec((step, size), lambda i: (i, 0)) for size in (width, hidden)]
    return pl.pallas_call(
        functools.partial(expert_kernel, capacity),
        grid=(count // step,),
        out_shape=[
            jax.ShapeDtypeStruct((count, hidden), BF16),
            jax.ShapeDtypeStruct((count, hidden), BF16),
            jax.ShapeDtypeStruct((count, width), BF16),
            jax.ShapeDtypeStruct((count, width), BF16),
            jax.ShapeDtypeStruct((count, width), BF16),
        ],
        in_specs=[
            by_rows[0],
            by_rows[0],
            pl.BlockSpec(w_in.shape, lambda i: (0, 0)),
            pl.BlockSpec(w_back.shape, lambda i: (0, 0)),
        ],
        out_specs=[by_rows[1], by_rows[1], by_rows[0], by_rows[0], by_rows[0]],
        compiler_params=pltpu.CompilerParams(vmem_limit_bytes=40 * 2**20),
        cost_estimate=pl.CostEstimate(
            flops=8 * count * width * hidden, bytes_accessed=2 * 10**7, transcendentals=count * hidden
        ),
    )(rows, grads, w_in, w_back)


def back_kernel(
    sizes,
    dims,
    cuts,
    sent_ref,
    result_ref,
    dispatch_ref,
    gout_ref,
    tok_ref,
    n1_ref,
    proj_ref,
    chance_ref,
    mixed_ref,
    w_all,
    small_all,
    hidden_ref,
    n2_ref,
    router_ref,
    wout_ref,
    bucket_ref,
    layer_ref,
    gtok_ref,
    gqkv_ref,
    gout_w_ref,
    grouter_ref,
    gsmall_ref,
    att_all,
    dqkv,
    sums,
    part_out,
    part_in,
    returned,
    send,
    recv,
    all_sems,
    *scratch,
):
    heads, experts, capacity, buckets = dims
    ys, xs, zs = sizes
    rows, width = tok_ref.shape
    half = width // 2
    seq = 2 * rows
    own_heads = heads // 2
    head = width // heads
    blocks = half // 128
    sets = [scratch[10 * i : 10 * i + 10] for i in range(3)]
    rep, mine = lax.axis_index("rep"), lax.axis_index("shard")
    other = 1 - mine
    core = lax.rem(rep, 2)
    z = lax.rem(rep // 2, zs)
    x = lax.rem(rep // (2 * zs), xs)
    y = rep // (2 * zs * xs)

    def place(y_at, x_at, z_at, core_at):
        return ((y_at * xs + x_at) * zs + z_at) * 2 + core_at

    xp = [lax.rem(x + step, xs) for step in range(1, xs)]
    yp = [lax.rem(y + step, ys) for step in range(1, ys)]
    zp = [lax.rem(z + step, zs) for step in range(1, zs)]
    core_peer = (place(y, x, z, 1 - core), mine)
    x_peers = [(place(y, at, z, core), mine) for at in xp]
    y_peers = [(place(at, x, z, core), mine) for at in yp]
    z_peers = [(place(y, x, at, core), mine) for at in zp]
    peer = (rep, other)
    devices = 2 * experts
    me = 2 * rep + mine
    greet_all(devices)
    number = [0]

    def send_to(source, target, to):
        i = number[0]
        number[0] += 1
        copy = pltpu.make_async_remote_copy(
            source, target, send.at[i], recv.at[i], to, device_id_type=MESH
        )
        copy.start()
        return copy

    def finish(copies):
        for copy in copies:
            copy.wait()

    wide = sent_ref.shape[0]
    step = min(wide, max(256, capacity))
    d_gate = jnp.concatenate(
        [lifted(sent_ref[at : at + step, :128], capacity) for at in range(0, wide, step)], axis=0
    )
    shift = capacity.bit_length() - 1
    own_lane = (iota((wide, 128), 0) >> (shift + 1)) == iota((wide, 128), 1)
    d_gate = jnp.where(own_lane, d_gate, 0.0)
    dispatch = dispatch_ref[...]
    high, low = two_parts(d_gate)
    d_router = matmul(dispatch, high) + matmul(dispatch, low)
    router = router_ref[...]
    d_logits = router * (d_router - jnp.sum(router * d_router, axis=-1, keepdims=True))
    d_logits = d_logits.astype(BF16)
    d_n2 = matmul(dispatch, sent_ref[...]) + matmul_t(d_logits, router_weight(small_all, half))
    hidden = hidden_ref[...]
    factor = rms_factor(hidden)
    unit = hidden * factor
    scaled = d_n2 * gain_row(small_all, half, blocks)
    d_hidden = gout_ref[...].astype(F32) + factor * (
        scaled - unit * jnp.mean(scaled * unit, axis=-1, keepdims=True)
    )
    att_all[mine] = d_hidden.astype(BF16)
    shared = send_to(att_all.at[mine], att_all.at[mine], peer)
    send_blocks(lambda to: result_ref.at[to], returned, devices, all_sems.at[0], all_sems.at[1])
    own_block = pltpu.make_async_copy(result_ref.at[me], returned.at[me], all_sems.at[2])
    own_block.start()
    gtok_ref[...] = d_hidden
    g_gain_two = jnp.sum(d_n2 * unit, axis=0, keepdims=True)
    g_router = t_matmul(n2_ref[...], d_logits)

    def span_of(which):
        both, n = cuts[which]
        return both if both else n

    def store(which, side, first, block):
        span, at = span_of(which), 0
        base = side * span
        while at < block.shape[0]:
            chunk_at, inside = divmod(first + at, span)
            count = min(span - inside, block.shape[0] - at)
            sets[which][0][
                chunk_at // 2, chunk_at % 2, base + inside : base + inside + count, :
            ] = block[at : at + count]
            at += count

    def replica_sum(which):
        comm, total_ref, chip_in, chip, row_in, column_in, row_sum, column_sum, deep, deep_in = (
            sets[which]
        )
        both, n = cuts[which]
        cut = up(n // 2, 16)
        first, second = pl.ds(0, cut), pl.ds(cut, n - cut)
        copies = [send_to(comm.at[:, 1 - core], chip_in, core_peer)]
        yield
        finish(copies)

        def add_chip(i, carry):
            total = comm[i, core].astype(F32) + chip_in[i].astype(F32)
            chip[i // (xs * zs), lax.rem(i // zs, xs), lax.rem(i, zs)] = total.astype(BF16)
            return carry

        lax.fori_loop(0, ys * xs * zs, add_chip, 0)
        copies = [
            send_to(chip.at[:, at, :, first], row_in.at[i], to)
            for i, (at, to) in enumerate(zip(xp, x_peers))
        ]
        copies += [
            send_to(chip.at[at, :, :, second], column_in.at[i], to)
            for i, (at, to) in enumerate(zip(yp, y_peers))
        ]
        yield
        finish(copies)

        def add_row(i, carry):
            for k in range(zs):
                total = chip[i, x, k, first].astype(F32)
                for j in range(xs - 1):
                    total = total + row_in[j, i, k].astype(F32)
                row_sum[i, k] = total.astype(BF16)
            return carry

        def add_column(i, carry):
            for k in range(zs):
                total = chip[y, i, k, second].astype(F32)
                for j in range(ys - 1):
                    total = total + column_in[j, i, k].astype(F32)
                column_sum[i, k] = total.astype(BF16)
            return carry

        lax.fori_loop(0, ys, add_row, 0)
        lax.fori_loop(0, xs, add_column, 0)
        copies = [
            send_to(row_sum.at[at], row_in.at[xs - 1 + i, 0], to)
            for i, (at, to) in enumerate(zip(yp, y_peers))
        ]
        copies += [
            send_to(column_sum.at[at], column_in.at[ys - 1 + i, 0], to)
            for i, (at, to) in enumerate(zip(xp, x_peers))
        ]
        yield
        finish(copies)
        for k in range(zs):
            total = row_sum[y, k].astype(F32)
            for i in range(ys - 1):
                total = total + row_in[xs - 1 + i, 0, k].astype(F32)
            deep[k, first] = total.astype(BF16)
            total = column_sum[x, k].astype(F32)
            for i in range(xs - 1):
                total = total + column_in[ys - 1 + i, 0, k].astype(F32)
            deep[k, second] = total.astype(BF16)
        copies = [
            send_to(deep.at[at], deep_in.at[i], to) for i, (at, to) in enumerate(zip(zp, z_peers))
        ]
        yield
        finish(copies)
        total = deep[z].astype(F32)
        for i in range(zs - 1):
            total = total + deep_in[i].astype(F32)
        deep_in[zs - 1] = total.astype(BF16)
        out = total_ref.at[y, x, z, core]
        if both:
            mine_at = pl.ds(pl.multiple_of(mine * both, 16), both)
            other_at = pl.ds(pl.multiple_of(other * both, 16), both)
            copies = [send_to(deep_in.at[zs - 1, other_at], out.at[mine_at], peer)]
            out[mine_at] = deep_in[zs - 1, mine_at]
            yield
            finish(copies)
        else:
            out[...] = deep_in[zs - 1]
        copies = [send_to(out, out, to) for to in z_peers]
        yield
        finish(copies)
        firsts = total_ref.at[y, x, :, core, first]
        seconds = total_ref.at[y, x, :, core, second]
        copies = [send_to(firsts, firsts, to) for to in y_peers]
        copies += [send_to(seconds, seconds, to) for to in x_peers]
        yield
        finish(copies)
        firsts = total_ref.at[:, x, :, core, first]
        seconds = total_ref.at[y, :, :, core, second]
        copies = [send_to(firsts, firsts, to) for to in x_peers]
        copies += [send_to(seconds, seconds, to) for to in y_peers]
        yield
        finish(copies)
        whole = total_ref.at[:, :, :, core]
        copies = [send_to(whole, whole, core_peer)]
        yield
        finish(copies)

    early = -(-5 * 3 * blocks // 9)
    tile_rows = (3 * blocks - early) * half
    for side in range(2):
        store(1, side, tile_rows, g_router[side * half : (side + 1) * half].astype(BF16))
    shared.wait()

    d_att = [att_all[0], att_all[1]]
    for block in range(2 * blocks):
        columns = slice(block * 128, (block + 1) * 128)
        grad = t_matmul(mixed_ref[:rows, :], d_att[0][:, columns])
        grad = grad + t_matmul(mixed_ref[rows:, :], d_att[1][:, columns])
        store(2, 0, block * half, grad.astype(BF16))
    sum_out = replica_sum(2)
    next(sum_out, None)
    d_mixed = jnp.concatenate(
        [matmul_t(part, wout_ref[...]).astype(BF16) for part in d_att], axis=0
    )
    scale = head ** (-0.5)
    flip = (iota((seq, seq), 0) + iota((seq, seq), 1) == seq - 1).astype(F32).astype(BF16)
    for h in range(own_heads):
        at = h * head
        query = proj_ref[:, at : at + head]
        key = proj_ref[:, half + at : half + at + head]
        value = proj_ref[:, 2 * half + at : 2 * half + at + head]
        d_o = d_mixed[:, at : at + head]
        chance = chance_ref[h]
        d_chance = matmul_t(d_o, value)
        wide_chance = chance.astype(F32)
        inner = jnp.sum(wide_chance * d_chance, axis=-1, keepdims=True)
        d_scores = (wide_chance * (d_chance - inner)).astype(BF16)
        dqkv[:, at : at + head] = (matmul(d_scores, key) * scale).astype(BF16)
        dqkv[:, half + at : half + at + head] = (t_matmul(d_scores, query) * scale).astype(BF16)
        dqkv[:, 2 * half + at : 2 * half + at + head] = t_matmul(chance, d_o).astype(BF16)
        flipped = matmul(flip, d_scores)
        flipped = jnp.concatenate([flipped, jnp.zeros((seq, seq), F32)], axis=1)
        lined = pltpu.roll(flipped, 0, 1, stride=1, stride_axis=0)
        sums[pl.ds(mine * own_heads + h, 1), :] = jnp.sum(lined, axis=0, keepdims=True)
        sums[pl.ds(other * own_heads + h, 1), :] = jnp.zeros((1, 2 * seq), F32)
        next(sum_out, None)

    theirs = pl.ds(pl.multiple_of(other * rows, 16), rows)
    ours = pl.ds(pl.multiple_of(mine * rows, 16), rows)

    def d_normed(which):
        return jnp.concatenate(
            [matmul_t(dqkv[which, :], w_all[side]) for side in range(2)], axis=1
        )

    part_out[...] = d_normed(theirs).astype(BF16)
    part_copy = send_to(part_out, part_in, peer)
    d_n1 = d_normed(ours)

    def weight_blocks(which, chosen):
        for i, block in enumerate(chosen):
            grad = t_matmul(n1_ref[...], dqkv[:, block * 128 : (block + 1) * 128]).astype(BF16)
            for side in range(2):
                store(which, side, i * half, grad[side * half : (side + 1) * half])

    weight_blocks(0, range(early))
    sum_early = replica_sum(0)
    next(sum_early, None)
    next(sum_out, None)
    weight_blocks(1, range(early, 3 * blocks))
    next(sum_early, None)
    next(sum_out, None)
    levels = iota((buckets, 2 * seq), 0)
    one_hot = (levels == bucket_ref[...]).astype(F32).astype(BF16)
    high, low = two_parts(sums[...])
    g_table = (matmul_t(one_hot, high) + matmul_t(one_hot, low)).astype(BF16)
    for side in range(2):
        part = g_table[side * (buckets // 2) : (side + 1) * (buckets // 2)]
        store(1, side, tile_rows + half + 16, part)
    part_copy.wait()
    d_n1 = d_n1 + part_in[...].astype(F32)
    values = tok_ref[...].astype(F32)
    factor = rms_factor(values)
    unit = values * factor
    scaled = d_n1 * gain_row(small_all, half, 0)
    gtok_ref[...] = gtok_ref[...] + factor * (
        scaled - unit * jnp.mean(scaled * unit, axis=-1, keepdims=True)
    )
    g_gain_one = jnp.sum(d_n1 * unit, axis=0, keepdims=True)
    for side in range(2):
        pieces = [
            gain[:, side * half + i * 128 : side * half + (i + 1) * 128]
            for gain in (g_gain_one, g_gain_two)
            for i in range(blocks)
        ]
        pieces.append(jnp.zeros((16 - 2 * blocks, 128), F32))
        store(1, side, tile_rows + half, jnp.concatenate(pieces, axis=0).astype(BF16))

    sum_late = replica_sum(1)
    next(sum_late, None)
    next(sum_early, None)
    next(sum_late, None)

    own_block.wait()
    wait_blocks(returned, devices, all_sems.at[0], all_sems.at[1])
    layer = hidden_ref[...]
    router_parts = two_parts(router_ref[...])
    per_step = step // capacity
    for i in range(wide // step):
        spread = (
            (iota((128, step), 1) + i * step) >> (shift + 1) == iota((128, step), 0)
        ).astype(F32).astype(BF16)
        weights = matmul(router_parts[0], spread) + matmul(router_parts[1], spread)
        weights = weights * dispatch_ref[:, i * step : (i + 1) * step].astype(F32)
        block = returned[i * per_step : (i + 1) * per_step].astype(F32)
        block = block.reshape(step, width).astype(BF16)
        for part in two_parts(weights):
            layer = layer + matmul(part, block)
    layer_ref[...] = layer.astype(BF16)
    for _ in range(10):
        for running in (sum_out, sum_early, sum_late):
            next(running, None)

    def load(which, side, start, count):
        span = span_of(which)
        base = side * span
        pieces, at = [], 0
        while at < count:
            chunk_at, inside = divmod(start + at, span)
            size = min(span - inside, count - at)
            spot = (
                chunk_at // (2 * zs * xs),
                (chunk_at // (2 * zs)) % xs,
                (chunk_at // 2) % zs,
                chunk_at % 2,
            )
            pieces.append(sets[which][1][spot + (slice(base + inside, base + inside + size),)])
            at += size
        return pieces[0] if len(pieces) == 1 else jnp.concatenate(pieces, axis=0)

    for side in range(2):
        for block in range(3 * blocks):
            at = (block // blocks) * width + side * half + (block % blocks) * 128
            which, i = (0, block) if block < early else (1, block - early)
            gqkv_ref[:, at : at + 128] = load(which, side, i * half, half)
    for block in range(2 * blocks):
        gout_w_ref[:, block * 128 : (block + 1) * 128] = load(2, 0, block * half, half)
    grouter_ref[...] = sum(load(1, side, tile_rows, half).astype(F32) for side in range(2))
    gsmall_ref[...] = sum(
        load(1, side, tile_rows + half, 16 + buckets // 2).astype(F32) for side in range(2)
    )


def back(sizes, dims, sent, result, dispatch, cotangent, tokens, kept, w_out, bucket_row):
    ys, xs, zs = sizes
    heads, experts, capacity, buckets = dims
    rows, width = tokens.shape
    half, seq, lanes = width // 2, 2 * rows, 128
    count = 2 * ys * xs * zs
    blocks = half // 128
    early = -(-5 * 3 * blocks // 9)
    late_rows = (3 * blocks - early) * half + half + 16 + buckets // 2
    both = [up(length, 16 * count) // count for length in (early * half, late_rows)]
    last = up(half * width // 128, 16 * count) // count
    cuts = [(both[0], 2 * both[0]), (both[1], 2 * both[1]), (0, last)]
    per_core = count // 2
    many = 3 * (4 * (xs + ys) + 2 * zs + 4)
    landing = []
    for _, n in cuts:
        cut = up(n // 2, 16)
        landing += [
            (per_core, 2, n, lanes),
            (ys, xs, zs, 2, n, lanes),
            (per_core, n, lanes),
            (ys, xs, zs, n, lanes),
            (xs + ys - 2, ys, zs, cut, lanes),
            (xs + ys - 2, xs, zs, n - cut, lanes),
            (ys, zs, cut, lanes),
            (xs, zs, n - cut, lanes),
            (zs, n, lanes),
            (zs, n, lanes),
        ]
    shapes = [
        ((rows, width), BF16),
        ((rows, width), F32),
        ((half, 3 * width), BF16),
        ((half, width), BF16),
        ((half, 128), F32),
        ((16 + buckets // 2, 128), F32),
    ]
    return pl.pallas_call(
        functools.partial(back_kernel, sizes, dims, cuts),
        out_shape=[jax.ShapeDtypeStruct(*shape) for shape in shapes],
        in_specs=[VMEM_SPEC] * 16,
        out_specs=[VMEM_SPEC] * len(shapes),
        scratch_shapes=[
            pltpu.VMEM((2, rows, width), BF16),
            pltpu.VMEM((seq, 3 * half), BF16),
            pltpu.VMEM((128, 2 * seq), F32),
            pltpu.VMEM((rows, width), BF16),
            pltpu.VMEM((rows, width), BF16),
            pltpu.VMEM(result.shape, BF16),
            pltpu.SemaphoreType.DMA((many,)),
            pltpu.SemaphoreType.DMA((many,)),
            pltpu.SemaphoreType.DMA((3,)),
        ]
        + [pltpu.VMEM(shape, BF16) for shape in landing],
        compiler_params=pltpu.CompilerParams(
            collective_id=1, has_side_effects=True, vmem_limit_bytes=56 * 2**20
        ),
        cost_estimate=pl.CostEstimate(flops=60 * 10**9, bytes_accessed=2 * 10**8, transcendentals=0),
    )(sent, result, dispatch, cotangent, tokens, *kept, w_out, bucket_row)


def body(
    sizes,
    tokens,
    cotangent,
    attn_gain,
    w_qkv,
    w_out,
    rel_bias,
    buckets,
    ffn_gain,
    w_router,
    w_in,
    w_back,
    choice_ids,
):
    rows, width = tokens.shape
    half = width // 2
    bucket_half, heads = rel_bias.shape
    experts = w_router.shape[1]
    top = choice_ids.shape[1]
    capacity = up(max(2, 5 * rows * top // (4 * experts)) + 1, 8)
    slots = experts * capacity
    seq = 2 * rows
    dims = (heads, experts, capacity, 2 * bucket_half)
    blocks = half // 128

    flat_ids = choice_ids.reshape(-1)
    levels = jnp.arange(experts, dtype=jnp.int32)
    member = (flat_ids[:, None] == levels[None, :]).astype(BF16)
    order = jnp.arange(rows * top, dtype=jnp.int32)
    before = (order[:, None] > order[None, :]).astype(BF16)
    earlier = matmul(before, member)
    rank = jnp.sum(earlier * member.astype(F32), axis=1).astype(jnp.int32)
    slot = (flat_ids * capacity + rank).reshape(rows, top)
    dispatch = jnp.sum(
        (slot[:, :, None] == jnp.arange(slots, dtype=jnp.int32)).astype(BF16), axis=1
    )
    dispatch_two = jnp.broadcast_to(
        dispatch.reshape(rows, experts, 1, capacity), (rows, experts, 2, capacity)
    ).reshape(rows, 2 * slots)

    def swap_all(all_rows):
        blocks = all_rows.reshape(2 * experts, capacity, width)
        got = lax.all_to_all(blocks, ("rep", "shard"), split_axis=0, concat_axis=0, tiled=True)
        return got.reshape(2 * slots, width)

    gains = jnp.concatenate([attn_gain.reshape(blocks, 128), ffn_gain.reshape(blocks, 128)])
    small = jnp.concatenate(
        [
            jnp.pad(w_router, ((0, 0), (0, 128 - experts))),
            jnp.pad(gains, ((0, 16 - 2 * blocks), (0, 0))),
            jnp.pad(rel_bias, ((0, 0), (0, 128 - heads))),
        ]
    )
    nothing = jnp.full((seq,), -1, jnp.int32)
    back_order = buckets[::-1]
    bucket_front = jnp.concatenate([buckets[:1], nothing, back_order[:-1]]).reshape(1, 2 * seq)
    bucket_back = jnp.concatenate([back_order, nothing]).reshape(1, 2 * seq)
    *kept, arrived, grad_rows = front(
        sizes, dims, tokens, small, w_qkv, w_out, bucket_front, dispatch, cotangent
    )
    arrived, grad_rows = (block.reshape(2 * slots, width) for block in (arrived, grad_rows))

    expert_in, expert_back = w_in[0], w_back[0]
    activated, grad_pre, grad_arrived, result, grad_result = expert(
        capacity, arrived, grad_rows, expert_in, expert_back
    )
    sent = swap_all(grad_arrived)
    result = result.reshape(2 * experts, capacity, width)
    grad_back_expert = t_matmul(activated, grad_result)
    grad_in_expert = t_matmul(arrived, grad_pre)

    layer_out, grad_tokens, g_qkv, g_out, g_router, g_small = back(
        sizes, dims, sent, result, dispatch_two, cotangent, tokens, kept, w_out, bucket_back
    )

    return (
        layer_out,
        grad_tokens,
        g_small[:blocks].reshape(half),
        g_qkv.astype(F32),
        g_out.astype(F32),
        g_small[16:, :heads],
        g_small[blocks : 2 * blocks].reshape(half),
        g_router[:, :experts],
        grad_in_expert[None],
        grad_back_expert[None],
    )


SIZES = {64: (4, 4, 2), 4: (2, 1, 1), 8: (2, 2, 1)}


def solution(mesh):
    in_specs = (
        P(("rep", "shard"), None),
        P(("rep", "shard"), None),
        P("shard"),
        P("shard", None),
        P("shard", None),
        P("shard", None),
        P(),
        P("shard"),
        P("shard", None),
        P("rep", None, "shard"),
        P("rep", "shard", None),
        P(("rep", "shard"), None),
    )
    out_specs = (
        P(("rep", "shard"), None),
        P(("rep", "shard"), None),
        P("shard"),
        P("shard", None),
        P("shard", None),
        P("shard", None),
        P("shard"),
        P("shard", None),
        P("rep", None, "shard"),
        P("rep", "shard", None),
    )
    sizes = SIZES[mesh.shape["rep"]]
    return jax.shard_map(
        functools.partial(body, sizes),
        mesh=mesh,
        in_specs=in_specs,
        out_specs=out_specs,
        check_vma=False,
    )
```

```python
import functools

import jax
import jax.numpy as jnp
from jax import lax
from jax.experimental import pallas as pl
from jax.experimental.pallas import tpu as pltpu
from jax.sharding import PartitionSpec as P

EPSILON = 1e-06
MASKED = -1e30
MESH = pl.DeviceIdType.MESH
VMEM_SPEC = pl.BlockSpec(memory_space=pltpu.VMEM)
F32 = jnp.float32
BF16 = jnp.bfloat16


def greet_all(count):
    me = 2 * lax.axis_index("rep") + lax.axis_index("shard")
    barrier = pltpu.get_barrier_semaphore()

    def signal(step, carry):
        to = lax.rem(me + step, count)
        pl.semaphore_signal(
            barrier, inc=1, device_id=(to // 2, lax.rem(to, 2)), device_id_type=MESH
        )
        return carry

    lax.fori_loop(1, count, signal, 0)
    pl.semaphore_wait(barrier, count - 1)


def send_blocks(source_of, target, count, send, recv):
    me = 2 * lax.axis_index("rep") + lax.axis_index("shard")

    def start(step, carry):
        to = lax.rem(me + step, count)
        pltpu.make_async_remote_copy(
            source_of(to),
            target.at[me],
            send,
            recv,
            (to // 2, lax.rem(to, 2)),
            device_id_type=MESH,
        ).start()
        return carry

    lax.fori_loop(1, count, start, 0)


def wait_blocks(target, count, send, recv):
    rep, mine = lax.axis_index("rep"), lax.axis_index("shard")
    most = target.at[pl.ds(0, count - 1)]
    pltpu.make_async_remote_copy(
        most, most, send, recv, (rep, 1 - mine), device_id_type=MESH
    ).wait()


def up(number, step):
    return -(-number // step) * step


def greet(peers):
    barrier = pltpu.get_barrier_semaphore()
    for peer in peers:
        pl.semaphore_signal(barrier, inc=1, device_id=peer, device_id_type=MESH)
    pl.semaphore_wait(barrier, len(peers))


def iota(shape, axis):
    return lax.broadcasted_iota(jnp.int32, shape, axis)


def dot(a, b, contract):
    return lax.dot_general(a, b, (contract, ((), ())), preferred_element_type=F32)


def matmul(a, b):
    return dot(a, b, ((1,), (0,)))


def matmul_t(a, b):
    return dot(a, b, ((1,), (1,)))


def t_matmul(a, b):
    return dot(a, b, ((0,), (0,)))


def two_parts(values):
    high = values.astype(BF16)
    return high, (values - high.astype(F32)).astype(BF16)


def rms_factor(values):
    return lax.rsqrt(jnp.mean(values * values, axis=-1, keepdims=True) + EPSILON)


def gain_row(small_ref, half, first):
    blocks = half // 128
    pieces = [
        small_ref[side, pl.ds(half + first + i, 1), :].astype(F32)
        for side in range(2)
        for i in range(blocks)
    ]
    return jnp.concatenate(pieces, axis=1)


def router_weight(small_ref, half):
    return jnp.concatenate([small_ref[0, :half, :], small_ref[1, :half, :]], axis=0)


def lifted(block, capacity):
    count = block.shape[0]
    shift = capacity.bit_length() - 1
    source, slot = iota((count, count), 1), iota((count, count), 0)
    carrier = (source == ((slot >> shift) << shift) + capacity - 1).astype(F32).astype(BF16)
    carried = matmul(carrier, block)
    lane, slot = iota((count, 128), 1), iota((count, 128), 0)
    mask = ((lane & (capacity - 1)) == (slot & (capacity - 1))) & (lane < 2 * capacity)
    return jnp.sum(jnp.where(mask, carried, 0.0), axis=1, keepdims=True)


def lowered(column, capacity):
    count = column.shape[0]
    shift = capacity.bit_length() - 1
    target, slot = iota((count, count), 0), iota((count, count), 1)
    carrier = (target == ((slot >> shift) << shift) + capacity - 1).astype(F32).astype(BF16)
    lane, slot = iota((count, 128), 1), iota((count, 128), 0) & (capacity - 1)
    high, low = two_parts(column)
    spread = jnp.where(lane == slot, high.astype(F32), 0.0)
    spread = spread + jnp.where(lane == slot + capacity, low.astype(F32), 0.0)
    return matmul(carrier, spread.astype(BF16))


def bucket_mask(bucket_ref, buckets, distance):
    row = bucket_ref[...]
    levels = iota((buckets, row.shape[1]), 0)
    low = jnp.sum((row < levels).astype(F32), axis=1, keepdims=True)
    high = jnp.sum((row <= levels).astype(F32), axis=1, keepdims=True)
    distance = distance.astype(F32)
    inside = (distance >= low) & (distance < high)
    return inside.astype(F32).astype(BF16)


def front_kernel(
    sizes,
    dims,
    tok_ref,
    small_ref,
    wqkv_ref,
    wout_ref,
    bucket_ref,
    dispatch_ref,
    gout_ref,
    n1_ref,
    proj_ref,
    chance_ref,
    mixed_ref,
    w_all,
    small_all,
    hidden_ref,
    n2_ref,
    router_ref,
    arrived_ref,
    grad_rows_ref,
    tok_all,
    bias_rows,
    part_out,
    part_in,
    outgoing,
    outgoing_grads,
    send,
    recv,
    local,
):
    heads, experts, capacity, buckets = dims
    ys, xs, zs = sizes
    rows, width = tok_ref.shape
    half = width // 2
    seq = 2 * rows
    own_heads = heads // 2
    head = width // heads
    slots = experts * capacity
    rep, mine = lax.axis_index("rep"), lax.axis_index("shard")
    other = 1 - mine
    core = lax.rem(rep, 2)
    peer = (rep, other)
    core_peer = (rep + 1 - 2 * core, mine)
    devices = 2 * experts
    me = 2 * rep + mine
    if zs == 2:
        z = lax.rem(rep // 2, 2)
        far_peer = (rep + 2 * (1 - 2 * z), other)
    greet_all(devices)

    def remote(i, source, target, to):
        copy = pltpu.make_async_remote_copy(
            source, target, send.at[i], recv.at[i], to, device_id_type=MESH
        )
        copy.start()
        return copy

    small_copy = remote(0, small_ref, small_all.at[mine], peer)
    near = half // 2 if zs == 1 else up(half // 12, 16)
    fetched = [(peer, 0, near)]
    if zs == 2:
        fetched.append((far_peer, near, half // 2 - near))
    weight_copies = []
    for j, (to, first, count) in enumerate(fetched):
        at = pl.ds(pl.multiple_of(core * (half // 2) + first, 16), count)
        for block in range(3):
            theirs = pl.ds(pl.multiple_of((2 * block + other) * half, 128), half)
            weight_copies.append(
                remote(
                    2 + 3 * j + block,
                    wqkv_ref.at[at, theirs],
                    w_all.at[mine, at, pl.ds(block * half, half)],
                    to,
                )
            )
    tok_copy = remote(1, tok_ref, tok_all.at[mine], peer)
    kept = [
        pltpu.make_async_copy(tok_ref, tok_all.at[mine], local.at[0]),
        pltpu.make_async_copy(small_ref, small_all.at[mine], local.at[1]),
    ]
    for block in range(3):
        ours = pl.ds(pl.multiple_of((2 * block + mine) * half, 128), half)
        kept.append(
            pltpu.make_async_copy(
                wqkv_ref.at[:, ours], w_all.at[mine, :, pl.ds(block * half, half)], local.at[2 + block]
            )
        )
    for copy in kept:
        copy.start()
    for copy in kept:
        copy.wait()
    small_copy.wait()

    table = jnp.concatenate([small_all[0, half + 16 :, :], small_all[1, half + 16 :, :]], axis=0)
    column = iota((buckets, 2 * seq), 1)
    distance = jnp.where(column == 0, 0, 2 * seq - column)
    one_hot = bucket_mask(bucket_ref, buckets, distance)
    bias_rows[...] = t_matmul(table, one_hot)
    gain_one = gain_row(small_all, half, 0)
    gain_two = gain_row(small_all, half, half // 128)
    dispatch = dispatch_ref[...]
    blocks = t_matmul(dispatch, gout_ref[...]).reshape(experts, capacity, width)
    outgoing_grads[...] = blocks.astype(BF16)

    for copy in weight_copies:
        copy.wait()
    got = w_all.at[other, pl.ds(pl.multiple_of(core * (half // 2), 16), half // 2)]
    passed = remote(8, got, got, core_peer)
    send_blocks(
        lambda to: outgoing_grads.at[to // 2], grad_rows_ref, devices, send.at[10], recv.at[10]
    )
    own_block = pltpu.make_async_copy(outgoing_grads.at[rep], grad_rows_ref.at[me], local.at[0])
    own_block.start()
    tok_copy.wait()
    for side in range(2):
        values = tok_all[side].astype(F32)
        n1_ref[side * rows : (side + 1) * rows, :] = (
            values * rms_factor(values) * gain_one
        ).astype(BF16)
    passed.wait()
    normed = n1_ref[...]
    for block in range(3):
        columns = pl.ds(block * half, half)
        total = matmul(normed[:, :half], w_all[0, :, columns])
        total = total + matmul(normed[:, half:], w_all[1, :, columns])
        proj_ref[:, columns] = total.astype(BF16)

    scale = head ** (-0.5)
    causal = iota((seq, seq), 0) >= iota((seq, seq), 1)
    for h in range(own_heads):
        at = h * head
        query = proj_ref[:, at : at + head]
        key = proj_ref[:, half + at : half + at + head]
        value = proj_ref[:, 2 * half + at : 2 * half + at + head]
        row = bias_rows[pl.ds(mine * own_heads + h, 1), :]
        bias = pltpu.roll(
            jnp.broadcast_to(row, (seq, 2 * seq)), 0, 1, stride=1, stride_axis=0
        )[:, :seq]
        scores = jnp.where(causal, matmul_t(query, key) * scale + bias, MASKED)
        raised = jnp.exp(scores - jnp.max(scores, axis=-1, keepdims=True))
        chance = (raised / jnp.sum(raised, axis=-1, keepdims=True)).astype(BF16)
        chance_ref[h] = chance
        mixed_ref[:, at : at + head] = matmul(chance, value).astype(BF16)

    theirs = pl.ds(pl.multiple_of(other * rows, 16), rows)
    ours = pl.ds(pl.multiple_of(mine * rows, 16), rows)
    part_out[...] = matmul(mixed_ref[theirs, :], wout_ref[...]).astype(BF16)
    part_copy = remote(9, part_out, part_in, peer)
    hidden = tok_ref[...].astype(F32) + matmul(mixed_ref[ours, :], wout_ref[...])
    part_copy.wait()
    hidden = hidden + part_in[...].astype(F32)
    hidden_ref[...] = hidden
    normed = (hidden * rms_factor(hidden) * gain_two).astype(BF16)
    n2_ref[...] = normed
    logits = matmul(normed, router_weight(small_all, half))
    logits = jnp.where(iota((rows, 128), 1) < experts, logits, MASKED)
    raised = jnp.exp(logits - jnp.max(logits, axis=-1, keepdims=True))
    router = raised / jnp.sum(raised, axis=-1, keepdims=True)
    router_ref[...] = router

    shift = capacity.bit_length() - 1
    spread = (iota((128, slots), 0) == (iota((128, slots), 1) >> shift)).astype(F32).astype(BF16)
    row_of, slot_of = iota((slots, slots), 0), iota((slots, slots), 1)
    carrier = ((row_of & (capacity - 1)) == capacity - 1) & (
        (row_of >> shift) == (slot_of >> shift)
    )
    place = iota((slots, 128), 0) & (capacity - 1)
    gates = jnp.zeros((slots, 128), F32)
    for i, part in enumerate(two_parts(router)):
        gate = jnp.sum(matmul(part, spread) * dispatch.astype(F32), axis=0, keepdims=True)
        left = jnp.where(carrier, gate, 0.0).astype(BF16)
        right = (place == iota((slots, 128), 1) - i * capacity).astype(F32).astype(BF16)
        gates = gates + matmul(left, right)
    sent = t_matmul(dispatch, normed)
    first = (sent[:, :128] + gates).reshape(experts, capacity, 128)
    outgoing[...] = sent.reshape(experts, capacity, width).astype(BF16)
    outgoing[:, :, :128] = first.astype(BF16)
    send_blocks(lambda to: outgoing.at[to // 2], arrived_ref, devices, send.at[11], recv.at[11])
    own_block.wait()
    own_block = pltpu.make_async_copy(outgoing.at[rep], arrived_ref.at[me], local.at[0])
    own_block.start()
    own_block.wait()
    wait_blocks(grad_rows_ref, devices, send.at[10], recv.at[10])
    wait_blocks(arrived_ref, devices, send.at[11], recv.at[11])


def front(sizes, dims, tokens, small, w_qkv, w_out, bucket_row, dispatch, cotangent):
    rows, width = tokens.shape
    heads, experts, capacity, buckets = dims
    half, seq, slots = width // 2, 2 * rows, experts * capacity
    shapes = [
        ((seq, width), BF16),
        ((seq, 3 * half), BF16),
        ((heads // 2, seq, seq), BF16),
        ((seq, half), BF16),
        ((2, half, 3 * half), BF16),
        ((2,) + small.shape, BF16),
        ((rows, width), F32),
        ((rows, width), BF16),
        ((rows, 128), F32),
        ((2 * experts, capacity, width), BF16),
        ((2 * experts, capacity, width), BF16),
    ]
    return pl.pallas_call(
        functools.partial(front_kernel, sizes, dims),
        out_shape=[jax.ShapeDtypeStruct(*shape) for shape in shapes],
        in_specs=[VMEM_SPEC] * 7,
        out_specs=[VMEM_SPEC] * len(shapes),
        scratch_shapes=[
            pltpu.VMEM((2, rows, width), BF16),
            pltpu.VMEM((128, 2 * seq), F32),
            pltpu.VMEM((rows, width), BF16),
            pltpu.VMEM((rows, width), BF16),
            pltpu.VMEM((experts, capacity, width), BF16),
            pltpu.VMEM((experts, capacity, width), BF16),
            pltpu.SemaphoreType.DMA((12,)),
            pltpu.SemaphoreType.DMA((12,)),
            pltpu.SemaphoreType.DMA((5,)),
        ],
        compiler_params=pltpu.CompilerParams(
            collective_id=0, has_side_effects=True, vmem_limit_bytes=48 * 2**20
        ),
        cost_estimate=pl.CostEstimate(flops=30 * 10**9, bytes_accessed=10**8, transcendentals=10**6),
    )(tokens, small, w_qkv, w_out, bucket_row, dispatch, cotangent)


def expert_kernel(
    capacity,
    rows_ref,
    grads_ref,
    in_ref,
    back_ref,
    active_ref,
    d_pre_ref,
    sent_ref,
    result_ref,
    d_result_ref,
):
    rows = rows_ref[...]
    grads = grads_ref[...]
    gate = lifted(rows[:, :128], capacity)
    d_result_ref[...] = (gate * grads.astype(F32)).astype(BF16)
    hidden = in_ref.shape[1]
    step = min(hidden, 512)
    root = 0.7978845608028654
    sent, result, d_gate = 0.0, 0.0, 0.0
    for at in range(0, hidden, step):
        w_in, w_back = in_ref[:, at : at + step], back_ref[at : at + step, :]
        pre = matmul(rows, w_in)
        d_active = matmul_t(grads, w_back)
        square = pre * pre
        wave = jnp.tanh(root * pre * (1.0 + 0.044715 * square))
        upper = 0.5 * (1.0 + wave)
        slope = upper + 0.5 * pre * (1.0 - wave * wave) * (
            root * (1.0 + 3 * 0.044715 * square)
        )
        active = (pre * upper).astype(BF16)
        d_gate = d_gate + jnp.sum(active.astype(F32) * d_active, axis=1, keepdims=True)
        d_pre = (gate * d_active * slope).astype(BF16)
        active_ref[:, at : at + step] = active
        d_pre_ref[:, at : at + step] = d_pre
        result = result + matmul(active, w_back)
        sent = sent + matmul_t(d_pre, w_in)
    result_ref[...] = result.astype(BF16)
    sent_ref[...] = sent.astype(BF16)
    sent_ref[:, :128] = (sent[:, :128] + lowered(d_gate, capacity)).astype(BF16)


def expert(capacity, rows, grads, w_in, w_back):
    count, width = rows.shape
    hidden = w_in.shape[1]
    step = min(count, max(256, capacity))
    by_rows = [pl.BlockSpec((step, size), lambda i: (i, 0)) for size in (width, hidden)]
    return pl.pallas_call(
        functools.partial(expert_kernel, capacity),
        grid=(count // step,),
        out_shape=[
            jax.ShapeDtypeStruct((count, hidden), BF16),
            jax.ShapeDtypeStruct((count, hidden), BF16),
            jax.ShapeDtypeStruct((count, width), BF16),
            jax.ShapeDtypeStruct((count, width), BF16),
            jax.ShapeDtypeStruct((count, width), BF16),
        ],
        in_specs=[
            by_rows[0],
            by_rows[0],
            pl.BlockSpec(w_in.shape, lambda i: (0, 0)),
            pl.BlockSpec(w_back.shape, lambda i: (0, 0)),
        ],
        out_specs=[by_rows[1], by_rows[1], by_rows[0], by_rows[0], by_rows[0]],
        compiler_params=pltpu.CompilerParams(vmem_limit_bytes=40 * 2**20),
        cost_estimate=pl.CostEstimate(
            flops=8 * count * width * hidden, bytes_accessed=2 * 10**7, transcendentals=count * hidden
        ),
    )(rows, grads, w_in, w_back)


def back_kernel(
    sizes,
    dims,
    both,
    cut,
    sent_ref,
    result_ref,
    dispatch_ref,
    gout_ref,
    tok_ref,
    n1_ref,
    proj_ref,
    chance_ref,
    mixed_ref,
    w_all,
    small_all,
    hidden_ref,
    n2_ref,
    router_ref,
    wout_ref,
    bucket_ref,
    layer_ref,
    gtok_ref,
    gqkv_ref,
    gout_w_ref,
    grouter_ref,
    gsmall_ref,
    att_all,
    dqkv,
    sums,
    part_out,
    part_in,
    comm,
    total_ref,
    chip_in,
    chip,
    row_in,
    column_in,
    row_sum,
    column_sum,
    deep,
    deep_in,
    returned,
    send,
    recv,
    all_sems,
):
    heads, experts, capacity, buckets = dims
    ys, xs, zs = sizes
    rows, width = tok_ref.shape
    half = width // 2
    seq = 2 * rows
    own_heads = heads // 2
    head = width // heads
    blocks = half // 128
    chunk_rows = comm.shape[2]
    rep, mine = lax.axis_index("rep"), lax.axis_index("shard")
    other = 1 - mine
    core = lax.rem(rep, 2)
    z = lax.rem(rep // 2, zs)
    x = lax.rem(rep // (2 * zs), xs)
    y = rep // (2 * zs * xs)

    def place(y_at, x_at, z_at, core_at):
        return ((y_at * xs + x_at) * zs + z_at) * 2 + core_at

    xp = [lax.rem(x + step, xs) for step in range(1, xs)]
    yp = [lax.rem(y + step, ys) for step in range(1, ys)]
    zp = [lax.rem(z + step, zs) for step in range(1, zs)]
    core_peer = (place(y, x, z, 1 - core), mine)
    x_peers = [(place(y, at, z, core), mine) for at in xp]
    y_peers = [(place(at, x, z, core), mine) for at in yp]
    z_peers = [(place(y, x, at, core), mine) for at in zp]
    peer = (rep, other)
    devices = 2 * experts
    me = 2 * rep + mine
    greet_all(devices)
    number = [0]

    def send_to(source, target, to):
        i = number[0]
        number[0] += 1
        copy = pltpu.make_async_remote_copy(
            source, target, send.at[i], recv.at[i], to, device_id_type=MESH
        )
        copy.start()
        return copy

    def finish(copies):
        for copy in copies:
            copy.wait()

    wide = sent_ref.shape[0]
    step = min(wide, max(256, capacity))
    d_gate = jnp.concatenate(
        [lifted(sent_ref[at : at + step, :128], capacity) for at in range(0, wide, step)], axis=0
    )
    shift = capacity.bit_length() - 1
    own_lane = (iota((wide, 128), 0) >> (shift + 1)) == iota((wide, 128), 1)
    d_gate = jnp.where(own_lane, d_gate, 0.0)
    dispatch = dispatch_ref[...]
    high, low = two_parts(d_gate)
    d_router = matmul(dispatch, high) + matmul(dispatch, low)
    router = router_ref[...]
    d_logits = router * (d_router - jnp.sum(router * d_router, axis=-1, keepdims=True))
    d_logits = d_logits.astype(BF16)
    d_n2 = matmul(dispatch, sent_ref[...]) + matmul_t(d_logits, router_weight(small_all, half))
    hidden = hidden_ref[...]
    factor = rms_factor(hidden)
    unit = hidden * factor
    scaled = d_n2 * gain_row(small_all, half, blocks)
    d_hidden = gout_ref[...].astype(F32) + factor * (
        scaled - unit * jnp.mean(scaled * unit, axis=-1, keepdims=True)
    )
    att_all[mine] = d_hidden.astype(BF16)
    shared = send_to(att_all.at[mine], att_all.at[mine], peer)
    send_blocks(lambda to: result_ref.at[to], returned, devices, all_sems.at[0], all_sems.at[1])
    own_block = pltpu.make_async_copy(result_ref.at[me], returned.at[me], all_sems.at[2])
    own_block.start()
    gtok_ref[...] = d_hidden
    g_gain_two = jnp.sum(d_n2 * unit, axis=0, keepdims=True)
    g_router = t_matmul(n2_ref[...], d_logits)

    def store(part, first, block):
        base = part * both
        span = both if part < 2 else chunk_rows - 2 * both
        at = 0
        while at < block.shape[0]:
            chunk_at, inside = divmod(first + at, span)
            count = min(span - inside, block.shape[0] - at)
            comm[chunk_at // 2, chunk_at % 2, base + inside : base + inside + count, :] = block[
                at : at + count
            ]
            at += count

    tile_rows = 3 * blocks * half
    for side in range(2):
        store(side, tile_rows, g_router[side * half : (side + 1) * half].astype(BF16))
    shared.wait()

    d_att = [att_all[0], att_all[1]]
    for block in range(2 * blocks):
        columns = slice(block * 128, (block + 1) * 128)
        grad = t_matmul(mixed_ref[:rows, :], d_att[0][:, columns])
        grad = grad + t_matmul(mixed_ref[rows:, :], d_att[1][:, columns])
        store(2, block * half, grad.astype(BF16))
    d_mixed = jnp.concatenate(
        [matmul_t(part, wout_ref[...]).astype(BF16) for part in d_att], axis=0
    )
    scale = head ** (-0.5)
    flip = (iota((seq, seq), 0) + iota((seq, seq), 1) == seq - 1).astype(F32).astype(BF16)
    for h in range(own_heads):
        at = h * head
        query = proj_ref[:, at : at + head]
        key = proj_ref[:, half + at : half + at + head]
        value = proj_ref[:, 2 * half + at : 2 * half + at + head]
        d_o = d_mixed[:, at : at + head]
        chance = chance_ref[h]
        d_chance = matmul_t(d_o, value)
        wide_chance = chance.astype(F32)
        inner = jnp.sum(wide_chance * d_chance, axis=-1, keepdims=True)
        d_scores = (wide_chance * (d_chance - inner)).astype(BF16)
        dqkv[:, at : at + head] = (matmul(d_scores, key) * scale).astype(BF16)
        dqkv[:, half + at : half + at + head] = (t_matmul(d_scores, query) * scale).astype(BF16)
        dqkv[:, 2 * half + at : 2 * half + at + head] = t_matmul(chance, d_o).astype(BF16)
        flipped = matmul(flip, d_scores)
        flipped = jnp.concatenate([flipped, jnp.zeros((seq, seq), F32)], axis=1)
        lined = pltpu.roll(flipped, 0, 1, stride=1, stride_axis=0)
        sums[pl.ds(mine * own_heads + h, 1), :] = jnp.sum(lined, axis=0, keepdims=True)
        sums[pl.ds(other * own_heads + h, 1), :] = jnp.zeros((1, 2 * seq), F32)

    theirs = pl.ds(pl.multiple_of(other * rows, 16), rows)
    ours = pl.ds(pl.multiple_of(mine * rows, 16), rows)

    def d_normed(which):
        return jnp.concatenate(
            [matmul_t(dqkv[which, :], w_all[side]) for side in range(2)], axis=1
        )

    part_out[...] = d_normed(theirs).astype(BF16)
    part_copy = send_to(part_out, part_in, peer)
    d_n1 = d_normed(ours)
    for block in range(3 * blocks):
        grad = t_matmul(n1_ref[...], dqkv[:, block * 128 : (block + 1) * 128]).astype(BF16)
        for side in range(2):
            store(side, block * half, grad[side * half : (side + 1) * half])
    one_hot = bucket_mask(bucket_ref, buckets, seq - 1 - iota((buckets, 2 * seq), 1))
    high, low = two_parts(sums[...])
    g_table = (matmul_t(one_hot, high) + matmul_t(one_hot, low)).astype(BF16)
    for side in range(2):
        part = g_table[side * (buckets // 2) : (side + 1) * (buckets // 2)]
        store(side, tile_rows + half + 16, part)
    part_copy.wait()
    d_n1 = d_n1 + part_in[...].astype(F32)
    values = tok_ref[...].astype(F32)
    factor = rms_factor(values)
    unit = values * factor
    scaled = d_n1 * gain_row(small_all, half, 0)
    gtok_ref[...] = gtok_ref[...] + factor * (
        scaled - unit * jnp.mean(scaled * unit, axis=-1, keepdims=True)
    )
    g_gain_one = jnp.sum(d_n1 * unit, axis=0, keepdims=True)
    for side in range(2):
        pieces = [
            gain[:, side * half + i * 128 : side * half + (i + 1) * 128]
            for gain in (g_gain_one, g_gain_two)
            for i in range(blocks)
        ]
        pieces.append(jnp.zeros((16 - 2 * blocks, 128), F32))
        store(side, tile_rows + half, jnp.concatenate(pieces, axis=0).astype(BF16))

    first, second = pl.ds(0, cut), pl.ds(cut, chunk_rows - cut)
    chip_copy = send_to(comm.at[:, 1 - core], chip_in, core_peer)
    finish([chip_copy])

    def add_chip(i, carry):
        total = comm[i, core].astype(F32) + chip_in[i].astype(F32)
        chip[i // (xs * zs), lax.rem(i // zs, xs), lax.rem(i, zs)] = total.astype(BF16)
        return carry

    lax.fori_loop(0, ys * xs * zs, add_chip, 0)
    copies = [
        send_to(chip.at[:, at, :, first], row_in.at[i], to)
        for i, (at, to) in enumerate(zip(xp, x_peers))
    ]
    copies += [
        send_to(chip.at[at, :, :, second], column_in.at[i], to)
        for i, (at, to) in enumerate(zip(yp, y_peers))
    ]

    own_block.wait()
    wait_blocks(returned, devices, all_sems.at[0], all_sems.at[1])
    layer = hidden_ref[...]
    router_parts = two_parts(router_ref[...])
    per_step = step // capacity
    for i in range(wide // step):
        spread = (
            (iota((128, step), 1) + i * step) >> (shift + 1) == iota((128, step), 0)
        ).astype(F32).astype(BF16)
        weights = matmul(router_parts[0], spread) + matmul(router_parts[1], spread)
        weights = weights * dispatch_ref[:, i * step : (i + 1) * step].astype(F32)
        block = returned[i * per_step : (i + 1) * per_step].astype(F32)
        block = block.reshape(step, width).astype(BF16)
        for part in two_parts(weights):
            layer = layer + matmul(part, block)
    layer_ref[...] = layer.astype(BF16)
    finish(copies)

    def add_row(i, carry):
        for k in range(zs):
            total = chip[i, x, k, first].astype(F32)
            for j in range(xs - 1):
                total = total + row_in[j, i, k].astype(F32)
            row_sum[i, k] = total.astype(BF16)
        return carry

    def add_column(i, carry):
        for k in range(zs):
            total = chip[y, i, k, second].astype(F32)
            for j in range(ys - 1):
                total = total + column_in[j, i, k].astype(F32)
            column_sum[i, k] = total.astype(BF16)
        return carry

    lax.fori_loop(0, ys, add_row, 0)
    lax.fori_loop(0, xs, add_column, 0)
    copies = [
        send_to(row_sum.at[at], row_in.at[xs - 1 + i, 0], to)
        for i, (at, to) in enumerate(zip(yp, y_peers))
    ]
    copies += [
        send_to(column_sum.at[at], column_in.at[ys - 1 + i, 0], to)
        for i, (at, to) in enumerate(zip(xp, x_peers))
    ]
    finish(copies)
    for k in range(zs):
        total = row_sum[y, k].astype(F32)
        for i in range(ys - 1):
            total = total + row_in[xs - 1 + i, 0, k].astype(F32)
        deep[k, first] = total.astype(BF16)
        total = column_sum[x, k].astype(F32)
        for i in range(xs - 1):
            total = total + column_in[ys - 1 + i, 0, k].astype(F32)
        deep[k, second] = total.astype(BF16)
    finish([send_to(deep.at[at], deep_in.at[i], to) for i, (at, to) in enumerate(zip(zp, z_peers))])
    total = deep[z].astype(F32)
    for i in range(zs - 1):
        total = total + deep_in[i].astype(F32)
    done = total.astype(BF16)
    mine_at = pl.ds(pl.multiple_of(mine * both, 16), both)
    other_at = pl.ds(pl.multiple_of(other * both, 16), both)
    deep_in[zs - 1] = done
    out = total_ref.at[y, x, z, core]
    copies = [send_to(deep_in.at[zs - 1, other_at], out.at[mine_at], peer)]
    out[mine_at] = deep_in[zs - 1, mine_at]
    out[2 * both :] = done[2 * both :]
    finish(copies)
    finish([send_to(out, out, to) for to in z_peers])
    firsts = total_ref.at[y, x, :, core, first]
    seconds = total_ref.at[y, x, :, core, second]
    copies = [send_to(firsts, firsts, to) for to in y_peers]
    copies += [send_to(seconds, seconds, to) for to in x_peers]
    finish(copies)
    firsts = total_ref.at[:, x, :, core, first]
    seconds = total_ref.at[y, :, :, core, second]
    copies = [send_to(firsts, firsts, to) for to in x_peers]
    copies += [send_to(seconds, seconds, to) for to in y_peers]
    finish(copies)
    whole = total_ref.at[:, :, :, core]
    finish([send_to(whole, whole, core_peer)])

    def load(part, start, count):
        base = part * both
        span = both if part < 2 else chunk_rows - 2 * both
        pieces, at = [], 0
        while at < count:
            chunk_at, inside = divmod(start + at, span)
            size = min(span - inside, count - at)
            spot = (
                chunk_at // (2 * zs * xs),
                (chunk_at // (2 * zs)) % xs,
                (chunk_at // 2) % zs,
                chunk_at % 2,
            )
            pieces.append(total_ref[spot + (slice(base + inside, base + inside + size),)])
            at += size
        return pieces[0] if len(pieces) == 1 else jnp.concatenate(pieces, axis=0)

    for side in range(2):
        for block in range(3 * blocks):
            at = (block // blocks) * width + side * half + (block % blocks) * 128
            gqkv_ref[:, at : at + 128] = load(side, block * half, half)
    for block in range(2 * blocks):
        gout_w_ref[:, block * 128 : (block + 1) * 128] = load(2, block * half, half)
    g_router = sum(load(side, tile_rows, half).astype(F32) for side in range(2))
    grouter_ref[...] = g_router.T[:experts]
    gsmall_ref[...] = sum(
        load(side, tile_rows + half, 16 + buckets // 2).astype(F32) for side in range(2)
    )


def back(sizes, dims, sent, result, dispatch, cotangent, tokens, kept, w_out, bucket_row):
    ys, xs, zs = sizes
    heads, experts, capacity, buckets = dims
    rows, width = tokens.shape
    half, seq, lanes = width // 2, 2 * rows, 128
    count = 2 * ys * xs * zs
    both = up(3 * half * half // 128 + half + 16 + buckets // 2, 16 * count) // count
    chunk_rows = 2 * both + up(half * width // 128, 16 * count) // count
    cut = up(chunk_rows // 2, 16)
    per_core = count // 2
    many = 4 * (xs + ys) + 2 * zs + 4
    shapes = [
        ((rows, width), BF16),
        ((rows, width), F32),
        ((half, 3 * width), BF16),
        ((half, width), BF16),
        ((experts, half), F32),
        ((16 + buckets // 2, 128), F32),
    ]
    return pl.pallas_call(
        functools.partial(back_kernel, sizes, dims, both, cut),
        out_shape=[jax.ShapeDtypeStruct(*shape) for shape in shapes],
        in_specs=[VMEM_SPEC] * 16,
        out_specs=[VMEM_SPEC] * len(shapes),
        scratch_shapes=[
            pltpu.VMEM((2, rows, width), BF16),
            pltpu.VMEM((seq, 3 * half), BF16),
            pltpu.VMEM((128, 2 * seq), F32),
            pltpu.VMEM((rows, width), BF16),
            pltpu.VMEM((rows, width), BF16),
            pltpu.VMEM((per_core, 2, chunk_rows, lanes), BF16),
            pltpu.VMEM((ys, xs, zs, 2, chunk_rows, lanes), BF16),
            pltpu.VMEM((per_core, chunk_rows, lanes), BF16),
            pltpu.VMEM((ys, xs, zs, chunk_rows, lanes), BF16),
            pltpu.VMEM((xs + ys - 2, ys, zs, cut, lanes), BF16),
            pltpu.VMEM((xs + ys - 2, xs, zs, chunk_rows - cut, lanes), BF16),
            pltpu.VMEM((ys, zs, cut, lanes), BF16),
            pltpu.VMEM((xs, zs, chunk_rows - cut, lanes), BF16),
            pltpu.VMEM((zs, chunk_rows, lanes), BF16),
            pltpu.VMEM((zs, chunk_rows, lanes), BF16),
            pltpu.VMEM(result.shape, BF16),
            pltpu.SemaphoreType.DMA((many,)),
            pltpu.SemaphoreType.DMA((many,)),
            pltpu.SemaphoreType.DMA((3,)),
        ],
        compiler_params=pltpu.CompilerParams(
            collective_id=1, has_side_effects=True, vmem_limit_bytes=56 * 2**20
        ),
        cost_estimate=pl.CostEstimate(flops=60 * 10**9, bytes_accessed=2 * 10**8, transcendentals=0),
    )(sent, result, dispatch, cotangent, tokens, *kept, w_out, bucket_row)


def body(
    sizes,
    tokens,
    cotangent,
    attn_gain,
    w_qkv,
    w_out,
    rel_bias,
    buckets,
    ffn_gain,
    w_router,
    w_in,
    w_back,
    choice_ids,
):
    rows, width = tokens.shape
    half = width // 2
    bucket_half, heads = rel_bias.shape
    experts = w_router.shape[1]
    top = choice_ids.shape[1]
    capacity = up(max(2, 5 * rows * top // (4 * experts)) + 1, 8)
    slots = experts * capacity
    seq = 2 * rows
    dims = (heads, experts, capacity, 2 * bucket_half)
    blocks = half // 128

    flat_ids = choice_ids.reshape(-1)
    levels = jnp.arange(experts, dtype=jnp.int32)
    member = (flat_ids[:, None] == levels[None, :]).astype(BF16)
    order = jnp.arange(rows * top, dtype=jnp.int32)
    before = (order[:, None] > order[None, :]).astype(BF16)
    earlier = matmul(before, member)
    rank = jnp.sum(earlier * member.astype(F32), axis=1).astype(jnp.int32)
    slot = (flat_ids * capacity + rank).reshape(rows, top)
    dispatch = jnp.sum(
        (slot[:, :, None] == jnp.arange(slots, dtype=jnp.int32)).astype(BF16), axis=1
    )
    dispatch_two = jnp.broadcast_to(
        dispatch.reshape(rows, experts, 1, capacity), (rows, experts, 2, capacity)
    ).reshape(rows, 2 * slots)

    def swap_all(all_rows):
        blocks = all_rows.reshape(2 * experts, capacity, width)
        got = lax.all_to_all(blocks, ("rep", "shard"), split_axis=0, concat_axis=0, tiled=True)
        return got.reshape(2 * slots, width)

    gains = jnp.concatenate([attn_gain.reshape(blocks, 128), ffn_gain.reshape(blocks, 128)])
    small = jnp.concatenate(
        [
            jnp.pad(w_router, ((0, 0), (0, 128 - experts))),
            jnp.pad(gains, ((0, 16 - 2 * blocks), (0, 0))),
            jnp.pad(rel_bias, ((0, 0), (0, 128 - heads))),
        ]
    )
    bucket_row = buckets.reshape(1, seq)
    *kept, arrived, grad_rows = front(
        sizes, dims, tokens, small, w_qkv, w_out, bucket_row, dispatch, cotangent
    )
    arrived, grad_rows = (block.reshape(2 * slots, width) for block in (arrived, grad_rows))

    expert_in, expert_back = w_in[0], w_back[0]
    activated, grad_pre, grad_arrived, result, grad_result = expert(
        capacity, arrived, grad_rows, expert_in, expert_back
    )
    sent = swap_all(grad_arrived)
    result = result.reshape(2 * experts, capacity, width)
    grad_back_expert = t_matmul(activated, grad_result)
    grad_in_expert = t_matmul(arrived, grad_pre)

    layer_out, grad_tokens, g_qkv, g_out, g_router, g_small = back(
        sizes, dims, sent, result, dispatch_two, cotangent, tokens, kept, w_out, bucket_row
    )

    return (
        layer_out,
        grad_tokens,
        g_small[:blocks].reshape(half),
        g_qkv.astype(F32),
        g_out.astype(F32),
        g_small[16:, :heads],
        g_small[blocks : 2 * blocks].reshape(half),
        g_router.T,
        grad_in_expert[None],
        grad_back_expert[None],
    )


SIZES = {64: (4, 4, 2), 4: (2, 1, 1), 8: (2, 2, 1)}


def solution(mesh):
    in_specs = (
        P(("rep", "shard"), None),
        P(("rep", "shard"), None),
        P("shard"),
        P("shard", None),
        P("shard", None),
        P("shard", None),
        P(),
        P("shard"),
        P("shard", None),
        P("rep", None, "shard"),
        P("rep", "shard", None),
        P(("rep", "shard"), None),
    )
    out_specs = (
        P(("rep", "shard"), None),
        P(("rep", "shard"), None),
        P("shard"),
        P("shard", None),
        P("shard", None),
        P("shard", None),
        P("shard"),
        P("shard", None),
        P("rep", None, "shard"),
        P("rep", "shard", None),
    )
    sizes = SIZES[mesh.shape["rep"]]
    return jax.shard_map(
        functools.partial(body, sizes),
        mesh=mesh,
        in_specs=in_specs,
        out_specs=out_specs,
        check_vma=False,
    )
```

```python
import functools

import jax
import jax.numpy as jnp
from jax import lax
from jax.experimental import pallas as pl
from jax.experimental.pallas import tpu as pltpu
from jax.sharding import PartitionSpec as P

EPSILON = 1e-06
MASKED = -1e30
MESH = pl.DeviceIdType.MESH
VMEM_SPEC = pl.BlockSpec(memory_space=pltpu.VMEM)
F32 = jnp.float32
BF16 = jnp.bfloat16


def greet_all(count):
    me = 2 * lax.axis_index("rep") + lax.axis_index("shard")
    barrier = pltpu.get_barrier_semaphore()

    def signal(step, carry):
        to = lax.rem(me + step, count)
        pl.semaphore_signal(
            barrier, inc=1, device_id=(to // 2, lax.rem(to, 2)), device_id_type=MESH
        )
        return carry

    lax.fori_loop(1, count, signal, 0)
    pl.semaphore_wait(barrier, count - 1)


def send_blocks(source_of, target, count, send, recv):
    me = 2 * lax.axis_index("rep") + lax.axis_index("shard")

    def start(step, carry):
        to = lax.rem(me + 37 * step, count)
        pltpu.make_async_remote_copy(
            source_of(to),
            target.at[me],
            send,
            recv,
            (to // 2, lax.rem(to, 2)),
            device_id_type=MESH,
        ).start()
        return carry

    lax.fori_loop(1, count, start, 0)


def wait_blocks(target, count, send, recv):
    rep, mine = lax.axis_index("rep"), lax.axis_index("shard")
    most = target.at[pl.ds(0, count - 1)]
    pltpu.make_async_remote_copy(
        most, most, send, recv, (rep, 1 - mine), device_id_type=MESH
    ).wait()


def up(number, step):
    return -(-number // step) * step


def greet(peers):
    barrier = pltpu.get_barrier_semaphore()
    for peer in peers:
        pl.semaphore_signal(barrier, inc=1, device_id=peer, device_id_type=MESH)
    pl.semaphore_wait(barrier, len(peers))


def iota(shape, axis):
    return lax.broadcasted_iota(jnp.int32, shape, axis)


def dot(a, b, contract):
    return lax.dot_general(a, b, (contract, ((), ())), preferred_element_type=F32)


def matmul(a, b):
    return dot(a, b, ((1,), (0,)))


def matmul_t(a, b):
    return dot(a, b, ((1,), (1,)))


def t_matmul(a, b):
    return dot(a, b, ((0,), (0,)))


def two_parts(values):
    high = values.astype(BF16)
    return high, (values - high.astype(F32)).astype(BF16)


def rms_factor(values):
    return lax.rsqrt(jnp.mean(values * values, axis=-1, keepdims=True) + EPSILON)


def gain_row(small_ref, half, first):
    blocks = half // 128
    pieces = [
        small_ref[side, pl.ds(half + first + i, 1), :].astype(F32)
        for side in range(2)
        for i in range(blocks)
    ]
    return jnp.concatenate(pieces, axis=1)


def router_weight(small_ref, half):
    return jnp.concatenate([small_ref[0, :half, :], small_ref[1, :half, :]], axis=0)


def lifted(block, capacity):
    count = block.shape[0]
    shift = capacity.bit_length() - 1
    source, slot = iota((count, count), 1), iota((count, count), 0)
    carrier = (source == ((slot >> shift) << shift) + capacity - 1).astype(F32).astype(BF16)
    carried = matmul(carrier, block)
    lane, slot = iota((count, 128), 1), iota((count, 128), 0)
    mask = ((lane & (capacity - 1)) == (slot & (capacity - 1))) & (lane < 2 * capacity)
    return jnp.sum(jnp.where(mask, carried, 0.0), axis=1, keepdims=True)


def lowered(column, capacity):
    count = column.shape[0]
    shift = capacity.bit_length() - 1
    target, slot = iota((count, count), 0), iota((count, count), 1)
    carrier = (target == ((slot >> shift) << shift) + capacity - 1).astype(F32).astype(BF16)
    lane, slot = iota((count, 128), 1), iota((count, 128), 0) & (capacity - 1)
    high, low = two_parts(column)
    spread = jnp.where(lane == slot, high.astype(F32), 0.0)
    spread = spread + jnp.where(lane == slot + capacity, low.astype(F32), 0.0)
    return matmul(carrier, spread.astype(BF16))


def bucket_mask(bucket_ref, buckets, distance):
    row = bucket_ref[...]
    levels = iota((buckets, row.shape[1]), 0)
    low = jnp.sum((row < levels).astype(F32), axis=1, keepdims=True)
    high = jnp.sum((row <= levels).astype(F32), axis=1, keepdims=True)
    distance = distance.astype(F32)
    inside = (distance >= low) & (distance < high)
    return inside.astype(F32).astype(BF16)


def front_kernel(
    sizes,
    dims,
    tok_ref,
    small_ref,
    wqkv_ref,
    wout_ref,
    bucket_ref,
    dispatch_ref,
    gout_ref,
    n1_ref,
    proj_ref,
    chance_ref,
    mixed_ref,
    w_all,
    small_all,
    hidden_ref,
    n2_ref,
    router_ref,
    arrived_ref,
    grad_rows_ref,
    tok_all,
    bias_rows,
    part_out,
    part_in,
    outgoing,
    outgoing_grads,
    send,
    recv,
    local,
):
    heads, experts, capacity, buckets = dims
    ys, xs, zs = sizes
    rows, width = tok_ref.shape
    half = width // 2
    seq = 2 * rows
    own_heads = heads // 2
    head = width // heads
    slots = experts * capacity
    rep, mine = lax.axis_index("rep"), lax.axis_index("shard")
    other = 1 - mine
    core = lax.rem(rep, 2)
    peer = (rep, other)
    core_peer = (rep + 1 - 2 * core, mine)
    devices = 2 * experts
    me = 2 * rep + mine
    if zs == 2:
        z = lax.rem(rep // 2, 2)
        far_peer = (rep + 2 * (1 - 2 * z), other)
    greet_all(devices)

    def remote(i, source, target, to):
        copy = pltpu.make_async_remote_copy(
            source, target, send.at[i], recv.at[i], to, device_id_type=MESH
        )
        copy.start()
        return copy

    small_copy = remote(0, small_ref, small_all.at[mine], peer)
    near = half // 2 if zs == 1 else up(half // 12, 16)
    fetched = [(peer, 0, near)]
    if zs == 2:
        fetched.append((far_peer, near, half // 2 - near))
    weight_copies = []
    for j, (to, first, count) in enumerate(fetched):
        at = pl.ds(pl.multiple_of(core * (half // 2) + first, 16), count)
        for block in range(3):
            theirs = pl.ds(pl.multiple_of((2 * block + other) * half, 128), half)
            weight_copies.append(
                remote(
                    2 + 3 * j + block,
                    wqkv_ref.at[at, theirs],
                    w_all.at[mine, at, pl.ds(block * half, half)],
                    to,
                )
            )
    tok_copy = remote(1, tok_ref, tok_all.at[mine], peer)
    kept = [
        pltpu.make_async_copy(tok_ref, tok_all.at[mine], local.at[0]),
        pltpu.make_async_copy(small_ref, small_all.at[mine], local.at[1]),
    ]
    for block in range(3):
        ours = pl.ds(pl.multiple_of((2 * block + mine) * half, 128), half)
        kept.append(
            pltpu.make_async_copy(
                wqkv_ref.at[:, ours], w_all.at[mine, :, pl.ds(block * half, half)], local.at[2 + block]
            )
        )
    for copy in kept:
        copy.start()
    for copy in kept:
        copy.wait()
    small_copy.wait()

    table = jnp.concatenate([small_all[0, half + 16 :, :], small_all[1, half + 16 :, :]], axis=0)
    column = iota((buckets, 2 * seq), 1)
    distance = jnp.where(column == 0, 0, 2 * seq - column)
    one_hot = bucket_mask(bucket_ref, buckets, distance)
    bias_rows[...] = t_matmul(table, one_hot)
    gain_one = gain_row(small_all, half, 0)
    gain_two = gain_row(small_all, half, half // 128)
    dispatch = dispatch_ref[...]
    blocks = t_matmul(dispatch, gout_ref[...]).reshape(experts, capacity, width)
    outgoing_grads[...] = blocks.astype(BF16)

    for copy in weight_copies:
        copy.wait()
    got = w_all.at[other, pl.ds(pl.multiple_of(core * (half // 2), 16), half // 2)]
    passed = remote(8, got, got, core_peer)
    send_blocks(
        lambda to: outgoing_grads.at[to // 2], grad_rows_ref, devices, send.at[10], recv.at[10]
    )
    own_block = pltpu.make_async_copy(outgoing_grads.at[rep], grad_rows_ref.at[me], local.at[0])
    own_block.start()
    tok_copy.wait()
    for side in range(2):
        values = tok_all[side].astype(F32)
        n1_ref[side * rows : (side + 1) * rows, :] = (
            values * rms_factor(values) * gain_one
        ).astype(BF16)
    passed.wait()
    normed = n1_ref[...]
    for block in range(3):
        columns = pl.ds(block * half, half)
        total = matmul(normed[:, :half], w_all[0, :, columns])
        total = total + matmul(normed[:, half:], w_all[1, :, columns])
        proj_ref[:, columns] = total.astype(BF16)

    scale = head ** (-0.5)
    causal = iota((seq, seq), 0) >= iota((seq, seq), 1)
    for h in range(own_heads):
        at = h * head
        query = proj_ref[:, at : at + head]
        key = proj_ref[:, half + at : half + at + head]
        value = proj_ref[:, 2 * half + at : 2 * half + at + head]
        row = bias_rows[pl.ds(mine * own_heads + h, 1), :]
        bias = pltpu.roll(
            jnp.broadcast_to(row, (seq, 2 * seq)), 0, 1, stride=1, stride_axis=0
        )[:, :seq]
        scores = jnp.where(causal, matmul_t(query, key) * scale + bias, MASKED)
        raised = jnp.exp(scores - jnp.max(scores, axis=-1, keepdims=True))
        chance = (raised / jnp.sum(raised, axis=-1, keepdims=True)).astype(BF16)
        chance_ref[h] = chance
        mixed_ref[:, at : at + head] = matmul(chance, value).astype(BF16)

    theirs = pl.ds(pl.multiple_of(other * rows, 16), rows)
    ours = pl.ds(pl.multiple_of(mine * rows, 16), rows)
    part_out[...] = matmul(mixed_ref[theirs, :], wout_ref[...]).astype(BF16)
    part_copy = remote(9, part_out, part_in, peer)
    hidden = tok_ref[...].astype(F32) + matmul(mixed_ref[ours, :], wout_ref[...])
    part_copy.wait()
    hidden = hidden + part_in[...].astype(F32)
    hidden_ref[...] = hidden
    normed = (hidden * rms_factor(hidden) * gain_two).astype(BF16)
    n2_ref[...] = normed
    logits = matmul(normed, router_weight(small_all, half))
    logits = jnp.where(iota((rows, 128), 1) < experts, logits, MASKED)
    raised = jnp.exp(logits - jnp.max(logits, axis=-1, keepdims=True))
    router = raised / jnp.sum(raised, axis=-1, keepdims=True)
    router_ref[...] = router

    shift = capacity.bit_length() - 1
    spread = (iota((128, slots), 0) == (iota((128, slots), 1) >> shift)).astype(F32).astype(BF16)
    row_of, slot_of = iota((slots, slots), 0), iota((slots, slots), 1)
    carrier = ((row_of & (capacity - 1)) == capacity - 1) & (
        (row_of >> shift) == (slot_of >> shift)
    )
    place = iota((slots, 128), 0) & (capacity - 1)
    gates = jnp.zeros((slots, 128), F32)
    for i, part in enumerate(two_parts(router)):
        gate = jnp.sum(matmul(part, spread) * dispatch.astype(F32), axis=0, keepdims=True)
        left = jnp.where(carrier, gate, 0.0).astype(BF16)
        right = (place == iota((slots, 128), 1) - i * capacity).astype(F32).astype(BF16)
        gates = gates + matmul(left, right)
    sent = t_matmul(dispatch, normed)
    first = (sent[:, :128] + gates).reshape(experts, capacity, 128)
    outgoing[...] = sent.reshape(experts, capacity, width).astype(BF16)
    outgoing[:, :, :128] = first.astype(BF16)
    send_blocks(lambda to: outgoing.at[to // 2], arrived_ref, devices, send.at[11], recv.at[11])
    own_block.wait()
    own_block = pltpu.make_async_copy(outgoing.at[rep], arrived_ref.at[me], local.at[0])
    own_block.start()
    own_block.wait()
    wait_blocks(grad_rows_ref, devices, send.at[10], recv.at[10])
    wait_blocks(arrived_ref, devices, send.at[11], recv.at[11])


def front(sizes, dims, tokens, small, w_qkv, w_out, bucket_row, dispatch, cotangent):
    rows, width = tokens.shape
    heads, experts, capacity, buckets = dims
    half, seq, slots = width // 2, 2 * rows, experts * capacity
    shapes = [
        ((seq, width), BF16),
        ((seq, 3 * half), BF16),
        ((heads // 2, seq, seq), BF16),
        ((seq, half), BF16),
        ((2, half, 3 * half), BF16),
        ((2,) + small.shape, BF16),
        ((rows, width), F32),
        ((rows, width), BF16),
        ((rows, 128), F32),
        ((2 * experts, capacity, width), BF16),
        ((2 * experts, capacity, width), BF16),
    ]
    return pl.pallas_call(
        functools.partial(front_kernel, sizes, dims),
        out_shape=[jax.ShapeDtypeStruct(*shape) for shape in shapes],
        in_specs=[VMEM_SPEC] * 7,
        out_specs=[VMEM_SPEC] * len(shapes),
        scratch_shapes=[
            pltpu.VMEM((2, rows, width), BF16),
            pltpu.VMEM((128, 2 * seq), F32),
            pltpu.VMEM((rows, width), BF16),
            pltpu.VMEM((rows, width), BF16),
            pltpu.VMEM((experts, capacity, width), BF16),
            pltpu.VMEM((experts, capacity, width), BF16),
            pltpu.SemaphoreType.DMA((12,)),
            pltpu.SemaphoreType.DMA((12,)),
            pltpu.SemaphoreType.DMA((5,)),
        ],
        compiler_params=pltpu.CompilerParams(
            collective_id=0, has_side_effects=True, vmem_limit_bytes=48 * 2**20
        ),
        cost_estimate=pl.CostEstimate(flops=30 * 10**9, bytes_accessed=10**8, transcendentals=10**6),
    )(tokens, small, w_qkv, w_out, bucket_row, dispatch, cotangent)


def expert_kernel(
    capacity,
    rows_ref,
    grads_ref,
    in_ref,
    back_ref,
    active_ref,
    d_pre_ref,
    sent_ref,
    result_ref,
    d_result_ref,
):
    rows = rows_ref[...]
    grads = grads_ref[...]
    gate = lifted(rows[:, :128], capacity)
    d_result_ref[...] = (gate * grads.astype(F32)).astype(BF16)
    hidden = in_ref.shape[1]
    step = min(hidden, 512)
    root = 0.7978845608028654
    sent, result, d_gate = 0.0, 0.0, 0.0
    for at in range(0, hidden, step):
        w_in, w_back = in_ref[:, at : at + step], back_ref[at : at + step, :]
        pre = matmul(rows, w_in)
        d_active = matmul_t(grads, w_back)
        square = pre * pre
        wave = jnp.tanh(root * pre * (1.0 + 0.044715 * square))
        upper = 0.5 * (1.0 + wave)
        slope = upper + 0.5 * pre * (1.0 - wave * wave) * (
            root * (1.0 + 3 * 0.044715 * square)
        )
        active = (pre * upper).astype(BF16)
        d_gate = d_gate + jnp.sum(active.astype(F32) * d_active, axis=1, keepdims=True)
        d_pre = (gate * d_active * slope).astype(BF16)
        active_ref[:, at : at + step] = active
        d_pre_ref[:, at : at + step] = d_pre
        result = result + matmul(active, w_back)
        sent = sent + matmul_t(d_pre, w_in)
    result_ref[...] = result.astype(BF16)
    sent_ref[...] = sent.astype(BF16)
    sent_ref[:, :128] = (sent[:, :128] + lowered(d_gate, capacity)).astype(BF16)


def expert(capacity, rows, grads, w_in, w_back):
    count, width = rows.shape
    hidden = w_in.shape[1]
    step = min(count, max(256, capacity))
    by_rows = [pl.BlockSpec((step, size), lambda i: (i, 0)) for size in (width, hidden)]
    return pl.pallas_call(
        functools.partial(expert_kernel, capacity),
        grid=(count // step,),
        out_shape=[
            jax.ShapeDtypeStruct((count, hidden), BF16),
            jax.ShapeDtypeStruct((count, hidden), BF16),
            jax.ShapeDtypeStruct((count, width), BF16),
            jax.ShapeDtypeStruct((count, width), BF16),
            jax.ShapeDtypeStruct((count, width), BF16),
        ],
        in_specs=[
            by_rows[0],
            by_rows[0],
            pl.BlockSpec(w_in.shape, lambda i: (0, 0)),
            pl.BlockSpec(w_back.shape, lambda i: (0, 0)),
        ],
        out_specs=[by_rows[1], by_rows[1], by_rows[0], by_rows[0], by_rows[0]],
        compiler_params=pltpu.CompilerParams(vmem_limit_bytes=40 * 2**20),
        cost_estimate=pl.CostEstimate(
            flops=8 * count * width * hidden, bytes_accessed=2 * 10**7, transcendentals=count * hidden
        ),
    )(rows, grads, w_in, w_back)


def back_kernel(
    sizes,
    dims,
    both,
    cut,
    sent_ref,
    result_ref,
    dispatch_ref,
    gout_ref,
    tok_ref,
    n1_ref,
    proj_ref,
    chance_ref,
    mixed_ref,
    w_all,
    small_all,
    hidden_ref,
    n2_ref,
    router_ref,
    wout_ref,
    bucket_ref,
    layer_ref,
    gtok_ref,
    gqkv_ref,
    gout_w_ref,
    grouter_ref,
    gsmall_ref,
    att_all,
    dqkv,
    sums,
    part_out,
    part_in,
    comm,
    total_ref,
    chip_in,
    chip,
    row_in,
    column_in,
    row_sum,
    column_sum,
    deep,
    deep_in,
    returned,
    send,
    recv,
    all_sems,
):
    heads, experts, capacity, buckets = dims
    ys, xs, zs = sizes
    rows, width = tok_ref.shape
    half = width // 2
    seq = 2 * rows
    own_heads = heads // 2
    head = width // heads
    blocks = half // 128
    chunk_rows = comm.shape[2]
    rep, mine = lax.axis_index("rep"), lax.axis_index("shard")
    other = 1 - mine
    core = lax.rem(rep, 2)
    z = lax.rem(rep // 2, zs)
    x = lax.rem(rep // (2 * zs), xs)
    y = rep // (2 * zs * xs)

    def place(y_at, x_at, z_at, core_at):
        return ((y_at * xs + x_at) * zs + z_at) * 2 + core_at

    xp = [lax.rem(x + step, xs) for step in range(1, xs)]
    yp = [lax.rem(y + step, ys) for step in range(1, ys)]
    zp = [lax.rem(z + step, zs) for step in range(1, zs)]
    core_peer = (place(y, x, z, 1 - core), mine)
    x_peers = [(place(y, at, z, core), mine) for at in xp]
    y_peers = [(place(at, x, z, core), mine) for at in yp]
    z_peers = [(place(y, x, at, core), mine) for at in zp]
    peer = (rep, other)
    devices = 2 * experts
    me = 2 * rep + mine
    greet_all(devices)
    number = [0]

    def send_to(source, target, to):
        i = number[0]
        number[0] += 1
        copy = pltpu.make_async_remote_copy(
            source, target, send.at[i], recv.at[i], to, device_id_type=MESH
        )
        copy.start()
        return copy

    def finish(copies):
        for copy in copies:
            copy.wait()

    wide = sent_ref.shape[0]
    step = min(wide, max(256, capacity))
    d_gate = jnp.concatenate(
        [lifted(sent_ref[at : at + step, :128], capacity) for at in range(0, wide, step)], axis=0
    )
    shift = capacity.bit_length() - 1
    own_lane = (iota((wide, 128), 0) >> (shift + 1)) == iota((wide, 128), 1)
    d_gate = jnp.where(own_lane, d_gate, 0.0)
    dispatch = dispatch_ref[...]
    high, low = two_parts(d_gate)
    d_router = matmul(dispatch, high) + matmul(dispatch, low)
    router = router_ref[...]
    d_logits = router * (d_router - jnp.sum(router * d_router, axis=-1, keepdims=True))
    d_logits = d_logits.astype(BF16)
    d_n2 = matmul(dispatch, sent_ref[...]) + matmul_t(d_logits, router_weight(small_all, half))
    hidden = hidden_ref[...]
    factor = rms_factor(hidden)
    unit = hidden * factor
    scaled = d_n2 * gain_row(small_all, half, blocks)
    d_hidden = gout_ref[...].astype(F32) + factor * (
        scaled - unit * jnp.mean(scaled * unit, axis=-1, keepdims=True)
    )
    att_all[mine] = d_hidden.astype(BF16)
    shared = send_to(att_all.at[mine], att_all.at[mine], peer)
    gtok_ref[...] = d_hidden
    g_gain_two = jnp.sum(d_n2 * unit, axis=0, keepdims=True)
    g_router = t_matmul(n2_ref[...], d_logits)

    def store(part, first, block):
        base = part * both
        span = both if part < 2 else chunk_rows - 2 * both
        at = 0
        while at < block.shape[0]:
            chunk_at, inside = divmod(first + at, span)
            count = min(span - inside, block.shape[0] - at)
            comm[chunk_at // 2, chunk_at % 2, base + inside : base + inside + count, :] = block[
                at : at + count
            ]
            at += count

    tile_rows = 3 * blocks * half
    for side in range(2):
        store(side, tile_rows, g_router[side * half : (side + 1) * half].astype(BF16))
    shared.wait()
    send_blocks(lambda to: result_ref.at[to], returned, devices, all_sems.at[0], all_sems.at[1])
    own_block = pltpu.make_async_copy(result_ref.at[me], returned.at[me], all_sems.at[2])
    own_block.start()

    d_att = [att_all[0], att_all[1]]
    for block in range(2 * blocks):
        columns = slice(block * 128, (block + 1) * 128)
        grad = t_matmul(mixed_ref[:rows, :], d_att[0][:, columns])
        grad = grad + t_matmul(mixed_ref[rows:, :], d_att[1][:, columns])
        store(2, block * half, grad.astype(BF16))
    d_mixed = jnp.concatenate(
        [matmul_t(part, wout_ref[...]).astype(BF16) for part in d_att], axis=0
    )
    scale = head ** (-0.5)
    flip = (iota((seq, seq), 0) + iota((seq, seq), 1) == seq - 1).astype(F32).astype(BF16)
    for h in range(own_heads):
        at = h * head
        query = proj_ref[:, at : at + head]
        key = proj_ref[:, half + at : half + at + head]
        value = proj_ref[:, 2 * half + at : 2 * half + at + head]
        d_o = d_mixed[:, at : at + head]
        chance = chance_ref[h]
        d_chance = matmul_t(d_o, value)
        wide_chance = chance.astype(F32)
        inner = jnp.sum(wide_chance * d_chance, axis=-1, keepdims=True)
        d_scores = (wide_chance * (d_chance - inner)).astype(BF16)
        dqkv[:, at : at + head] = (matmul(d_scores, key) * scale).astype(BF16)
        dqkv[:, half + at : half + at + head] = (t_matmul(d_scores, query) * scale).astype(BF16)
        dqkv[:, 2 * half + at : 2 * half + at + head] = t_matmul(chance, d_o).astype(BF16)
        flipped = matmul(flip, d_scores)
        flipped = jnp.concatenate([flipped, jnp.zeros((seq, seq), F32)], axis=1)
        lined = pltpu.roll(flipped, 0, 1, stride=1, stride_axis=0)
        sums[pl.ds(mine * own_heads + h, 1), :] = jnp.sum(lined, axis=0, keepdims=True)
        sums[pl.ds(other * own_heads + h, 1), :] = jnp.zeros((1, 2 * seq), F32)

    theirs = pl.ds(pl.multiple_of(other * rows, 16), rows)
    ours = pl.ds(pl.multiple_of(mine * rows, 16), rows)

    def d_normed(which):
        return jnp.concatenate(
            [matmul_t(dqkv[which, :], w_all[side]) for side in range(2)], axis=1
        )

    part_out[...] = d_normed(theirs).astype(BF16)
    part_copy = send_to(part_out, part_in, peer)
    d_n1 = d_normed(ours)
    for block in range(3 * blocks):
        grad = t_matmul(n1_ref[...], dqkv[:, block * 128 : (block + 1) * 128]).astype(BF16)
        for side in range(2):
            store(side, block * half, grad[side * half : (side + 1) * half])
    one_hot = bucket_mask(bucket_ref, buckets, seq - 1 - iota((buckets, 2 * seq), 1))
    high, low = two_parts(sums[...])
    g_table = (matmul_t(one_hot, high) + matmul_t(one_hot, low)).astype(BF16)
    for side in range(2):
        part = g_table[side * (buckets // 2) : (side + 1) * (buckets // 2)]
        store(side, tile_rows + half + 16, part)
    part_copy.wait()
    d_n1 = d_n1 + part_in[...].astype(F32)
    values = tok_ref[...].astype(F32)
    factor = rms_factor(values)
    unit = values * factor
    scaled = d_n1 * gain_row(small_all, half, 0)
    gtok_ref[...] = gtok_ref[...] + factor * (
        scaled - unit * jnp.mean(scaled * unit, axis=-1, keepdims=True)
    )
    g_gain_one = jnp.sum(d_n1 * unit, axis=0, keepdims=True)
    for side in range(2):
        pieces = [
            gain[:, side * half + i * 128 : side * half + (i + 1) * 128]
            for gain in (g_gain_one, g_gain_two)
            for i in range(blocks)
        ]
        pieces.append(jnp.zeros((16 - 2 * blocks, 128), F32))
        store(side, tile_rows + half, jnp.concatenate(pieces, axis=0).astype(BF16))

    first, second = pl.ds(0, cut), pl.ds(cut, chunk_rows - cut)
    chip_copy = send_to(comm.at[:, 1 - core], chip_in, core_peer)
    finish([chip_copy])

    def add_chip(i, carry):
        total = comm[i, core].astype(F32) + chip_in[i].astype(F32)
        chip[i // (xs * zs), lax.rem(i // zs, xs), lax.rem(i, zs)] = total.astype(BF16)
        return carry

    lax.fori_loop(0, ys * xs * zs, add_chip, 0)
    copies = [
        send_to(chip.at[:, at, :, first], row_in.at[i], to)
        for i, (at, to) in enumerate(zip(xp, x_peers))
    ]
    copies += [
        send_to(chip.at[at, :, :, second], column_in.at[i], to)
        for i, (at, to) in enumerate(zip(yp, y_peers))
    ]

    own_block.wait()
    wait_blocks(returned, devices, all_sems.at[0], all_sems.at[1])
    layer = hidden_ref[...]
    router_parts = two_parts(router_ref[...])
    per_step = step // capacity
    for i in range(wide // step):
        spread = (
            (iota((128, step), 1) + i * step) >> (shift + 1) == iota((128, step), 0)
        ).astype(F32).astype(BF16)
        weights = matmul(router_parts[0], spread) + matmul(router_parts[1], spread)
        weights = weights * dispatch_ref[:, i * step : (i + 1) * step].astype(F32)
        block = returned[i * per_step : (i + 1) * per_step].astype(F32)
        block = block.reshape(step, width).astype(BF16)
        for part in two_parts(weights):
            layer = layer + matmul(part, block)
    layer_ref[...] = layer.astype(BF16)
    finish(copies)

    def add_row(i, carry):
        for k in range(zs):
            total = chip[i, x, k, first].astype(F32)
            for j in range(xs - 1):
                total = total + row_in[j, i, k].astype(F32)
            row_sum[i, k] = total.astype(BF16)
        return carry

    def add_column(i, carry):
        for k in range(zs):
            total = chip[y, i, k, second].astype(F32)
            for j in range(ys - 1):
                total = total + column_in[j, i, k].astype(F32)
            column_sum[i, k] = total.astype(BF16)
        return carry

    lax.fori_loop(0, ys, add_row, 0)
    lax.fori_loop(0, xs, add_column, 0)
    copies = [
        send_to(row_sum.at[at], row_in.at[xs - 1 + i, 0], to)
        for i, (at, to) in enumerate(zip(yp, y_peers))
    ]
    copies += [
        send_to(column_sum.at[at], column_in.at[ys - 1 + i, 0], to)
        for i, (at, to) in enumerate(zip(xp, x_peers))
    ]
    finish(copies)
    for k in range(zs):
        total = row_sum[y, k].astype(F32)
        for i in range(ys - 1):
            total = total + row_in[xs - 1 + i, 0, k].astype(F32)
        deep[k, first] = total.astype(BF16)
        total = column_sum[x, k].astype(F32)
        for i in range(xs - 1):
            total = total + column_in[ys - 1 + i, 0, k].astype(F32)
        deep[k, second] = total.astype(BF16)
    finish([send_to(deep.at[at], deep_in.at[i], to) for i, (at, to) in enumerate(zip(zp, z_peers))])
    total = deep[z].astype(F32)
    for i in range(zs - 1):
        total = total + deep_in[i].astype(F32)
    done = total.astype(BF16)
    mine_at = pl.ds(pl.multiple_of(mine * both, 16), both)
    other_at = pl.ds(pl.multiple_of(other * both, 16), both)
    deep_in[zs - 1] = done
    out = total_ref.at[y, x, z, core]
    copies = [send_to(deep_in.at[zs - 1, other_at], out.at[mine_at], peer)]
    out[mine_at] = deep_in[zs - 1, mine_at]
    out[2 * both :] = done[2 * both :]
    finish(copies)
    finish([send_to(out, out, to) for to in z_peers])
    firsts = total_ref.at[y, x, :, core, first]
    seconds = total_ref.at[y, x, :, core, second]
    copies = [send_to(firsts, firsts, to) for to in y_peers]
    copies += [send_to(seconds, seconds, to) for to in x_peers]
    finish(copies)
    firsts = total_ref.at[:, x, :, core, first]
    seconds = total_ref.at[y, :, :, core, second]
    copies = [send_to(firsts, firsts, to) for to in x_peers]
    copies += [send_to(seconds, seconds, to) for to in y_peers]
    finish(copies)
    whole = total_ref.at[:, :, :, core]
    finish([send_to(whole, whole, core_peer)])

    def load(part, start, count):
        base = part * both
        span = both if part < 2 else chunk_rows - 2 * both
        pieces, at = [], 0
        while at < count:
            chunk_at, inside = divmod(start + at, span)
            size = min(span - inside, count - at)
            spot = (
                chunk_at // (2 * zs * xs),
                (chunk_at // (2 * zs)) % xs,
                (chunk_at // 2) % zs,
                chunk_at % 2,
            )
            pieces.append(total_ref[spot + (slice(base + inside, base + inside + size),)])
            at += size
        return pieces[0] if len(pieces) == 1 else jnp.concatenate(pieces, axis=0)

    for side in range(2):
        for block in range(3 * blocks):
            at = (block // blocks) * width + side * half + (block % blocks) * 128
            gqkv_ref[:, at : at + 128] = load(side, block * half, half)
    for block in range(2 * blocks):
        gout_w_ref[:, block * 128 : (block + 1) * 128] = load(2, block * half, half)
    g_router = sum(load(side, tile_rows, half).astype(F32) for side in range(2))
    grouter_ref[...] = g_router.T[:experts]
    gsmall_ref[...] = sum(
        load(side, tile_rows + half, 16 + buckets // 2).astype(F32) for side in range(2)
    )


def back(sizes, dims, sent, result, dispatch, cotangent, tokens, kept, w_out, bucket_row):
    ys, xs, zs = sizes
    heads, experts, capacity, buckets = dims
    rows, width = tokens.shape
    half, seq, lanes = width // 2, 2 * rows, 128
    count = 2 * ys * xs * zs
    both = up(3 * half * half // 128 + half + 16 + buckets // 2, 16 * count) // count
    chunk_rows = 2 * both + up(half * width // 128, 16 * count) // count
    cut = up(chunk_rows // 2, 16)
    per_core = count // 2
    many = 4 * (xs + ys) + 2 * zs + 4
    shapes = [
        ((rows, width), BF16),
        ((rows, width), F32),
        ((half, 3 * width), BF16),
        ((half, width), BF16),
        ((experts, half), F32),
        ((16 + buckets // 2, 128), F32),
    ]
    return pl.pallas_call(
        functools.partial(back_kernel, sizes, dims, both, cut),
        out_shape=[jax.ShapeDtypeStruct(*shape) for shape in shapes],
        in_specs=[VMEM_SPEC] * 16,
        out_specs=[VMEM_SPEC] * len(shapes),
        scratch_shapes=[
            pltpu.VMEM((2, rows, width), BF16),
            pltpu.VMEM((seq, 3 * half), BF16),
            pltpu.VMEM((128, 2 * seq), F32),
            pltpu.VMEM((rows, width), BF16),
            pltpu.VMEM((rows, width), BF16),
            pltpu.VMEM((per_core, 2, chunk_rows, lanes), BF16),
            pltpu.VMEM((ys, xs, zs, 2, chunk_rows, lanes), BF16),
            pltpu.VMEM((per_core, chunk_rows, lanes), BF16),
            pltpu.VMEM((ys, xs, zs, chunk_rows, lanes), BF16),
            pltpu.VMEM((xs + ys - 2, ys, zs, cut, lanes), BF16),
            pltpu.VMEM((xs + ys - 2, xs, zs, chunk_rows - cut, lanes), BF16),
            pltpu.VMEM((ys, zs, cut, lanes), BF16),
            pltpu.VMEM((xs, zs, chunk_rows - cut, lanes), BF16),
            pltpu.VMEM((zs, chunk_rows, lanes), BF16),
            pltpu.VMEM((zs, chunk_rows, lanes), BF16),
            pltpu.VMEM(result.shape, BF16),
            pltpu.SemaphoreType.DMA((many,)),
            pltpu.SemaphoreType.DMA((many,)),
            pltpu.SemaphoreType.DMA((3,)),
        ],
        compiler_params=pltpu.CompilerParams(
            collective_id=1, has_side_effects=True, vmem_limit_bytes=56 * 2**20
        ),
        cost_estimate=pl.CostEstimate(flops=60 * 10**9, bytes_accessed=2 * 10**8, transcendentals=0),
    )(sent, result, dispatch, cotangent, tokens, *kept, w_out, bucket_row)


def body(
    sizes,
    tokens,
    cotangent,
    attn_gain,
    w_qkv,
    w_out,
    rel_bias,
    buckets,
    ffn_gain,
    w_router,
    w_in,
    w_back,
    choice_ids,
):
    rows, width = tokens.shape
    half = width // 2
    bucket_half, heads = rel_bias.shape
    experts = w_router.shape[1]
    top = choice_ids.shape[1]
    capacity = up(max(2, 5 * rows * top // (4 * experts)) + 1, 8)
    slots = experts * capacity
    seq = 2 * rows
    dims = (heads, experts, capacity, 2 * bucket_half)
    blocks = half // 128

    flat_ids = choice_ids.reshape(-1)
    levels = jnp.arange(experts, dtype=jnp.int32)
    member = (flat_ids[:, None] == levels[None, :]).astype(BF16)
    order = jnp.arange(rows * top, dtype=jnp.int32)
    before = (order[:, None] > order[None, :]).astype(BF16)
    earlier = matmul(before, member)
    rank = jnp.sum(earlier * member.astype(F32), axis=1).astype(jnp.int32)
    slot = (flat_ids * capacity + rank).reshape(rows, top)
    dispatch = jnp.sum(
        (slot[:, :, None] == jnp.arange(slots, dtype=jnp.int32)).astype(BF16), axis=1
    )
    dispatch_two = jnp.broadcast_to(
        dispatch.reshape(rows, experts, 1, capacity), (rows, experts, 2, capacity)
    ).reshape(rows, 2 * slots)

    def swap_all(all_rows):
        blocks = all_rows.reshape(2 * experts, capacity, width)
        got = lax.all_to_all(blocks, ("rep", "shard"), split_axis=0, concat_axis=0, tiled=True)
        return got.reshape(2 * slots, width)

    gains = jnp.concatenate([attn_gain.reshape(blocks, 128), ffn_gain.reshape(blocks, 128)])
    small = jnp.concatenate(
        [
            jnp.pad(w_router, ((0, 0), (0, 128 - experts))),
            jnp.pad(gains, ((0, 16 - 2 * blocks), (0, 0))),
            jnp.pad(rel_bias, ((0, 0), (0, 128 - heads))),
        ]
    )
    bucket_row = buckets.reshape(1, seq)
    *kept, arrived, grad_rows = front(
        sizes, dims, tokens, small, w_qkv, w_out, bucket_row, dispatch, cotangent
    )
    arrived, grad_rows = (block.reshape(2 * slots, width) for block in (arrived, grad_rows))

    expert_in, expert_back = w_in[0], w_back[0]
    activated, grad_pre, grad_arrived, result, grad_result = expert(
        capacity, arrived, grad_rows, expert_in, expert_back
    )
    sent = swap_all(grad_arrived)
    result = result.reshape(2 * experts, capacity, width)
    grad_back_expert = t_matmul(activated, grad_result)
    grad_in_expert = t_matmul(arrived, grad_pre)

    layer_out, grad_tokens, g_qkv, g_out, g_router, g_small = back(
        sizes, dims, sent, result, dispatch_two, cotangent, tokens, kept, w_out, bucket_row
    )

    return (
        layer_out,
        grad_tokens,
        g_small[:blocks].reshape(half),
        g_qkv.astype(F32),
        g_out.astype(F32),
        g_small[16:, :heads],
        g_small[blocks : 2 * blocks].reshape(half),
        g_router.T,
        grad_in_expert[None],
        grad_back_expert[None],
    )


SIZES = {64: (4, 4, 2), 4: (2, 1, 1), 8: (2, 2, 1)}


def solution(mesh):
    in_specs = (
        P(("rep", "shard"), None),
        P(("rep", "shard"), None),
        P("shard"),
        P("shard", None),
        P("shard", None),
        P("shard", None),
        P(),
        P("shard"),
        P("shard", None),
        P("rep", None, "shard"),
        P("rep", "shard", None),
        P(("rep", "shard"), None),
    )
    out_specs = (
        P(("rep", "shard"), None),
        P(("rep", "shard"), None),
        P("shard"),
        P("shard", None),
        P("shard", None),
        P("shard", None),
        P("shard"),
        P("shard", None),
        P("rep", None, "shard"),
        P("rep", "shard", None),
    )
    sizes = SIZES[mesh.shape["rep"]]
    return jax.shard_map(
        functools.partial(body, sizes),
        mesh=mesh,
        in_specs=in_specs,
        out_specs=out_specs,
        check_vma=False,
    )
```

```python
import functools

import jax
import jax.numpy as jnp
from jax import lax
from jax.experimental import pallas as pl
from jax.experimental.pallas import tpu as pltpu
from jax.sharding import PartitionSpec as P

EPSILON = 1e-06
MASKED = -1e30
MESH = pl.DeviceIdType.MESH
VMEM_SPEC = pl.BlockSpec(memory_space=pltpu.VMEM)
F32 = jnp.float32
BF16 = jnp.bfloat16


def greet_all(count):
    me = 2 * lax.axis_index("rep") + lax.axis_index("shard")
    barrier = pltpu.get_barrier_semaphore()

    def signal(step, carry):
        to = lax.rem(me + step, count)
        pl.semaphore_signal(
            barrier, inc=1, device_id=(to // 2, lax.rem(to, 2)), device_id_type=MESH
        )
        return carry

    lax.fori_loop(1, count, signal, 0)
    pl.semaphore_wait(barrier, count - 1)


def send_blocks(source_of, target, count, send, recv):
    me = 2 * lax.axis_index("rep") + lax.axis_index("shard")

    def start(step, carry):
        to = lax.rem(me + 37 * step, count)
        pltpu.make_async_remote_copy(
            source_of(to),
            target.at[me],
            send,
            recv,
            (to // 2, lax.rem(to, 2)),
            device_id_type=MESH,
        ).start()
        return carry

    lax.fori_loop(1, count, start, 0)


def wait_blocks(target, count, send, recv):
    rep, mine = lax.axis_index("rep"), lax.axis_index("shard")
    most = target.at[pl.ds(0, count - 1)]
    pltpu.make_async_remote_copy(
        most, most, send, recv, (rep, 1 - mine), device_id_type=MESH
    ).wait()


def up(number, step):
    return -(-number // step) * step


def greet(peers):
    barrier = pltpu.get_barrier_semaphore()
    for peer in peers:
        pl.semaphore_signal(barrier, inc=1, device_id=peer, device_id_type=MESH)
    pl.semaphore_wait(barrier, len(peers))


def iota(shape, axis):
    return lax.broadcasted_iota(jnp.int32, shape, axis)


def dot(a, b, contract):
    return lax.dot_general(a, b, (contract, ((), ())), preferred_element_type=F32)


def matmul(a, b):
    return dot(a, b, ((1,), (0,)))


def matmul_t(a, b):
    return dot(a, b, ((1,), (1,)))


def t_matmul(a, b):
    return dot(a, b, ((0,), (0,)))


def two_parts(values):
    high = values.astype(BF16)
    return high, (values - high.astype(F32)).astype(BF16)


def rms_factor(values):
    return lax.rsqrt(jnp.mean(values * values, axis=-1, keepdims=True) + EPSILON)


def gain_row(small_ref, half, first):
    blocks = half // 128
    pieces = [
        small_ref[side, pl.ds(half + first + i, 1), :].astype(F32)
        for side in range(2)
        for i in range(blocks)
    ]
    return jnp.concatenate(pieces, axis=1)


def router_weight(small_ref, half):
    return jnp.concatenate([small_ref[0, :half, :], small_ref[1, :half, :]], axis=0)


def lifted(block, capacity):
    count = block.shape[0]
    shift = capacity.bit_length() - 1
    source, slot = iota((count, count), 1), iota((count, count), 0)
    carrier = (source == ((slot >> shift) << shift) + capacity - 1).astype(F32).astype(BF16)
    carried = matmul(carrier, block)
    lane, slot = iota((count, 128), 1), iota((count, 128), 0)
    mask = ((lane & (capacity - 1)) == (slot & (capacity - 1))) & (lane < 2 * capacity)
    return jnp.sum(jnp.where(mask, carried, 0.0), axis=1, keepdims=True)


def lowered(column, capacity):
    count = column.shape[0]
    shift = capacity.bit_length() - 1
    target, slot = iota((count, count), 0), iota((count, count), 1)
    carrier = (target == ((slot >> shift) << shift) + capacity - 1).astype(F32).astype(BF16)
    lane, slot = iota((count, 128), 1), iota((count, 128), 0) & (capacity - 1)
    high, low = two_parts(column)
    spread = jnp.where(lane == slot, high.astype(F32), 0.0)
    spread = spread + jnp.where(lane == slot + capacity, low.astype(F32), 0.0)
    return matmul(carrier, spread.astype(BF16))


def bucket_mask(bucket_ref, buckets, distance):
    row = bucket_ref[...]
    levels = iota((buckets, row.shape[1]), 0)
    low = jnp.sum((row < levels).astype(F32), axis=1, keepdims=True)
    high = jnp.sum((row <= levels).astype(F32), axis=1, keepdims=True)
    distance = distance.astype(F32)
    inside = (distance >= low) & (distance < high)
    return inside.astype(F32).astype(BF16)


def front_kernel(
    sizes,
    dims,
    tok_ref,
    small_ref,
    wqkv_ref,
    wout_ref,
    bucket_ref,
    dispatch_ref,
    gout_ref,
    n1_ref,
    proj_ref,
    chance_ref,
    mixed_ref,
    w_all,
    small_all,
    hidden_ref,
    n2_ref,
    router_ref,
    arrived_ref,
    grad_rows_ref,
    tok_all,
    bias_rows,
    part_out,
    part_in,
    outgoing,
    outgoing_grads,
    send,
    recv,
    local,
):
    heads, experts, capacity, buckets = dims
    ys, xs, zs = sizes
    rows, width = tok_ref.shape
    half = width // 2
    seq = 2 * rows
    own_heads = heads // 2
    head = width // heads
    slots = experts * capacity
    rep, mine = lax.axis_index("rep"), lax.axis_index("shard")
    other = 1 - mine
    core = lax.rem(rep, 2)
    peer = (rep, other)
    core_peer = (rep + 1 - 2 * core, mine)
    devices = 2 * experts
    me = 2 * rep + mine
    if zs == 2:
        z = lax.rem(rep // 2, 2)
        far_peer = (rep + 2 * (1 - 2 * z), other)
    greet_all(devices)

    def remote(i, source, target, to):
        copy = pltpu.make_async_remote_copy(
            source, target, send.at[i], recv.at[i], to, device_id_type=MESH
        )
        copy.start()
        return copy

    small_copy = remote(0, small_ref, small_all.at[mine], peer)
    near = half // 2 if zs == 1 else up(half // 12, 16)
    fetched = [(peer, 0, near)]
    if zs == 2:
        fetched.append((far_peer, near, half // 2 - near))
    weight_copies = []
    for j, (to, first, count) in enumerate(fetched):
        at = pl.ds(pl.multiple_of(core * (half // 2) + first, 16), count)
        for block in range(3):
            theirs = pl.ds(pl.multiple_of((2 * block + other) * half, 128), half)
            weight_copies.append(
                remote(
                    2 + 3 * j + block,
                    wqkv_ref.at[at, theirs],
                    w_all.at[mine, at, pl.ds(block * half, half)],
                    to,
                )
            )
    tok_copy = remote(1, tok_ref, tok_all.at[mine], peer)
    kept = [
        pltpu.make_async_copy(tok_ref, tok_all.at[mine], local.at[0]),
        pltpu.make_async_copy(small_ref, small_all.at[mine], local.at[1]),
    ]
    for block in range(3):
        ours = pl.ds(pl.multiple_of((2 * block + mine) * half, 128), half)
        kept.append(
            pltpu.make_async_copy(
                wqkv_ref.at[:, ours], w_all.at[mine, :, pl.ds(block * half, half)], local.at[2 + block]
            )
        )
    for copy in kept:
        copy.start()
    for copy in kept:
        copy.wait()
    small_copy.wait()

    table = jnp.concatenate([small_all[0, half + 16 :, :], small_all[1, half + 16 :, :]], axis=0)
    column = iota((buckets, 2 * seq), 1)
    distance = jnp.where(column == 0, 0, 2 * seq - column)
    one_hot = bucket_mask(bucket_ref, buckets, distance)
    bias_rows[...] = t_matmul(table, one_hot)
    gain_one = gain_row(small_all, half, 0)
    gain_two = gain_row(small_all, half, half // 128)
    dispatch = dispatch_ref[...]
    blocks = t_matmul(dispatch, gout_ref[...]).reshape(experts, capacity, width)
    outgoing_grads[...] = blocks.astype(BF16)

    for copy in weight_copies:
        copy.wait()
    got = w_all.at[other, pl.ds(pl.multiple_of(core * (half // 2), 16), half // 2)]
    passed = remote(8, got, got, core_peer)
    send_blocks(
        lambda to: outgoing_grads.at[to // 2], grad_rows_ref, devices, send.at[10], recv.at[10]
    )
    own_block = pltpu.make_async_copy(outgoing_grads.at[rep], grad_rows_ref.at[me], local.at[0])
    own_block.start()
    tok_copy.wait()
    for side in range(2):
        values = tok_all[side].astype(F32)
        n1_ref[side * rows : (side + 1) * rows, :] = (
            values * rms_factor(values) * gain_one
        ).astype(BF16)
    passed.wait()
    normed = n1_ref[...]
    for block in range(3):
        columns = pl.ds(block * half, half)
        total = matmul(normed[:, :half], w_all[0, :, columns])
        total = total + matmul(normed[:, half:], w_all[1, :, columns])
        proj_ref[:, columns] = total.astype(BF16)

    scale = head ** (-0.5)
    causal = iota((seq, seq), 0) >= iota((seq, seq), 1)
    for h in range(own_heads):
        at = h * head
        query = proj_ref[:, at : at + head]
        key = proj_ref[:, half + at : half + at + head]
        value = proj_ref[:, 2 * half + at : 2 * half + at + head]
        row = bias_rows[pl.ds(mine * own_heads + h, 1), :]
        bias = pltpu.roll(
            jnp.broadcast_to(row, (seq, 2 * seq)), 0, 1, stride=1, stride_axis=0
        )[:, :seq]
        scores = jnp.where(causal, matmul_t(query, key) * scale + bias, MASKED)
        raised = jnp.exp(scores - jnp.max(scores, axis=-1, keepdims=True))
        chance = (raised / jnp.sum(raised, axis=-1, keepdims=True)).astype(BF16)
        chance_ref[h] = chance
        mixed_ref[:, at : at + head] = matmul(chance, value).astype(BF16)

    theirs = pl.ds(pl.multiple_of(other * rows, 16), rows)
    ours = pl.ds(pl.multiple_of(mine * rows, 16), rows)
    part_out[...] = matmul(mixed_ref[theirs, :], wout_ref[...]).astype(BF16)
    part_copy = remote(9, part_out, part_in, peer)
    hidden = tok_ref[...].astype(F32) + matmul(mixed_ref[ours, :], wout_ref[...])
    part_copy.wait()
    hidden = hidden + part_in[...].astype(F32)
    hidden_ref[...] = hidden
    normed = (hidden * rms_factor(hidden) * gain_two).astype(BF16)
    n2_ref[...] = normed
    logits = matmul(normed, router_weight(small_all, half))
    logits = jnp.where(iota((rows, 128), 1) < experts, logits, MASKED)
    raised = jnp.exp(logits - jnp.max(logits, axis=-1, keepdims=True))
    router = raised / jnp.sum(raised, axis=-1, keepdims=True)
    router_ref[...] = router

    shift = capacity.bit_length() - 1
    spread = (iota((128, slots), 0) == (iota((128, slots), 1) >> shift)).astype(F32).astype(BF16)
    row_of, slot_of = iota((slots, slots), 0), iota((slots, slots), 1)
    carrier = ((row_of & (capacity - 1)) == capacity - 1) & (
        (row_of >> shift) == (slot_of >> shift)
    )
    place = iota((slots, 128), 0) & (capacity - 1)
    gates = jnp.zeros((slots, 128), F32)
    for i, part in enumerate(two_parts(router)):
        gate = jnp.sum(matmul(part, spread) * dispatch.astype(F32), axis=0, keepdims=True)
        left = jnp.where(carrier, gate, 0.0).astype(BF16)
        right = (place == iota((slots, 128), 1) - i * capacity).astype(F32).astype(BF16)
        gates = gates + matmul(left, right)
    sent = t_matmul(dispatch, normed)
    first = (sent[:, :128] + gates).reshape(experts, capacity, 128)
    outgoing[...] = sent.reshape(experts, capacity, width).astype(BF16)
    outgoing[:, :, :128] = first.astype(BF16)
    send_blocks(lambda to: outgoing.at[to // 2], arrived_ref, devices, send.at[11], recv.at[11])
    own_block.wait()
    own_block = pltpu.make_async_copy(outgoing.at[rep], arrived_ref.at[me], local.at[0])
    own_block.start()
    own_block.wait()
    wait_blocks(grad_rows_ref, devices, send.at[10], recv.at[10])
    wait_blocks(arrived_ref, devices, send.at[11], recv.at[11])


def front(sizes, dims, tokens, small, w_qkv, w_out, bucket_row, dispatch, cotangent):
    rows, width = tokens.shape
    heads, experts, capacity, buckets = dims
    half, seq, slots = width // 2, 2 * rows, experts * capacity
    shapes = [
        ((seq, width), BF16),
        ((seq, 3 * half), BF16),
        ((heads // 2, seq, seq), BF16),
        ((seq, half), BF16),
        ((2, half, 3 * half), BF16),
        ((2,) + small.shape, BF16),
        ((rows, width), F32),
        ((rows, width), BF16),
        ((rows, 128), F32),
        ((2 * experts, capacity, width), BF16),
        ((2 * experts, capacity, width), BF16),
    ]
    return pl.pallas_call(
        functools.partial(front_kernel, sizes, dims),
        out_shape=[jax.ShapeDtypeStruct(*shape) for shape in shapes],
        in_specs=[VMEM_SPEC] * 7,
        out_specs=[VMEM_SPEC] * len(shapes),
        scratch_shapes=[
            pltpu.VMEM((2, rows, width), BF16),
            pltpu.VMEM((128, 2 * seq), F32),
            pltpu.VMEM((rows, width), BF16),
            pltpu.VMEM((rows, width), BF16),
            pltpu.VMEM((experts, capacity, width), BF16),
            pltpu.VMEM((experts, capacity, width), BF16),
            pltpu.SemaphoreType.DMA((12,)),
            pltpu.SemaphoreType.DMA((12,)),
            pltpu.SemaphoreType.DMA((5,)),
        ],
        compiler_params=pltpu.CompilerParams(
            collective_id=0, has_side_effects=True, vmem_limit_bytes=48 * 2**20
        ),
        cost_estimate=pl.CostEstimate(flops=30 * 10**9, bytes_accessed=10**8, transcendentals=10**6),
    )(tokens, small, w_qkv, w_out, bucket_row, dispatch, cotangent)


def expert_kernel(
    capacity,
    rows_ref,
    grads_ref,
    in_ref,
    back_ref,
    active_ref,
    d_pre_ref,
    sent_ref,
    result_ref,
    d_result_ref,
):
    rows = rows_ref[...]
    grads = grads_ref[...]
    gate = lifted(rows[:, :128], capacity)
    d_result_ref[...] = (gate * grads.astype(F32)).astype(BF16)
    hidden = in_ref.shape[1]
    step = min(hidden, 512)
    root = 0.7978845608028654
    sent, result, d_gate = 0.0, 0.0, 0.0
    for at in range(0, hidden, step):
        w_in, w_back = in_ref[:, at : at + step], back_ref[at : at + step, :]
        pre = matmul(rows, w_in)
        d_active = matmul_t(grads, w_back)
        square = pre * pre
        wave = jnp.tanh(root * pre * (1.0 + 0.044715 * square))
        upper = 0.5 * (1.0 + wave)
        slope = upper + 0.5 * pre * (1.0 - wave * wave) * (
            root * (1.0 + 3 * 0.044715 * square)
        )
        active = (pre * upper).astype(BF16)
        d_gate = d_gate + jnp.sum(active.astype(F32) * d_active, axis=1, keepdims=True)
        d_pre = (gate * d_active * slope).astype(BF16)
        active_ref[:, at : at + step] = active
        d_pre_ref[:, at : at + step] = d_pre
        result = result + matmul(active, w_back)
        sent = sent + matmul_t(d_pre, w_in)
    result_ref[...] = result.astype(BF16)
    sent_ref[...] = sent.astype(BF16)
    sent_ref[:, :128] = (sent[:, :128] + lowered(d_gate, capacity)).astype(BF16)


def expert(capacity, rows, grads, w_in, w_back):
    count, width = rows.shape
    hidden = w_in.shape[1]
    step = min(count, max(256, capacity))
    by_rows = [pl.BlockSpec((step, size), lambda i: (i, 0)) for size in (width, hidden)]
    return pl.pallas_call(
        functools.partial(expert_kernel, capacity),
        grid=(count // step,),
        out_shape=[
            jax.ShapeDtypeStruct((count, hidden), BF16),
            jax.ShapeDtypeStruct((count, hidden), BF16),
            jax.ShapeDtypeStruct((count, width), BF16),
            jax.ShapeDtypeStruct((count, width), BF16),
            jax.ShapeDtypeStruct((count, width), BF16),
        ],
        in_specs=[
            by_rows[0],
            by_rows[0],
            pl.BlockSpec(w_in.shape, lambda i: (0, 0)),
            pl.BlockSpec(w_back.shape, lambda i: (0, 0)),
        ],
        out_specs=[by_rows[1], by_rows[1], by_rows[0], by_rows[0], by_rows[0]],
        compiler_params=pltpu.CompilerParams(vmem_limit_bytes=40 * 2**20),
        cost_estimate=pl.CostEstimate(
            flops=8 * count * width * hidden, bytes_accessed=2 * 10**7, transcendentals=count * hidden
        ),
    )(rows, grads, w_in, w_back)


def back_kernel(
    sizes,
    dims,
    both,
    cut,
    sent_ref,
    result_ref,
    dispatch_ref,
    gout_ref,
    tok_ref,
    n1_ref,
    proj_ref,
    chance_ref,
    mixed_ref,
    w_all,
    small_all,
    hidden_ref,
    n2_ref,
    router_ref,
    wout_ref,
    bucket_ref,
    layer_ref,
    gtok_ref,
    gqkv_ref,
    gout_w_ref,
    grouter_ref,
    ggain_one_ref,
    ggain_two_ref,
    gtable_ref,
    att_all,
    dqkv,
    sums,
    part_out,
    part_in,
    comm,
    total_ref,
    chip_in,
    chip,
    row_in,
    column_in,
    row_sum,
    column_sum,
    deep,
    deep_in,
    returned,
    send,
    recv,
    all_sems,
):
    heads, experts, capacity, buckets = dims
    ys, xs, zs = sizes
    rows, width = tok_ref.shape
    half = width // 2
    seq = 2 * rows
    own_heads = heads // 2
    head = width // heads
    blocks = half // 128
    chunk_rows = comm.shape[2]
    rep, mine = lax.axis_index("rep"), lax.axis_index("shard")
    other = 1 - mine
    core = lax.rem(rep, 2)
    z = lax.rem(rep // 2, zs)
    x = lax.rem(rep // (2 * zs), xs)
    y = rep // (2 * zs * xs)

    def place(y_at, x_at, z_at, core_at):
        return ((y_at * xs + x_at) * zs + z_at) * 2 + core_at

    xp = [lax.rem(x + step, xs) for step in range(1, xs)]
    yp = [lax.rem(y + step, ys) for step in range(1, ys)]
    zp = [lax.rem(z + step, zs) for step in range(1, zs)]
    core_peer = (place(y, x, z, 1 - core), mine)
    x_peers = [(place(y, at, z, core), mine) for at in xp]
    y_peers = [(place(at, x, z, core), mine) for at in yp]
    z_peers = [(place(y, x, at, core), mine) for at in zp]
    peer = (rep, other)
    devices = 2 * experts
    me = 2 * rep + mine
    greet_all(devices)
    number = [0]

    def send_to(source, target, to):
        i = number[0]
        number[0] += 1
        copy = pltpu.make_async_remote_copy(
            source, target, send.at[i], recv.at[i], to, device_id_type=MESH
        )
        copy.start()
        return copy

    def finish(copies):
        for copy in copies:
            copy.wait()

    wide = sent_ref.shape[0]
    step = min(wide, max(256, capacity))
    d_gate = jnp.concatenate(
        [lifted(sent_ref[at : at + step, :128], capacity) for at in range(0, wide, step)], axis=0
    )
    shift = capacity.bit_length() - 1
    own_lane = (iota((wide, 128), 0) >> (shift + 1)) == iota((wide, 128), 1)
    d_gate = jnp.where(own_lane, d_gate, 0.0)
    dispatch = dispatch_ref[...]
    high, low = two_parts(d_gate)
    d_router = matmul(dispatch, high) + matmul(dispatch, low)
    router = router_ref[...]
    d_logits = router * (d_router - jnp.sum(router * d_router, axis=-1, keepdims=True))
    d_logits = d_logits.astype(BF16)
    d_n2 = matmul(dispatch, sent_ref[...]) + matmul_t(d_logits, router_weight(small_all, half))
    hidden = hidden_ref[...]
    factor = rms_factor(hidden)
    unit = hidden * factor
    scaled = d_n2 * gain_row(small_all, half, blocks)
    d_hidden = gout_ref[...].astype(F32) + factor * (
        scaled - unit * jnp.mean(scaled * unit, axis=-1, keepdims=True)
    )
    att_all[mine] = d_hidden.astype(BF16)
    shared = send_to(att_all.at[mine], att_all.at[mine], peer)
    gtok_ref[...] = d_hidden
    g_gain_two = jnp.sum(d_n2 * unit, axis=0, keepdims=True)
    g_router = t_matmul(n2_ref[...], d_logits)

    def store(part, first, block):
        base = part * both
        span = both if part < 2 else chunk_rows - 2 * both
        at = 0
        while at < block.shape[0]:
            chunk_at, inside = divmod(first + at, span)
            count = min(span - inside, block.shape[0] - at)
            comm[chunk_at // 2, chunk_at % 2, base + inside : base + inside + count, :] = block[
                at : at + count
            ]
            at += count

    tile_rows = 3 * blocks * half
    for side in range(2):
        store(side, tile_rows, g_router[side * half : (side + 1) * half].astype(BF16))
    shared.wait()
    send_blocks(lambda to: result_ref.at[to], returned, devices, all_sems.at[0], all_sems.at[1])
    own_block = pltpu.make_async_copy(result_ref.at[me], returned.at[me], all_sems.at[2])
    own_block.start()

    d_att = [att_all[0], att_all[1]]
    for block in range(2 * blocks):
        columns = slice(block * 128, (block + 1) * 128)
        grad = t_matmul(mixed_ref[:rows, :], d_att[0][:, columns])
        grad = grad + t_matmul(mixed_ref[rows:, :], d_att[1][:, columns])
        store(2, block * half, grad.astype(BF16))
    d_mixed = jnp.concatenate(
        [matmul_t(part, wout_ref[...]).astype(BF16) for part in d_att], axis=0
    )
    scale = head ** (-0.5)
    flip = (iota((seq, seq), 0) + iota((seq, seq), 1) == seq - 1).astype(F32).astype(BF16)
    for h in range(own_heads):
        at = h * head
        query = proj_ref[:, at : at + head]
        key = proj_ref[:, half + at : half + at + head]
        value = proj_ref[:, 2 * half + at : 2 * half + at + head]
        d_o = d_mixed[:, at : at + head]
        chance = chance_ref[h]
        d_chance = matmul_t(d_o, value)
        wide_chance = chance.astype(F32)
        inner = jnp.sum(wide_chance * d_chance, axis=-1, keepdims=True)
        d_scores = (wide_chance * (d_chance - inner)).astype(BF16)
        dqkv[:, at : at + head] = (matmul(d_scores, key) * scale).astype(BF16)
        dqkv[:, half + at : half + at + head] = (t_matmul(d_scores, query) * scale).astype(BF16)
        dqkv[:, 2 * half + at : 2 * half + at + head] = t_matmul(chance, d_o).astype(BF16)
        flipped = matmul(flip, d_scores)
        flipped = jnp.concatenate([flipped, jnp.zeros((seq, seq), F32)], axis=1)
        lined = pltpu.roll(flipped, 0, 1, stride=1, stride_axis=0)
        sums[pl.ds(mine * own_heads + h, 1), :] = jnp.sum(lined, axis=0, keepdims=True)
        sums[pl.ds(other * own_heads + h, 1), :] = jnp.zeros((1, 2 * seq), F32)

    theirs = pl.ds(pl.multiple_of(other * rows, 16), rows)
    ours = pl.ds(pl.multiple_of(mine * rows, 16), rows)

    def d_normed(which):
        return jnp.concatenate(
            [matmul_t(dqkv[which, :], w_all[side]) for side in range(2)], axis=1
        )

    part_out[...] = d_normed(theirs).astype(BF16)
    part_copy = send_to(part_out, part_in, peer)
    d_n1 = d_normed(ours)
    for block in range(3 * blocks):
        grad = t_matmul(n1_ref[...], dqkv[:, block * 128 : (block + 1) * 128]).astype(BF16)
        for side in range(2):
            store(side, block * half, grad[side * half : (side + 1) * half])
    one_hot = bucket_mask(bucket_ref, buckets, seq - 1 - iota((buckets, 2 * seq), 1))
    high, low = two_parts(sums[...])
    g_table = (matmul_t(one_hot, high) + matmul_t(one_hot, low)).astype(BF16)
    for side in range(2):
        part = g_table[side * (buckets // 2) : (side + 1) * (buckets // 2)]
        store(side, tile_rows + half + 16, part)
    part_copy.wait()
    d_n1 = d_n1 + part_in[...].astype(F32)
    values = tok_ref[...].astype(F32)
    factor = rms_factor(values)
    unit = values * factor
    scaled = d_n1 * gain_row(small_all, half, 0)
    gtok_ref[...] = gtok_ref[...] + factor * (
        scaled - unit * jnp.mean(scaled * unit, axis=-1, keepdims=True)
    )
    g_gain_one = jnp.sum(d_n1 * unit, axis=0, keepdims=True)
    for side in range(2):
        pieces = [
            gain[:, side * half + i * 128 : side * half + (i + 1) * 128]
            for gain in (g_gain_one, g_gain_two)
            for i in range(blocks)
        ]
        pieces.append(jnp.zeros((16 - 2 * blocks, 128), F32))
        store(side, tile_rows + half, jnp.concatenate(pieces, axis=0).astype(BF16))

    first, second = pl.ds(0, cut), pl.ds(cut, chunk_rows - cut)
    chip_copy = send_to(comm.at[:, 1 - core], chip_in, core_peer)
    finish([chip_copy])

    def add_chip(i, carry):
        total = comm[i, core].astype(F32) + chip_in[i].astype(F32)
        chip[i // (xs * zs), lax.rem(i // zs, xs), lax.rem(i, zs)] = total.astype(BF16)
        return carry

    lax.fori_loop(0, ys * xs * zs, add_chip, 0)
    copies = [
        send_to(chip.at[:, at, :, first], row_in.at[i], to)
        for i, (at, to) in enumerate(zip(xp, x_peers))
    ]
    copies += [
        send_to(chip.at[at, :, :, second], column_in.at[i], to)
        for i, (at, to) in enumerate(zip(yp, y_peers))
    ]

    own_block.wait()
    wait_blocks(returned, devices, all_sems.at[0], all_sems.at[1])
    layer = hidden_ref[...]
    router_parts = two_parts(router_ref[...])
    per_step = step // capacity
    for i in range(wide // step):
        spread = (
            (iota((128, step), 1) + i * step) >> (shift + 1) == iota((128, step), 0)
        ).astype(F32).astype(BF16)
        weights = matmul(router_parts[0], spread) + matmul(router_parts[1], spread)
        weights = weights * dispatch_ref[:, i * step : (i + 1) * step].astype(F32)
        block = returned[i * per_step : (i + 1) * per_step].astype(F32)
        block = block.reshape(step, width).astype(BF16)
        for part in two_parts(weights):
            layer = layer + matmul(part, block)
    layer_ref[...] = layer.astype(BF16)
    finish(copies)

    def add_row(i, carry):
        for k in range(zs):
            total = chip[i, x, k, first].astype(F32)
            for j in range(xs - 1):
                total = total + row_in[j, i, k].astype(F32)
            row_sum[i, k] = total.astype(BF16)
        return carry

    def add_column(i, carry):
        for k in range(zs):
            total = chip[y, i, k, second].astype(F32)
            for j in range(ys - 1):
                total = total + column_in[j, i, k].astype(F32)
            column_sum[i, k] = total.astype(BF16)
        return carry

    lax.fori_loop(0, ys, add_row, 0)
    lax.fori_loop(0, xs, add_column, 0)
    copies = [
        send_to(row_sum.at[at], row_in.at[xs - 1 + i, 0], to)
        for i, (at, to) in enumerate(zip(yp, y_peers))
    ]
    copies += [
        send_to(column_sum.at[at], column_in.at[ys - 1 + i, 0], to)
        for i, (at, to) in enumerate(zip(xp, x_peers))
    ]
    finish(copies)
    for k in range(zs):
        total = row_sum[y, k].astype(F32)
        for i in range(ys - 1):
            total = total + row_in[xs - 1 + i, 0, k].astype(F32)
        deep[k, first] = total.astype(BF16)
        total = column_sum[x, k].astype(F32)
        for i in range(xs - 1):
            total = total + column_in[ys - 1 + i, 0, k].astype(F32)
        deep[k, second] = total.astype(BF16)
    finish([send_to(deep.at[at], deep_in.at[i], to) for i, (at, to) in enumerate(zip(zp, z_peers))])
    total = deep[z].astype(F32)
    for i in range(zs - 1):
        total = total + deep_in[i].astype(F32)
    done = total.astype(BF16)
    mine_at = pl.ds(pl.multiple_of(mine * both, 16), both)
    other_at = pl.ds(pl.multiple_of(other * both, 16), both)
    deep_in[zs - 1] = done
    out = total_ref.at[y, x, z, core]
    copies = [send_to(deep_in.at[zs - 1, other_at], out.at[mine_at], peer)]
    out[mine_at] = deep_in[zs - 1, mine_at]
    out[2 * both :] = done[2 * both :]
    finish(copies)
    finish([send_to(out, out, to) for to in z_peers])
    firsts = total_ref.at[y, x, :, core, first]
    seconds = total_ref.at[y, x, :, core, second]
    copies = [send_to(firsts, firsts, to) for to in y_peers]
    copies += [send_to(seconds, seconds, to) for to in x_peers]
    finish(copies)
    firsts = total_ref.at[:, x, :, core, first]
    seconds = total_ref.at[y, :, :, core, second]
    copies = [send_to(firsts, firsts, to) for to in x_peers]
    copies += [send_to(seconds, seconds, to) for to in y_peers]
    finish(copies)
    whole = total_ref.at[:, :, :, core]
    finish([send_to(whole, whole, core_peer)])

    def load(part, start, count):
        base = part * both
        span = both if part < 2 else chunk_rows - 2 * both
        pieces, at = [], 0
        while at < count:
            chunk_at, inside = divmod(start + at, span)
            size = min(span - inside, count - at)
            spot = (
                chunk_at // (2 * zs * xs),
                (chunk_at // (2 * zs)) % xs,
                (chunk_at // 2) % zs,
                chunk_at % 2,
            )
            pieces.append(total_ref[spot + (slice(base + inside, base + inside + size),)])
            at += size
        return pieces[0] if len(pieces) == 1 else jnp.concatenate(pieces, axis=0)

    for side in range(2):
        for block in range(3 * blocks):
            at = (block // blocks) * width + side * half + (block % blocks) * 128
            gqkv_ref[:, at : at + 128] = load(side, block * half, half)
    for block in range(2 * blocks):
        gout_w_ref[:, block * 128 : (block + 1) * 128] = load(2, block * half, half)
    g_router = sum(load(side, tile_rows, half).astype(F32) for side in range(2))
    grouter_ref[...] = g_router.T[:experts]
    g_small = sum(
        load(side, tile_rows + half, 16 + buckets // 2).astype(F32) for side in range(2)
    )
    ggain_one_ref[...] = g_small[:blocks]
    ggain_two_ref[...] = g_small[blocks : 2 * blocks]
    gtable_ref[...] = g_small[16:, :heads]


def back(sizes, dims, sent, result, dispatch, cotangent, tokens, kept, w_out, bucket_row):
    ys, xs, zs = sizes
    heads, experts, capacity, buckets = dims
    rows, width = tokens.shape
    half, seq, lanes = width // 2, 2 * rows, 128
    count = 2 * ys * xs * zs
    both = up(3 * half * half // 128 + half + 16 + buckets // 2, 16 * count) // count
    chunk_rows = 2 * both + up(half * width // 128, 16 * count) // count
    cut = up(chunk_rows // 2, 16)
    per_core = count // 2
    many = 4 * (xs + ys) + 2 * zs + 4
    shapes = [
        ((rows, width), BF16),
        ((rows, width), F32),
        ((half, 3 * width), BF16),
        ((half, width), BF16),
        ((experts, half), F32),
        ((half // 128, 128), F32),
        ((half // 128, 128), F32),
        ((buckets // 2, heads), F32),
    ]
    return pl.pallas_call(
        functools.partial(back_kernel, sizes, dims, both, cut),
        out_shape=[jax.ShapeDtypeStruct(*shape) for shape in shapes],
        in_specs=[VMEM_SPEC] * 16,
        out_specs=[VMEM_SPEC] * len(shapes),
        scratch_shapes=[
            pltpu.VMEM((2, rows, width), BF16),
            pltpu.VMEM((seq, 3 * half), BF16),
            pltpu.VMEM((128, 2 * seq), F32),
            pltpu.VMEM((rows, width), BF16),
            pltpu.VMEM((rows, width), BF16),
            pltpu.VMEM((per_core, 2, chunk_rows, lanes), BF16),
            pltpu.VMEM((ys, xs, zs, 2, chunk_rows, lanes), BF16),
            pltpu.VMEM((per_core, chunk_rows, lanes), BF16),
            pltpu.VMEM((ys, xs, zs, chunk_rows, lanes), BF16),
            pltpu.VMEM((xs + ys - 2, ys, zs, cut, lanes), BF16),
            pltpu.VMEM((xs + ys - 2, xs, zs, chunk_rows - cut, lanes), BF16),
            pltpu.VMEM((ys, zs, cut, lanes), BF16),
            pltpu.VMEM((xs, zs, chunk_rows - cut, lanes), BF16),
            pltpu.VMEM((zs, chunk_rows, lanes), BF16),
            pltpu.VMEM((zs, chunk_rows, lanes), BF16),
            pltpu.VMEM(result.shape, BF16),
            pltpu.SemaphoreType.DMA((many,)),
            pltpu.SemaphoreType.DMA((many,)),
            pltpu.SemaphoreType.DMA((3,)),
        ],
        compiler_params=pltpu.CompilerParams(
            collective_id=1, has_side_effects=True, vmem_limit_bytes=56 * 2**20
        ),
        cost_estimate=pl.CostEstimate(flops=60 * 10**9, bytes_accessed=2 * 10**8, transcendentals=0),
    )(sent, result, dispatch, cotangent, tokens, *kept, w_out, bucket_row)


def body(
    sizes,
    tokens,
    cotangent,
    attn_gain,
    w_qkv,
    w_out,
    rel_bias,
    buckets,
    ffn_gain,
    w_router,
    w_in,
    w_back,
    choice_ids,
):
    rows, width = tokens.shape
    half = width // 2
    bucket_half, heads = rel_bias.shape
    experts = w_router.shape[1]
    top = choice_ids.shape[1]
    capacity = up(max(2, 5 * rows * top // (4 * experts)) + 1, 8)
    slots = experts * capacity
    seq = 2 * rows
    dims = (heads, experts, capacity, 2 * bucket_half)
    blocks = half // 128

    flat_ids = choice_ids.reshape(-1)
    levels = jnp.arange(experts, dtype=jnp.int32)
    member = (flat_ids[:, None] == levels[None, :]).astype(BF16)
    order = jnp.arange(rows * top, dtype=jnp.int32)
    before = (order[:, None] > order[None, :]).astype(BF16)
    earlier = matmul(before, member)
    rank = jnp.sum(earlier * member.astype(F32), axis=1).astype(jnp.int32)
    slot = (flat_ids * capacity + rank).reshape(rows, top)
    dispatch = jnp.sum(
        (slot[:, :, None] == jnp.arange(slots, dtype=jnp.int32)).astype(BF16), axis=1
    )
    dispatch_two = jnp.broadcast_to(
        dispatch.reshape(rows, experts, 1, capacity), (rows, experts, 2, capacity)
    ).reshape(rows, 2 * slots)

    def swap_all(all_rows):
        blocks = all_rows.reshape(2 * experts, capacity, width)
        got = lax.all_to_all(blocks, ("rep", "shard"), split_axis=0, concat_axis=0, tiled=True)
        return got.reshape(2 * slots, width)

    gains = jnp.concatenate([attn_gain.reshape(blocks, 128), ffn_gain.reshape(blocks, 128)])
    small = jnp.concatenate(
        [
            jnp.pad(w_router, ((0, 0), (0, 128 - experts))),
            jnp.pad(gains, ((0, 16 - 2 * blocks), (0, 0))),
            jnp.pad(rel_bias, ((0, 0), (0, 128 - heads))),
        ]
    )
    bucket_row = buckets.reshape(1, seq)
    *kept, arrived, grad_rows = front(
        sizes, dims, tokens, small, w_qkv, w_out, bucket_row, dispatch, cotangent
    )
    arrived, grad_rows = (block.reshape(2 * slots, width) for block in (arrived, grad_rows))

    expert_in, expert_back = w_in[0], w_back[0]
    activated, grad_pre, grad_arrived, result, grad_result = expert(
        capacity, arrived, grad_rows, expert_in, expert_back
    )
    sent = swap_all(grad_arrived)
    result = result.reshape(2 * experts, capacity, width)
    grad_back_expert = t_matmul(activated, grad_result)
    grad_in_expert = t_matmul(arrived, grad_pre)

    layer_out, grad_tokens, g_qkv, g_out, g_router, g_gain_one, g_gain_two, g_table = back(
        sizes, dims, sent, result, dispatch_two, cotangent, tokens, kept, w_out, bucket_row
    )

    return (
        layer_out,
        grad_tokens,
        g_gain_one.reshape(half),
        g_qkv.astype(F32),
        g_out.astype(F32),
        g_table,
        g_gain_two.reshape(half),
        g_router.T,
        grad_in_expert[None],
        grad_back_expert[None],
    )


SIZES = {64: (4, 4, 2), 4: (2, 1, 1), 8: (2, 2, 1)}


def solution(mesh):
    in_specs = (
        P(("rep", "shard"), None),
        P(("rep", "shard"), None),
        P("shard"),
        P("shard", None),
        P("shard", None),
        P("shard", None),
        P(),
        P("shard"),
        P("shard", None),
        P("rep", None, "shard"),
        P("rep", "shard", None),
        P(("rep", "shard"), None),
    )
    out_specs = (
        P(("rep", "shard"), None),
        P(("rep", "shard"), None),
        P("shard"),
        P("shard", None),
        P("shard", None),
        P("shard", None),
        P("shard"),
        P("shard", None),
        P("rep", None, "shard"),
        P("rep", "shard", None),
    )
    sizes = SIZES[mesh.shape["rep"]]
    return jax.shard_map(
        functools.partial(body, sizes),
        mesh=mesh,
        in_specs=in_specs,
        out_specs=out_specs,
        check_vma=False,
    )
```
